32 devices in a mesh: seq: 8 (over z, x), ch: 4 (over y, core).
Axes of the slice: x: 2, y: 2, z: 4, core: 2. Of those that a mesh axis runs over, the one named last changes fastest.
Arguments:
- token_ids: int32 [16, 2048], P(None, 'seq'), may hold values from 0 to 255
- counts: int32 [16], replicated, may hold values from 1024 to 2048, as said below
- embedding: bfloat16 [256, 512], replicated, may hold values from -6 to 6
- gain_one: float32 [512], replicated, may hold values from 0.5 to 1.5
- ema_rate: float32 [512, 16], P('ch'), may hold values from 4.8828126e-05 to 0.05
- ema_beta: float32 [512, 16], P('ch'), may hold values from -6 to 6
- ema_eta: float32 [512, 16], P('ch'), may hold values from -3 to 3
- ema_omega: float32 [512], P('ch'), may hold values from -5 to 5
- w_value: bfloat16 [512, 1024], P(None, 'ch'), may hold values from -0.25 to 0.25
- w_reset: bfloat16 [512, 1024], P(None, 'ch'), may hold values from -0.25 to 0.25
- w_z: bfloat16 [512, 128], replicated, may hold values from -0.25 to 0.25
- z_scale: float32 [2, 128], replicated, may hold values from -6 to 6
- z_offset: float32 [2, 128], replicated, may hold values from -3 to 3
- position_bias: float32 [255], replicated, may hold values from -3 to 3
- w_update: bfloat16 [512, 512], P(None, 'ch'), may hold values from -0.25 to 0.25
- w_cand: bfloat16 [512, 512], P(None, 'ch'), may hold values from -0.25 to 0.25
- w_out: bfloat16 [1024, 512], P('ch'), may hold values from -0.375 to 0.375
- gain_two: float32 [512], replicated, may hold values from 0.5 to 1.5
- w_up: bfloat16 [512, 1024], P(None, 'ch'), may hold values from -0.25 to 0.25
- w_down: bfloat16 [1024, 512], P('ch'), may hold values from -0.1875 to 0.1875
- cotangent: bfloat16 [16, 2048, 512], P(None, 'seq'), may hold values from -6 to 6
Outputs:
- output: float32 [16, 2048, 512], P(None, 'seq')
- input_grad: float32 [16, 2048, 512], P(None, 'seq')
- grad_embedding: float32 [256, 512], replicated
- grad_gain_one: float32 [512], replicated
- grad_ema_rate: float32 [512, 16], P('ch')
- grad_ema_beta: float32 [512, 16], P('ch')
- grad_ema_eta: float32 [512, 16], P('ch')
- grad_ema_omega: float32 [512], P('ch')
- grad_w_value: float32 [512, 1024], P(None, 'ch')
- grad_w_reset: float32 [512, 1024], P(None, 'ch')
- grad_w_z: float32 [512, 128], replicated
- grad_z_scale: float32 [2, 128], replicated
- grad_z_offset: float32 [2, 128], replicated
- grad_position_bias: float32 [255], replicated
- grad_w_update: float32 [512, 512], P(None, 'ch')
- grad_w_cand: float32 [512, 512], P(None, 'ch')
- grad_w_out: float32 [1024, 512], P('ch')
- grad_gain_two: float32 [512], replicated
- grad_w_up: float32 [512, 1024], P(None, 'ch')
- grad_w_down: float32 [1024, 512], P('ch')
The draws below stay inside these ranges and needn't reach their ends.
Inputs may be any that keep to these rules, and one draw needn't show every extreme that they name: Valid positions of each sequence; positions from counts on are padding; some sequence is full.
All inputs are finite; a program needn't handle non-finite values.
Results may differ from the reference program's by a relative error of at most 0.024.
Values may be sent and summed in bfloat16 or wider, within the bound.
No kernel may reach another device: no remote copies, remote signals or barrier semaphores. Data moves between devices by JAX's collectives and lax.ppermute only.
A program may use at most 320 MiB of HBM per device.

```python
import math
import jax
import jax.numpy as jnp
import numpy as np
from jax import lax

D = 512
Z = 128
V = 1024
H = 16
C = 128
F = 1024
VOC = 256
SEQS = 16
LENGTH = 2048


def draw_counts(key, part):
    filled = jax.random.randint(jax.random.fold_in(key, 11), (SEQS,), LENGTH // 2, LENGTH + 1)
    chosen = jax.random.randint(jax.random.fold_in(key, 12), (), 0, SEQS)
    return jnp.where(jnp.arange(SEQS) == chosen, LENGTH, filled).astype(jnp.int32)


def place_ends(values, own_key, smallest, largest):
    shape = values.shape
    index_at = [jax.random.randint(jax.random.fold_in(own_key, axis), (), 0, shape[axis]) for axis in range(len(shape))]
    values = values.at[tuple(index_at)].set(smallest)
    longest = shape.index(max(shape))
    index_at[longest] = (index_at[longest] + 1) % shape[longest]
    return values.at[tuple(index_at)].set(largest)


def shard_levels(key, shape, pieces, low, high):
    loudness = 1.0
    for dim, blocks in pieces:
        steps = jax.random.uniform(jax.random.fold_in(jax.random.fold_in(key, 6), dim), (blocks,), jnp.float32, low / len(pieces), high / len(pieces))
        loudness = loudness * jnp.repeat(jnp.exp(steps), shape[dim] // blocks).reshape((-1,) + (1,) * (len(shape) - 1 - dim))
    return loudness


def rank_table(count, skew):
    loads = [(1 << 20) // math.isqrt(grade ** skew) + 1 for grade in range(1, count + 1)]
    deviation = 1 + sum(loads) // (1 << 30)
    return np.cumsum(np.array([max(1, weight // deviation) for weight in loads]))


def ranked(rng, dims, count, slope):
    listing = rank_table(count, slope)
    lot = jax.random.randint(jax.random.fold_in(rng, 1), dims, 0, int(listing[count - 1]))
    standing = jnp.searchsorted(jnp.asarray(listing, jnp.int32), lot, side="right")
    return jax.random.permutation(jax.random.fold_in(rng, 2), count)[standing].astype(jnp.int32)


def centred(key, dims, width, reach, pieces=(), kind=jnp.bfloat16):
    result = jax.random.normal(key, dims, jnp.float32) * width
    if len(pieces) > 0:
        result = shard_levels(key, dims, pieces, -0.22, 0.18) * result
    return jnp.clip(result, min=-reach, max=reach).astype(kind)


def setup_inputs(seed: int = 0) -> dict:
    streams_of = jax.random.split(jax.random.key(seed), 22)
    token_ids = place_ends(ranked(streams_of[0], (SEQS, LENGTH), VOC, 2), jax.random.fold_in(streams_of[0], 3), 0, VOC - 1).astype(jnp.int32)
    counts = draw_counts(jax.random.fold_in(streams_of[21], 71), 0)
    embedding = centred(streams_of[2], (VOC, D), 1.0, 6.0)
    gain_one = jnp.clip(1.0 + 0.1 * jax.random.normal(streams_of[3], (D,), jnp.float32), 0.5, 1.5)
    ema_rate = jnp.clip(jnp.exp(math.log(0.05) - 6.931472 * jax.random.uniform(streams_of[4], (D, H), jnp.float32) ** shard_levels(streams_of[4], (D, H), ((0, 4),), -0.2, 0.2)), 4.882812572759576e-05, 0.05)
    ema_beta = centred(streams_of[5], (D, H), 1.5, 6.0, ((0, 4),), jnp.float32)
    ema_eta = centred(streams_of[6], (D, H), 0.5, 3.0, ((0, 4),), jnp.float32)
    ema_omega = centred(streams_of[7], (D,), 1.0, 5.0, ((0, 4),), jnp.float32)
    w_value = centred(streams_of[8], (D, V), D ** -0.5, 0.25, ((1, 4),))
    w_reset = centred(streams_of[9], (D, V), D ** -0.5, 0.25, ((1, 4),))
    w_z = centred(streams_of[10], (D, Z), D ** -0.5, 0.25)
    z_scale = centred(streams_of[11], (2, Z), 1.5, 6.0, (), jnp.float32)
    z_offset = centred(streams_of[12], (2, Z), 0.5, 3.0, (), jnp.float32)
    position_bias = centred(streams_of[13], (2 * C - 1,), 0.5, 3.0, (), jnp.float32)
    w_update = centred(streams_of[14], (D, D), D ** -0.5, 0.25, ((1, 4),))
    w_cand = centred(streams_of[15], (D, D), D ** -0.5, 0.25, ((1, 4),))
    w_out = centred(streams_of[16], (V, D), (V // 4) ** -0.5, 0.375, ((0, 4),))
    gain_two = jnp.clip(1.0 + 0.1 * jax.random.normal(streams_of[17], (D,), jnp.float32), 0.5, 1.5)
    w_up = centred(streams_of[18], (D, F), D ** -0.5, 0.25, ((1, 4),))
    w_down = centred(streams_of[19], (F, D), F ** -0.5, 0.1875, ((0, 4),))
    cotangent = centred(streams_of[20], (SEQS, LENGTH, D), 1.0, 6.0, ((1, 8),))
    return dict(token_ids=token_ids, counts=counts, embedding=embedding, gain_one=gain_one, ema_rate=ema_rate, ema_beta=ema_beta, ema_eta=ema_eta, ema_omega=ema_omega, w_value=w_value, w_reset=w_reset, w_z=w_z, z_scale=z_scale, z_offset=z_offset, position_bias=position_bias, w_update=w_update, w_cand=w_cand, w_out=w_out, gain_two=gain_two, w_up=w_up, w_down=w_down, cotangent=cotangent)


@jax.custom_vjp
def low(v):
    return lax.optimization_barrier(v.astype(jnp.bfloat16)).astype(jnp.float32)

@jax.custom_vjp
def low_back(v):
    return v

def low_keep(v):
    return (low(v), None)

def low_pass(kept, grad):
    return (grad,)

def back_keep(v):
    return (v, None)

def back_low(kept, grad):
    return (low(grad),)
low.defvjp(low_keep, low_pass)
low_back.defvjp(back_keep, back_low)
EPS = 1e-05

def dot_high(left, right):
    return jnp.dot(left, right, precision=lax.Precision.HIGHEST)

def rms_norm(values, gain):
    inverse = lax.rsqrt(lax.optimization_barrier(jnp.mean(values * values, axis=-1, keepdims=True)) + EPS)
    return values * inverse * gain

def pair_chain(earlier, later):
    return (earlier[0] * later[0], later[0] * earlier[1] + later[1])

def one_sequence(weights, embedded):
    gain_one, ema_rate, ema_beta, ema_eta, ema_omega, w_value, w_reset, w_z, z_scale, z_offset, position_bias, w_update, w_cand, w_out, gain_two, w_up, w_down = weights
    normed = rms_norm(embedded, gain_one)
    decay = jnp.exp(-ema_rate)
    drive = (1.0 - decay) * ema_beta * normed[:, :, None]
    _, states = lax.associative_scan(pair_chain, (jnp.broadcast_to(decay, drive.shape), drive), axis=0)
    ema_sum = lax.optimization_barrier(jnp.sum(ema_eta * states, axis=-1)) + ema_omega * normed
    ema_act = low(jax.nn.silu(ema_sum))
    normed_low = low(normed)
    value_pre = low_back(dot_high(normed_low, w_value))
    values = low(jax.nn.silu(value_pre))
    reset = jax.nn.silu(low_back(dot_high(ema_act, w_reset)))
    z_pre = low_back(dot_high(ema_act, w_z))
    z_act = jax.nn.silu(z_pre)
    query = low(z_act * z_scale[0] + z_offset[0])
    keys = low(z_act * z_scale[1] + z_offset[1])
    blocks = LENGTH // C
    query_blocks = query.reshape(blocks, C, Z)
    key_blocks = keys.reshape(blocks, C, Z)
    value_blocks = values.reshape(blocks, C, V)
    offsets = C - 1 - jnp.arange(C, dtype=jnp.int32)[:, None] + jnp.arange(C, dtype=jnp.int32)[None, :]
    bias_table = position_bias[offsets]
    scores = low_back(jnp.einsum('kqz,kpz->kqp', query_blocks, key_blocks, precision=lax.Precision.HIGHEST) * Z ** (-0.5)) + bias_table[None]
    causal = jnp.arange(C)[:, None] >= jnp.arange(C)[None, :]
    scores = jnp.where(causal[None], scores, -1e+30)
    shifted = jnp.exp(scores - lax.optimization_barrier(jnp.max(scores, axis=-1, keepdims=True)))
    weights_soft = shifted / lax.optimization_barrier(jnp.sum(shifted, axis=-1, keepdims=True))
    mixed = low_back(jnp.einsum('kqp,kpv->kqv', low(weights_soft), value_blocks, precision=lax.Precision.HIGHEST)).reshape(LENGTH, V)
    gated = low(reset * mixed)
    update = jax.nn.sigmoid(low_back(dot_high(ema_act, w_update)))
    cand = jax.nn.silu(low_back(dot_high(ema_act, w_cand) + dot_high(gated, w_out)))
    resid = update * cand + (1.0 - update) * embedded
    ff_in = low(rms_norm(resid, gain_two))
    hidden = low(jax.nn.silu(low_back(dot_high(ff_in, w_up))))
    return resid + dot_high(hidden, w_down)

def reference(token_ids, counts, embedding, gain_one, ema_rate, ema_beta, ema_eta, ema_omega, w_value, w_reset, w_z, z_scale, z_offset, position_bias, w_update, w_cand, w_out, gain_two, w_up, w_down, cotangent):
    places = jnp.arange(LENGTH, dtype=jnp.int32)
    present = (places[None, :] < counts[:, None]).astype(jnp.float32)
    table = embedding.astype(jnp.float32)
    looked, lookup_pull = jax.vjp(lambda rows_table: rows_table[token_ids], table)
    params = (gain_one, ema_rate, ema_beta, ema_eta, ema_omega, w_value.astype(jnp.float32), w_reset.astype(jnp.float32), w_z.astype(jnp.float32), z_scale, z_offset, position_bias, w_update.astype(jnp.float32), w_cand.astype(jnp.float32), w_out.astype(jnp.float32), gain_two, w_up.astype(jnp.float32), w_down.astype(jnp.float32))

    def forward(raw, weights):
        embedded = raw * present[:, :, None]
        return lax.map(jax.checkpoint(lambda single: one_sequence(weights, single)), embedded)
    output, pull = jax.vjp(forward, looked, params)
    grad_raw, grads = pull(cotangent.astype(jnp.float32) * present[:, :, None])
    grad_embedding = lookup_pull(grad_raw)[0]
    return (output, grad_raw, grad_embedding, grads[0], grads[1], grads[2], grads[3], grads[4], grads[5], grads[6], grads[7], grads[8], grads[9], grads[10], grads[11], grads[12], grads[13], grads[14], grads[15], grads[16])
```

```python
import functools

import jax
import jax.numpy as jnp
from jax import lax
from jax.experimental import pallas as pl
from jax.experimental.pallas import tpu as pltpu
from jax.sharding import PartitionSpec as P

C = 128
BLK = 256
LANES = 8
STEP = BLK // LANES
EPS = 1e-05
BF = jnp.bfloat16
F32 = jnp.float32
VMEM = 60 * 1024 * 1024


def cost(us):
    return pl.CostEstimate(flops=us * 10**9, bytes_accessed=10**5, transcendentals=0)


def sig(v):
    return 0.5 * jnp.tanh(0.5 * v) + 0.5


def mm(a, b):
    return jnp.dot(a, b, preferred_element_type=F32)


def mm_nt(a, b):
    return lax.dot_general(a, b, (((1,), (1,)), ((), ())), preferred_element_type=F32)


def mm_tn(a, b):
    return lax.dot_general(a, b, (((0,), (0,)), ((), ())), preferred_element_type=F32)


def slope(v, s):
    return s * (1.0 + v * (1.0 - s))


def wide(row):
    return jnp.broadcast_to(row, (LANES, 128))


def lane_iota():
    return lax.broadcasted_iota(jnp.int32, (LANES, 128), 0)


def shift_down(v, k, row):
    return jnp.where(row >= k, pltpu.roll(v, k, axis=0), 0.0)


def shift_up(v, k, row):
    return jnp.where(row < LANES - k, pltpu.roll(v, LANES - k, axis=0), 0.0)


def chain(values, rates, row, shift):
    for k in (1, 2, 4):
        values = [
            v + jnp.exp(r * (-float(STEP * k))) * shift(v, k, row) for v, r in zip(values, rates)
        ]
    return values


def at(t):
    return pl.ds(pl.multiple_of(t * LANES, LANES), LANES)


def one_hot_t(ids, vocab):
    hit = lax.broadcasted_iota(jnp.int32, (vocab, BLK), 0) == ids
    return jnp.where(hit, 1.0, 0.0).astype(BF)


def one_less_exp(rate):
    near = rate * (1.0 - rate * (0.5 - rate * (1.0 / 6.0 - rate * (1.0 / 24.0))))
    return jnp.where(rate < 0.02, near, 1.0 - jnp.exp(-rate))


def prep_kernel(rate_ref, beta_ref, eta_ref, omega_ref, out_ref):
    dims = rate_ref.shape[0]
    rate, beta, eta = rate_ref[...], beta_ref[...], eta_ref[...]
    decay, rise = jnp.exp(-rate), one_less_exp(rate)
    for k, v in enumerate((rate, eta * rise * beta, rise * beta, eta * rise, -decay * eta * beta)):
        out_ref[k * dims : (k + 1) * dims, :] = v
    out_ref[5 * dims :, :] = jnp.broadcast_to(omega_ref[...], (8, omega_ref.shape[1]))


def split3(v):
    parts = []
    for _ in range(3):
        parts.append(v.astype(BF))
        v = v - parts[-1].astype(F32)
    return parts


def skew(v, sign):
    row = lax.broadcasted_iota(jnp.int32, v.shape, 0)
    for b in range(7):
        k = 1 << b
        v = jnp.where((row & k) != 0, pltpu.roll(v, k if sign > 0 else 256 - k, axis=1), v)
    return v


def table_kernel(bias_ref, out_ref):
    v = jnp.broadcast_to(bias_ref[...], (C, 256))
    v = skew(pltpu.roll(v, 256 - (C - 1), axis=1), 1)[:, :C]
    off = jnp.zeros((C, C), F32)
    v = jnp.concatenate(
        [jnp.concatenate([v, off], axis=1), jnp.concatenate([off, v], axis=1)], axis=0
    )
    perm = to_natural(None)
    v = sum(mm_tn(perm, p) for p in split3(v))
    v = sum(mm(p, perm) for p in split3(v))
    r = lax.broadcasted_iota(jnp.int32, (BLK, BLK), 0)
    c = lax.broadcasted_iota(jnp.int32, (BLK, BLK), 1)
    query = (r & (LANES - 1)) * STEP + (r >> 3)
    key = (c & (LANES - 1)) * STEP + (c >> 3)
    seen = jnp.logical_and(key <= query, key >= (query & C))
    out_ref[...] = jnp.where(seen, v, -1e30)


def embed_kernel(ids_ref, tab_ref, gain_ref, x_ref, emb_ref):
    emb = mm_tn(one_hot_t(ids_ref[0], tab_ref.shape[0]), tab_ref[...])
    inv = lax.rsqrt(jnp.mean(emb * emb, axis=-1, keepdims=True) + EPS)
    x_ref[0] = emb * inv * gain_ref[...]
    emb_ref[0] = emb.astype(BF)


def enter_kernel(x_ref, par_ref, ex_ref, lv_ref):
    dims, width = lv_ref.shape[1:]

    row = lane_iota()
    for c0 in range(0, width, 128):
        sl = pl.ds(c0, 128)
        rates = [wide(par_ref[pl.ds(j, 1), sl]) for j in range(dims)]
        decay = [jnp.exp(-r) for r in rates]

        def body(t, s):
            xt = x_ref[0, at(t), sl]
            return tuple(d * v + xt for d, v in zip(decay, s))

        s = lax.fori_loop(
            0, STEP, body, tuple(jnp.zeros((LANES, 128), F32) for _ in range(dims)), unroll=8
        )
        s = chain(list(s), rates, row, shift_down)
        for j in range(dims):
            ex_ref[0, j, :, sl] = shift_down(s[j], 1, row)
            lv_ref[0, pl.ds(j, 1), sl] = s[j][LANES - 1 :, :]


def run_kernel(x_ref, ex_ref, se_ref, par_ref, out_ref):
    dims, width = se_ref.shape[1:]
    place = lane_iota().astype(F32)
    for c0 in range(0, width, 128):
        sl = pl.ds(c0, 128)
        rates = [wide(par_ref[pl.ds(j, 1), sl]) for j in range(dims)]
        decay = [jnp.exp(-r) for r in rates]
        ws = [wide(par_ref[pl.ds(dims + j, 1), sl]) for j in range(dims)]
        omega = wide(par_ref[pl.ds(5 * dims, 1), sl])
        start = tuple(
            ex_ref[0, j, :, sl]
            + jnp.exp(rates[j] * place * (-float(STEP))) * wide(se_ref[0, pl.ds(j, 1), sl])
            for j in range(dims)
        )

        def body(t, s):
            xt = x_ref[0, at(t), sl]
            s = tuple(d * v + xt for d, v in zip(decay, s))
            parts = [w * v for w, v in zip(ws, s)]
            while len(parts) > 1:
                parts = [a + b for a, b in zip(parts[::2], parts[1::2])]
            out_ref[0, at(t), sl] = parts[0] + omega * xt
            return s

        lax.fori_loop(0, STEP, body, start, unroll=4)


def to_natural(mask_row):
    q = lax.broadcasted_iota(jnp.int32, (BLK, BLK), 0)
    r = lax.broadcasted_iota(jnp.int32, (BLK, BLK), 1)
    hit = q == (r & (LANES - 1)) * STEP + (r >> 3)
    if mask_row is not None:
        hit = jnp.logical_and(hit, mask_row >= 0)
    return jnp.where(hit, 1.0, 0.0).astype(BF)


def from_natural(mask_row):
    r = lax.broadcasted_iota(jnp.int32, (BLK, BLK), 0)
    q = lax.broadcasted_iota(jnp.int32, (BLK, BLK), 1)
    hit = q == (r & (LANES - 1)) * STEP + (r >> 3)
    if mask_row is not None:
        hit = jnp.logical_and(hit, mask_row >= 0)
    return jnp.where(hit, 1.0, 0.0).astype(BF)


def fill(refs, rows, to_ref):
    for r, ref in enumerate(refs):
        to_ref[:, pl.ds(r * 256, 256)] = ref[rows : rows + 512, :]


def fill_rows(refs, rows, to_ref):
    for r, ref in enumerate(refs):
        to_ref[pl.ds(r * 256, 256), 0:256] = ref[rows : rows + 256, :]
        to_ref[pl.ds(r * 256, 256), 256:512] = ref[rows + 256 : rows + 512, :]


def fill_gates(me, refs, wu_ref, wc_ref):
    for r, ref in enumerate(refs):
        own = pl.ds(pl.multiple_of((me ^ r) * 128, 128), 128)
        wu_ref[:, own] = ref[0:512, 0:128]
        wc_ref[:, own] = ref[0:512, 128:256]


def slots(keep_ref, send_ref):
    return ((keep_ref, 0), (send_ref, 0), (keep_ref, 1), (send_ref, 1))


def softmax_rows(query, keys, bias, factor):
    scores = mm_nt(query, keys) * factor + bias
    shifted = jnp.exp(scores - jnp.max(scores, axis=-1, keepdims=True))
    return shifted / jnp.sum(shifted, axis=-1, keepdims=True)


def forward_kernel(me_ref, es_ref, x_ref, emb_ref, bias_ref, wz_ref, zs_ref, zo_ref, *rest):
    packs, rest = rest[:8], rest[8:]
    (vp_ref, rp_ref, mix_ref, zp_ref, up_ref, cp_ref, res_ref) = rest[:7]
    (wv_ref, wr_ref, wu_ref, wc_ref, wo_ref) = rest[7:]

    @pl.when(pl.program_id(0) == 0)
    def _():
        fill(packs[0:4], 0, wv_ref)
        fill(packs[0:4], 512, wr_ref)
        fill_gates(me_ref[0], packs[4:8], wu_ref, wc_ref)
        fill_rows(packs[4:8], 512, wo_ref)

    es = es_ref[0]
    e = (es * sig(es)).astype(BF)
    zp = mm(e, wz_ref[...])
    zp_ref[0] = zp
    za = zp * sig(zp)
    query = (za * zs_ref[0:1, :] + zo_ref[0:1, :]).astype(BF)
    keys = (za * zs_ref[1:2, :] + zo_ref[1:2, :]).astype(BF)
    weights = softmax_rows(query, keys, bias_ref[...], zp.shape[-1] ** -0.5).astype(BF)
    vp = mm(x_ref[0].astype(BF), wv_ref[...])
    vp_ref[0] = vp.astype(BF)
    values = (vp * sig(vp)).astype(BF)
    mixed = mm(weights, values)
    mix_ref[0] = mixed.astype(BF)
    rp = mm(e, wr_ref[...])
    rp_ref[0] = rp.astype(BF)
    gated = (rp * sig(rp) * mixed).astype(BF)
    up = mm(e, wu_ref[...])
    up_ref[0] = up.astype(BF)
    cp = mm(e, wc_ref[...]) + mm(gated, wo_ref[...])
    cp_ref[0] = cp.astype(BF)
    emb = emb_ref[0].astype(F32)
    res_ref[0] = emb + sig(up) * (cp * sig(cp) - emb)


def ff_kernel(me_ref, nat_ref, cot_ref, res_ref, gain_ref, *rest):
    packs, rest = rest[:4], rest[4:]
    out_ref, gr_ref, keep_ref, send_ref, gg_ref, w_up_ref, w_down_ref, au_ref, ad_ref = rest
    step = pl.program_id(0)

    @pl.when(step == 0)
    def _():
        fill(packs, 0, w_up_ref)
        fill_rows(packs, 512, w_down_ref)
        au_ref[...] = jnp.zeros_like(au_ref)
        ad_ref[...] = jnp.zeros_like(ad_ref)
        gg_ref[...] = jnp.zeros_like(gg_ref)

    resid = res_ref[0]
    inv = lax.rsqrt(jnp.mean(resid * resid, axis=-1, keepdims=True) + EPS)
    unit = resid * inv
    gain = gain_ref[...]
    ff_in = (unit * gain).astype(BF)
    hp = mm(ff_in, w_up_ref[...])
    s = sig(hp)
    hidden = (hp * s).astype(BF)
    out = resid + mm(hidden, w_down_ref[...])
    out_ref[0] = mm(to_natural(None), out.astype(BF)).astype(BF)
    grad_out = mm(from_natural(nat_ref[0]), cot_ref[0])
    grad_low = grad_out.astype(BF)
    ad_ref[...] += mm_tn(hidden, grad_low)
    grad_up = (mm_nt(grad_low, w_down_ref[...]) * slope(hp, s)).astype(BF)
    au_ref[...] += mm_tn(ff_in, grad_up)
    grad_norm = mm_nt(grad_up, w_up_ref[...])
    gain_part = jnp.sum(grad_norm * unit, axis=0, keepdims=True)
    for k in range(4):
        gg_ref[k : k + 1, :] += gain_part[:, k * 128 : (k + 1) * 128]
    scaled = grad_norm * gain
    gr_ref[0] = grad_out + inv * (
        scaled - unit * jnp.mean(scaled * unit, axis=-1, keepdims=True)
    )

    @pl.when(step == pl.num_programs(0) - 1)
    def _():
        for r, (ref, slot) in enumerate(slots(keep_ref, send_ref)):
            ref[slot, 0:512, :] = au_ref[:, r * 256 : r * 256 + 256].astype(BF)
            ref[slot, 512:768, :] = ad_ref[r * 256 : r * 256 + 256, 0:256].astype(BF)
            ref[slot, 768:1024, :] = ad_ref[r * 256 : r * 256 + 256, 256:512].astype(BF)


def gates_back_kernel(me_ref, es_ref, emb_ref, rp_ref, mix_ref, up_ref, cp_ref, gr_ref, *rest):
    packs, rest = rest[:8], rest[8:]
    (gm_ref, ge_ref, dir_ref, keep_ref, send_ref) = rest[:5]
    (wr_ref, wu_ref, wc_ref, wo_ref, ar_ref, au_ref, ac_ref, ao_ref) = rest[5:]
    me = me_ref[0]
    step = pl.program_id(0)

    @pl.when(step == 0)
    def _():
        fill(packs[0:4], 0, wr_ref)
        fill_gates(me, packs[4:8], wu_ref, wc_ref)
        fill_rows(packs[4:8], 512, wo_ref)
        for ref in (ar_ref, au_ref, ac_ref, ao_ref):
            ref[...] = jnp.zeros_like(ref)

    es = es_ref[0]
    e_t = (es * sig(es)).astype(BF).T
    emb = emb_ref[0].astype(F32)
    grad_resid = gr_ref[0]
    up = sig(up_ref[0].astype(F32))
    cp = cp_ref[0].astype(F32)
    cs = sig(cp)
    gcp = (grad_resid * up * slope(cp, cs)).astype(BF)
    gup = (grad_resid * (cp * cs - emb) * up * (1.0 - up)).astype(BF)
    dir_ref[0] = (grad_resid * (1.0 - up)).astype(BF)
    ac_ref[...] += mm(e_t, gcp)
    au_ref[...] += mm(e_t, gup)
    rp = rp_ref[0].astype(F32)
    rs = sig(rp)
    reset = rp * rs
    mixed = mix_ref[0].astype(F32)
    ao_ref[...] += mm_tn((reset * mixed).astype(BF), gcp)
    grad_gated = mm_nt(gcp, wo_ref[...])
    gm_ref[0] = (grad_gated * reset).astype(BF)
    grp = (grad_gated * mixed * slope(rp, rs)).astype(BF)
    ar_ref[...] += mm(e_t, grp)
    ge_ref[0] = mm_nt(grp, wr_ref[...]) + mm_nt(gup, wu_ref[...]) + mm_nt(gcp, wc_ref[...])

    @pl.when(step == pl.num_programs(0) - 1)
    def _():
        for r, (ref, slot) in enumerate(slots(keep_ref, send_ref)):
            units = pl.ds(r * 256, 256)
            own = pl.ds(pl.multiple_of((me ^ r) * 128, 128), 128)
            ref[slot, 0:512, :] = ar_ref[:, units].astype(BF)
            ref[slot, 512:1024, 0:128] = au_ref[:, own].astype(BF)
            ref[slot, 512:1024, 128:256] = ac_ref[:, own].astype(BF)
            ref[slot, 1024:1280, :] = ao_ref[units, 0:256].astype(BF)
            ref[slot, 1280:1536, :] = ao_ref[units, 256:512].astype(BF)


def mix_back_kernel(
    es_ref, x_ref, vp_ref, zp_ref, gm_ref, ge_ref,
    bias_ref, wz_ref, zs_ref, zo_ref, par_ref, gg_ref, *rest,
):
    packs, rest = rest[:4], rest[4:]
    (g_ref, gnv_ref, ae_ref, lb_ref, keep_ref, send_ref) = rest[:6]
    (wv_ref, av_ref, az_ref, gz_ref, gb_ref) = rest[6:]
    step = pl.program_id(0)

    @pl.when(step == 0)
    def _():
        fill(packs, 0, wv_ref)
        for ref in (av_ref, az_ref, gz_ref, gb_ref):
            ref[...] = jnp.zeros_like(ref)

    es = es_ref[0]
    es_sig = sig(es)
    e_t = (es * es_sig).astype(BF).T
    gm = gm_ref[0]
    zp = zp_ref[0]
    zsig = sig(zp)
    za = zp * zsig
    factor = zp.shape[-1] ** -0.5
    s0, s1 = zs_ref[0:1, :], zs_ref[1:2, :]
    query = (za * s0 + zo_ref[0:1, :]).astype(BF)
    keys = (za * s1 + zo_ref[1:2, :]).astype(BF)
    weights = softmax_rows(query, keys, bias_ref[...], factor)
    vp = vp_ref[0].astype(F32)
    vs = sig(vp)
    values = (vp * vs).astype(BF)
    gvp = (mm_tn(weights.astype(BF), gm) * slope(vp, vs)).astype(BF)
    gnv_ref[0] = mm_nt(gvp, wv_ref[...]).astype(BF)
    av_ref[...] += mm_tn(x_ref[0].astype(BF), gvp)
    gw = mm_nt(gm, values)
    gsf = weights * (gw - jnp.sum(weights * gw, axis=-1, keepdims=True))
    gb_ref[...] += gsf
    gs = gsf.astype(BF)
    gq = mm(gs, keys) * factor
    gk = mm_tn(gs, query) * factor
    gz_ref[0:1, :] += jnp.sum(za * gq, axis=0, keepdims=True)
    gz_ref[1:2, :] += jnp.sum(za * gk, axis=0, keepdims=True)
    gz_ref[2:3, :] += jnp.sum(gq, axis=0, keepdims=True)
    gz_ref[3:4, :] += jnp.sum(gk, axis=0, keepdims=True)
    gzp = ((gq * s0 + gk * s1) * slope(zp, zsig)).astype(BF)
    az_ref[...] += mm(e_t, gzp)
    g_ref[0] = (ge_ref[0] + mm_nt(gzp, wz_ref[...])) * slope(es, es_sig)

    dims, width = lb_ref.shape[1:]
    row = lane_iota()
    for c0 in range(0, width, 128):
        sl = pl.ds(c0, 128)
        rates = [wide(par_ref[pl.ds(j, 1), sl]) for j in range(dims)]
        decay = [jnp.exp(-r) for r in rates]

        def body(t, a):
            gt = g_ref[0, at(STEP - 1 - t), sl]
            return tuple(d * v + gt for d, v in zip(decay, a))

        a = lax.fori_loop(
            0, STEP, body, tuple(jnp.zeros((LANES, 128), F32) for _ in range(dims)), unroll=8
        )
        a = chain(list(a), rates, row, shift_up)
        for j in range(dims):
            ae_ref[0, j, :, sl] = shift_up(a[j], 1, row)
            lb_ref[0, pl.ds(j, 1), sl] = a[j][0:1, :]

    @pl.when(step == pl.num_programs(0) - 1)
    def _():
        perm = to_natural(None)
        v = sum(mm(perm, p) for p in split3(gb_ref[...]))
        v = sum(mm_nt(p, perm) for p in split3(v))
        v = v[:C, :C] + v[C:, C:]
        v = jnp.concatenate([v, jnp.zeros((C, C), F32)], axis=1)
        bias = jnp.sum(pltpu.roll(skew(v, -1), C - 1, axis=1), axis=0, keepdims=True)
        zero = jnp.zeros((6, 128), F32)
        small = jnp.concatenate(
            [gz_ref[0:4, :], bias[:, :128], bias[:, 128:], gg_ref[...], zero], axis=0
        )
        for r, (ref, slot) in enumerate(slots(keep_ref, send_ref)):
            ref[slot, 0:512, :] = av_ref[:, r * 256 : r * 256 + 256].astype(BF)
            ref[slot, 512:768, 0:128] = az_ref[0:256, :].astype(BF)
            ref[slot, 512:768, 128:256] = az_ref[256:512, :].astype(BF)
            ref[slot, 768:896, :] = jnp.zeros((128, 256), BF)
            ref[slot, 768:784, 0:128] = small.astype(BF)


def leave_kernel(
    me_ref, ids_ref, emb_ref, x_ref, g_ref, ae_ref, ar_ref, ex_ref, se_ref, dir_ref, gnv_ref,
    par_ref, gain_ref, ig_ref, keep_ref, send_ref,
    gn_ref, m_ref, n_ref, ge_ref, go_ref, gg_ref, sum_ref,
):
    step = pl.program_id(0)
    dims, width = se_ref.shape[1:]

    @pl.when(step == 0)
    def _():
        for ref in (ge_ref, go_ref, gg_ref, m_ref, n_ref):
            ref[...] = jnp.zeros_like(ref)

    place = lane_iota().astype(F32)
    half = 8
    for c0 in range(0, width, 128):
        sl = pl.ds(c0, 128)
        omega = wide(par_ref[pl.ds(5 * dims, 1), sl])
        for j0 in range(0, dims, half):
            js = range(j0, j0 + half)
            rates = [wide(par_ref[pl.ds(j, 1), sl]) for j in js]
            decay = [jnp.exp(-r) for r in rates]
            ws = [wide(par_ref[pl.ds(dims + j, 1), sl]) for j in js]
            a_end = [
                ae_ref[0, j, :, sl]
                + jnp.exp(r * (LANES - 1.0 - place) * (-float(STEP)))
                * wide(ar_ref[0, pl.ds(j, 1), sl])
                for j, r in zip(js, rates)
            ]

            def emit(t, a, gt):
                parts = [w * v for w, v in zip(ws, a)]
                while len(parts) > 1:
                    parts = [p + q for p, q in zip(parts[::2], parts[1::2])]
                if j0 == 0:
                    gn_ref[at(t), sl] = parts[0] + omega * gt
                else:
                    gn_ref[at(t), sl] += parts[0]

            gt = g_ref[0, at(STEP - 1), sl]
            xt = x_ref[0, at(STEP - 1), sl]
            a = tuple(gt + d * v for d, v in zip(decay, a_end))
            emit(STEP - 1, a, gt)
            m = tuple(xt * v for v in a)
            zero = tuple(jnp.zeros((LANES, 128), F32) for _ in js)

            def body(i, carry):
                a, b, m, n = carry
                t = STEP - 2 - i
                gt = g_ref[0, at(t), sl]
                xt = x_ref[0, at(t), sl]
                b = tuple(u + d * v for d, u, v in zip(decay, a, b))
                a = tuple(gt + d * v for d, v in zip(decay, a))
                emit(t, a, gt)
                m = tuple(u + xt * v for u, v in zip(m, a))
                n = tuple(u + xt * v for u, v in zip(n, b))
                return a, b, m, n

            a, b, m, n = lax.fori_loop(0, STEP - 1, body, (a, zero, m, zero))
            for k, j in enumerate(js):
                start = ex_ref[0, j, :, sl] + jnp.exp(rates[k] * place * (-float(STEP))) * wide(
                    se_ref[0, pl.ds(j, 1), sl]
                )
                m_ref[j, :, sl] += m[k]
                n_ref[j, :, sl] += n[k] + start * (a[k] + decay[k] * b[k])

    go_ref[...] += jnp.sum(g_ref[0] * x_ref[0], axis=0, keepdims=True)
    emb = emb_ref[0].astype(F32)
    inv = lax.rsqrt(jnp.mean(emb * emb, axis=-1, keepdims=True) + EPS)
    unit = emb * inv
    gn = gn_ref[...] + gnv_ref[0].astype(F32)
    gg_ref[...] += jnp.sum(gn * unit, axis=0, keepdims=True)
    scaled = gn * gain_ref[...]
    ig = dir_ref[0].astype(F32) + inv * (
        scaled - unit * jnp.mean(scaled * unit, axis=-1, keepdims=True)
    )
    ig = ig.astype(BF)
    ids = ids_ref[0]
    ig_ref[0] = mm(to_natural(ids), ig).astype(BF)
    ge_ref[...] += mm(one_hot_t(ids, ge_ref.shape[0]), ig)

    @pl.when(step == pl.num_programs(0) - 1)
    def _():
        for j in range(dims):
            sum_ref[pl.ds(j, 1), :] = jnp.sum(m_ref[j], axis=0, keepdims=True)
            sum_ref[pl.ds(dims + j, 1), :] = jnp.sum(n_ref[j], axis=0, keepdims=True)
        m, n = sum_ref[0:dims, :], sum_ref[dims : 2 * dims, :]
        rb, er, eb = (par_ref[k * dims : (k + 1) * dims, :] for k in (2, 3, 4))
        rise = one_less_exp(par_ref[0:dims, :])
        sum_ref[0:dims, :] = eb * (rise * n - m)
        sum_ref[dims : 2 * dims, :] = er * m
        sum_ref[2 * dims : 3 * dims, :] = rb * m
        pad = jnp.zeros((8, 128), F32)
        gains = [gg_ref[:, k * 128 : (k + 1) * 128] for k in range(4)]
        for r, (ref, slot) in enumerate(slots(keep_ref, send_ref)):
            own = pl.ds(pl.multiple_of((me_ref[0] ^ r) * 128, 128), 128)
            part = pl.ds(pl.multiple_of((me_ref[0] ^ r) * 64, 64), 64)
            ref[slot, 0:64, :] = ge_ref[part, 0:256].astype(BF)
            ref[slot, 64:128, :] = ge_ref[part, 256:512].astype(BF)
            ref[slot, 128:256, :] = jnp.zeros((128, 256), BF)
            ref[slot, 128:144, 0:128] = sum_ref[0:dims, own].astype(BF)
            ref[slot, 128:144, 128:256] = sum_ref[dims : 2 * dims, own].astype(BF)
            ref[slot, 144:160, 0:128] = sum_ref[2 * dims : 3 * dims, own].astype(BF)
            ref[slot, 160:176, 0:128] = jnp.concatenate(
                [jnp.broadcast_to(go_ref[:, own], (4, 128)), *gains, pad], axis=0
            ).astype(BF)


def add_kernel(n, *refs):
    acc = refs[0][...].astype(F32)
    for ref in refs[1:n]:
        acc = acc + ref[...].astype(F32)
    refs[n][...] = acc[0].astype(BF)
    refs[n + 1][...] = acc[1].astype(BF)


def cut_kernel(bit, at_ref, near_ref, far_ref, keep_ref, send_ref, sum_ref):
    rows = keep_ref.shape[0]
    sum_ref[...] = near_ref[...].astype(F32) + far_ref[...].astype(F32)
    upper = (at_ref[0] // bit) % 2
    keep_ref[...] = sum_ref[pl.ds(pl.multiple_of(upper * rows, rows), rows), :].astype(BF)
    send_ref[...] = sum_ref[pl.ds(pl.multiple_of((1 - upper) * rows, rows), rows), :].astype(BF)


def sum_kernel(*refs):
    refs[-1][...] = total([ref[...] for ref in refs[:-1]]).astype(BF)


def join_kernel(put, at_ref, *refs):
    ins, outs, whole = refs[:2], refs[2:-1], refs[-1]
    rows = whole.shape[0] // 8
    slots = (0, 4, 2, 6, 1, 5, 3, 7)
    for k, slot in enumerate(slots):
        of = at_ref[0] ^ slot
        place = (of % 2) * 4 + ((of // 2) % 2) * 2 + of // 4
        piece = ins[k // 4][(k % 4) * rows : (k % 4 + 1) * rows, :]
        whole[pl.ds(pl.multiple_of(place * rows, rows), rows), :] = piece.astype(F32)
    put(whole, *outs)


def widen_kernel(me_ref, *refs):
    for r, ref in enumerate(refs[:4]):

        @pl.when(pl.program_id(0) == r)
        def _(ref=ref):
            refs[-1][...] = ref[...].astype(F32)


def pairs(axis, bit):
    return [(i, i ^ bit) for i in range(lax.axis_size(axis))]


def swap(v, axis, bit):
    return lax.ppermute(v, axis, pairs(axis, bit))


def gather_pack(v):
    far = swap(v, "ch", 2)
    return [v, swap(v, "ch", 1), far, swap(far, "ch", 1)]


def exclusive(total, rate, span, backward):
    count, mine = lax.axis_size("seq"), lax.axis_index("seq")
    out = jnp.zeros_like(total)
    bit = 1
    while bit < count:
        recv = swap(total, "seq", bit)
        upper = (mine & bit) != 0
        inside = mine & (bit - 1)
        decay = jnp.exp(rate * (-float(bit * span)))
        gap = bit - 1 - inside if backward else inside
        near = jnp.exp(-rate * (gap * span).astype(F32))
        first = jnp.logical_not(upper) if backward else upper
        out = jnp.where(first, out + recv * near, out)
        total = jnp.where(first, total + decay * recv, recv + decay * total)
        bit *= 2
    return out


def block_states(local, rate, span, backward):
    per = span // BLK
    local = local.reshape((-1, per) + local.shape[1:])
    decay = jnp.exp(rate * (-float(BLK)))
    order = range(per)[::-1] if backward else range(per)
    total = 0.0
    for k in order:
        total = total * decay + local[:, k]
    state = exclusive(total, rate, span, backward)
    states = [None] * per
    for k in order:
        states[k] = state
        state = state * decay + local[:, k]
    return jnp.stack(states, axis=1).reshape((-1,) + rate.shape)


def total(parts):
    acc = parts[0].astype(F32)
    for p in parts[1:]:
        acc = acc + p.astype(F32)
    return acc


def small_call(kernel, name, scalars, args, outs, scratch=(), after=()):
    vmem = pl.BlockSpec(memory_space=pltpu.VMEM)
    smem = pl.BlockSpec(memory_space=pltpu.SMEM)
    n = len(scalars) + len(args)

    def body(*refs):
        kernel(*refs[:n], *refs[n + len(after) :])

    return pl.pallas_call(
        body,
        in_specs=[smem] * len(scalars)
        + [vmem] * len(args)
        + [pl.BlockSpec(memory_space=pl.ANY)] * len(after),
        out_specs=[vmem] * len(outs),
        out_shape=[jax.ShapeDtypeStruct(s, t) for s, t in outs],
        scratch_shapes=[pltpu.VMEM(s, t) for s, t in scratch],
        compiler_params=pltpu.CompilerParams(vmem_limit_bytes=VMEM),
        cost_estimate=cost(2),
        name=name,
    )(*scalars, *args, *after)


class Reduction:
    def __init__(self, name, at, keeps, sends):
        self.name, self.at = name, at
        self.args = list(keeps) + [swap(s, "ch", 1) for s in sends]
        self.rows = keeps[0].shape[1]
        self.wide = lax.axis_size("seq") != 8

    def shards(self):
        shape = (self.rows, 256)
        near, far = small_call(
            functools.partial(add_kernel, len(self.args)), self.name + "_add", [], self.args,
            [(shape, BF), (shape, BF)],
        )
        self.near, self.far = near, swap(far, "ch", 2)
        return near

    def whole_seq(self):
        self.whole = lax.psum(total([self.near, self.far]).astype(BF), "seq").astype(F32)

    def scatter(self, bit):
        if self.wide:
            if bit == 1:
                self.whole_seq()
            return self.whole
        rows = self.near.shape[0]
        near, far = small_call(
            functools.partial(cut_kernel, bit), self.name + "_cut", [self.at], [self.near, self.far],
            [((rows // 2, 256), BF)] * 2, [((rows, 256), F32)],
        )
        self.near, self.far = near, swap(far, "seq", bit)
        return near

    def sums(self):
        if self.wide:
            return self.whole
        shape = self.near.shape
        (self.near,) = small_call(
            sum_kernel, self.name + "_sum", [], [self.near, self.far], [(shape, BF)]
        )
        self.far = swap(self.near, "seq", 4)
        return self.near

    def grow(self, bit):
        if self.wide:
            return self.whole
        self.near = jnp.concatenate([self.near, self.far], axis=0)
        self.far = swap(self.near, "seq", bit)
        return self.near

    def join(self, put, outs):
        if self.wide:
            return small_call(put, self.name + "_join", [], [self.whole], outs)
        return small_call(
            functools.partial(join_kernel, put), self.name + "_join", [self.at],
            [self.near, self.far], outs, [((self.rows, 256), F32)],
        )

    def rest(self, put, outs, scatters=()):
        for bit in scatters:
            self.scatter(bit)
        self.sums()
        self.grow(2)
        self.grow(1)
        return self.join(put, outs)


def put_ff(whole, up_ref, down_ref):
    up_ref[...] = whole[0:512, :]
    down_ref[:, 0:256] = whole[512:768, :]
    down_ref[:, 256:512] = whole[768:1024, :]


def put_gates(whole, reset_ref, update_ref, cand_ref, out_ref):
    reset_ref[...] = whole[0:512, :]
    update_ref[...] = whole[512:1024, 0:128]
    cand_ref[...] = whole[512:1024, 128:256]
    out_ref[:, 0:256] = whole[1024:1280, :]
    out_ref[:, 256:512] = whole[1280:1536, :]


def put_mix(whole, value_ref, z_ref, small_ref):
    value_ref[...] = whole[0:512, :]
    z_ref[0:256, :] = whole[512:768, 0:128]
    z_ref[256:512, :] = whole[512:768, 128:256]
    small_ref[...] = whole[768:784, 0:128]


def put_late(whole, emb_ref, rate_ref, beta_ref, eta_ref, small_ref):
    emb_ref[:, 0:256] = whole[0:64, :].astype(BF)
    emb_ref[:, 256:512] = whole[64:128, :].astype(BF)
    rate_ref[...] = whole[128:144, 0:128]
    beta_ref[...] = whole[128:144, 128:256]
    eta_ref[...] = whole[144:160, 0:128]
    small_ref[...] = whole[160:176, 0:128]


def spread(v, me, base, first, blocks):
    far = swap(v, "ch", 2)
    near = swap(v, "ch", 1)
    parts = [v, near, far, swap(far, "ch", 1)]
    n, _, width = v.shape
    step = n if blocks % n == 0 and first % n == 0 else 1
    inner = n // step

    def held(k):
        return lambda r, b, me_ref: (jnp.where(r == k, b, jnp.where(r > k, inner - 1, 0)), 0, 0)

    extra = [] if base is None else [base]
    return pl.pallas_call(
        widen_kernel,
        grid_spec=pltpu.PrefetchScalarGridSpec(
            num_scalar_prefetch=1,
            grid=(4, inner),
            in_specs=[pl.BlockSpec((step, BLK, width), held(k)) for k in range(4)]
            + [pl.BlockSpec(memory_space=pl.ANY)] * len(extra),
            out_specs=pl.BlockSpec(
                (step, BLK, width),
                lambda r, b, me_ref: (((me_ref[0] ^ r) * blocks + first) // step + b, 0, 0),
            ),
        ),
        out_shape=jax.ShapeDtypeStruct((4 * blocks, BLK, width), F32),
        input_output_aliases={5: 0} if extra else {},
        compiler_params=pltpu.CompilerParams(
            dimension_semantics=("arbitrary", "arbitrary"), vmem_limit_bytes=VMEM
        ),
        cost_estimate=cost(4),
        name="widen",
    )(me, *parts, *extra)


def row_block(shape, first=0):
    zeros = (0,) * (len(shape) - 1)
    return pl.BlockSpec((1,) + tuple(shape[1:]), lambda i, *_: (i + first,) + zeros)


def whole_block(shape):
    zeros = (0,) * len(shape)
    return pl.BlockSpec(tuple(shape), lambda i, *_: zeros)


def call(kernel, name, span, us, scalars, rows, fixed, row_outs, fixed_outs, scratch, specs=None, after=()):
    first, count = span
    if specs is None:
        specs = [row_block(v.shape, first if v.shape[0] > count else 0) for v in rows]
    specs = specs + [v[1] if isinstance(v, tuple) else whole_block(v.shape) for v in fixed]
    specs = specs + [pl.BlockSpec(memory_space=pl.ANY)] * len(after)
    fixed = [v[0] if isinstance(v, tuple) else v for v in fixed]
    n = len(scalars) + len(rows) + len(fixed)

    def body(*refs):
        kernel(*refs[:n], *refs[n + len(after) :])

    row_outs = [((count,) + s[1:], t) for s, t in row_outs]
    return pl.pallas_call(
        body,
        grid_spec=pltpu.PrefetchScalarGridSpec(
            num_scalar_prefetch=len(scalars),
            grid=(count,),
            in_specs=specs,
            out_specs=[row_block(s) for s, _ in row_outs] + [whole_block(s) for s, _ in fixed_outs],
            scratch_shapes=[pltpu.VMEM(s, t) for s, t in scratch],
        ),
        out_shape=[jax.ShapeDtypeStruct(s, t) for s, t in row_outs + fixed_outs],
        compiler_params=pltpu.CompilerParams(
            dimension_semantics=("arbitrary",), vmem_limit_bytes=VMEM
        ),
        cost_estimate=cost(us),
        name=name,
    )(*scalars, *rows, *fixed, *after)


def local(
    token_ids, counts, embedding, gain_one, ema_rate, ema_beta, ema_eta, ema_omega, w_value, w_reset,
    w_z, z_scale, z_offset, position_bias, w_update, w_cand, w_out, gain_two, w_up, w_down, cotangent,
):
    batch, span = token_ids.shape
    vocab, width = embedding.shape
    group = lax.axis_size("ch")
    mine = lax.axis_index("ch")
    channels, dims = ema_rate.shape
    z_width = w_z.shape[1]
    units = w_value.shape[1] * group
    seqs = batch // group
    blocks = seqs * span // BLK
    rows = blocks * BLK
    me = mine.astype(jnp.int32).reshape(1)

    pack1 = gather_pack(jnp.concatenate([w_value, w_reset], axis=0))
    halves = width // 2
    pack2 = gather_pack(
        jnp.concatenate(
            [jnp.concatenate([w_update, w_cand], axis=1), w_out[:, :halves], w_out[:, halves:]], axis=0
        )
    )
    pack3 = gather_pack(
        jnp.concatenate([w_up, w_down[:, :halves], w_down[:, halves:]], axis=0)
    )

    par = pl.pallas_call(
        prep_kernel, out_shape=jax.ShapeDtypeStruct((5 * dims + 8, channels), F32), name="prep"
    )(ema_rate.T, ema_beta.T, ema_eta.T, ema_omega[None])
    par = lax.all_gather(par, "ch", axis=1, tiled=True)
    rate = par[:dims]
    g_one, g_two = gain_one[None], gain_two[None]

    ids = lax.dynamic_slice_in_dim(token_ids, mine * seqs, seqs, 0)
    own_counts = lax.dynamic_slice_in_dim(counts, mine * seqs, seqs, 0)
    places = lax.axis_index("seq") * span + jnp.arange(span, dtype=jnp.int32)
    ids = jnp.where(places[None, :] < own_counts[:, None], ids, -1)
    ids_nat = ids.reshape(blocks, 1, BLK)
    ids_tm = ids.reshape(blocks, LANES, STEP).transpose(0, 2, 1).reshape(blocks, 1, BLK)

    bias = jnp.concatenate([position_bias, jnp.zeros((1,), F32)])[None]
    (bias,) = small_call(table_kernel, "table", [], [bias], [((BLK, BLK), F32)])

    row = (blocks, BLK, width)
    row_v = (blocks, BLK, units)
    states = (blocks, dims, LANES, width)
    edge = (blocks, dims, width)
    every = (0, blocks)
    x, emb = call(
        embed_kernel, "embed", every, 4, [], [ids_tm], [embedding, g_one], [(row, F32), (row, BF)], [], []
    )
    ex, lv = call(
        enter_kernel, "enter", every, 6, [], [x], [par], [(states, F32), (edge, F32)], [], []
    )
    se = block_states(lv, rate, span, False)
    (es,) = call(run_kernel, "run", every, 7, [], [x, ex, se], [par], [(row, F32)], [], [])
    vp, rp, mix, zp, up, cp, res = call(
        forward_kernel, "forward", every, 12, [me], [es, x, emb],
        [bias, w_z, z_scale, z_offset, *pack1, *pack2],
        [(row_v, BF), (row_v, BF), (row_v, BF), ((blocks, BLK, z_width), F32), (row, BF), (row, BF),
         (row, F32)],
        [],
        [((width, units), BF), ((width, units), BF), ((width, width), BF), ((width, width), BF),
         ((units, width), BF)],
    )
    at_seq = lax.axis_index("seq").astype(jnp.int32).reshape(1)
    cot = cotangent.reshape(batch * span // BLK, BLK, width)

    def pack_outs(rows):
        return [((2, rows, 256), BF), ((2, rows, 256), BF)]

    out, gr, keep3, send3, gg2 = call(
        ff_kernel, "ff", every, 14, [me], [ids_nat, cot, res], [g_two, *pack3],
        [(row, BF), (row, F32)],
        pack_outs(1024) + [((4, 128), F32)],
        [((width, units), BF), ((units, width), BF), ((width, units), F32), ((units, width), F32)],
        specs=[
            row_block(ids_nat.shape),
            pl.BlockSpec((1, BLK, width), lambda i, me_ref: (me_ref[0] * blocks + i, 0, 0)),
            row_block(res.shape),
        ],
    )
    sum3 = Reduction("ff", at_seq, [keep3], [send3])
    output = spread(out, me, None, 0, blocks).reshape(batch, span, width)

    def half_of(pack, k):
        return [(v, pl.BlockSpec((512, 256), lambda i, *_: (k, 0))) for v in pack]

    gm, ge, direct, keep2, send2 = call(
        gates_back_kernel, "gates_back", every, 17, [me], [es, emb, rp, mix, up, cp, gr],
        [*half_of(pack1, 1), *pack2],
        [(row_v, BF), (row, F32), (row, BF)],
        pack_outs(1536),
        [((width, units), BF), ((width, width), BF), ((width, width), BF), ((units, width), BF),
         ((width, units), F32), ((width, width), F32), ((width, width), F32), ((units, width), F32)],
    )
    sum2 = Reduction("gates", at_seq, [keep2], [send2])
    g, gnv, ae, lb, keep1, send1 = call(
        mix_back_kernel, "mix_back", every, 24, [], [es, x, vp, zp, gm, ge],
        [bias, w_z, z_scale, z_offset, par, gg2, *half_of(pack1, 0)],
        [(row, F32), (row, BF), (states, F32), (edge, F32)],
        pack_outs(896),
        [((width, units), BF), ((width, units), F32), ((width, z_width), F32),
         ((8, z_width), F32), ((BLK, BLK), F32)],
        after=[sum3.shards()],
    )
    sum1 = Reduction("mix", at_seq, [keep1], [send1])
    ar = block_states(lb, rate, span, True)
    sum3.whole_seq()
    pins = [[sum2.shards(), sum1.shards()], [sum2.scatter(1)]]
    parts = [(0, blocks // 2), (blocks // 2, blocks // 2)]
    keep, send = [], []
    input_grad = None
    for part, pin in zip(parts, pins):
        ig, kept, sent = call(
            leave_kernel, "leave", part, 15, [me],
            [ids_tm, emb, x, g, ae, ar, ex, se, direct, gnv],
            [par, g_one],
            [(row, BF)],
            pack_outs(256),
            [((BLK, width), F32), ((dims, LANES, width), F32), ((dims, LANES, width), F32),
             ((vocab, width), F32), ((1, width), F32), ((1, width), F32), ((3 * dims, width), F32)],
            after=pin,
        )
        keep.append(kept)
        send.append(sent)
        input_grad = spread(ig, me, input_grad, part[0], blocks)
    input_grad = input_grad.reshape(batch, span, width)
    last = Reduction("late", at_seq, keep, send)
    last.shards()
    emb_part, grad_rate, grad_beta, grad_eta, late = last.rest(
        put_late,
        [((64, width), BF), ((dims, channels), F32), ((dims, channels), F32),
         ((dims, channels), F32), ((16, 128), F32)],
        (1, 2, 4),
    )
    ge = lax.all_gather(emb_part, "ch", axis=0, tiled=True).astype(F32)
    grad_up, grad_down = small_call(
        put_ff, "ff_join", [], [sum3.whole], [((width, 256), F32), ((256, width), F32)]
    )
    grad_reset, grad_update, grad_cand, grad_out = sum2.rest(
        put_gates,
        [((width, 256), F32), ((width, 128), F32), ((width, 128), F32), ((256, width), F32)],
        (2, 4),
    )
    grad_value, grad_z, small = sum1.rest(
        put_mix, [((width, 256), F32), ((width, z_width), F32), ((16, 128), F32)], (1, 2, 4)
    )
    return (
        output,
        input_grad,
        ge,
        late[4:8].reshape(-1),
        grad_rate.T,
        grad_beta.T,
        grad_eta.T,
        late[0],
        grad_value,
        grad_reset,
        grad_z,
        small[0:2],
        small[2:4],
        small[4:6].reshape(-1)[:-1],
        grad_update,
        grad_cand,
        grad_out,
        small[6:10].reshape(-1),
        grad_up,
        grad_down,
    )


def solution(mesh):
    return jax.shard_map(
        local,
        mesh=mesh,
        in_specs=(
            P(None, "seq"), P(), P(), P(), P("ch", None), P("ch", None), P("ch", None), P("ch"),
            P(None, "ch"), P(None, "ch"), P(), P(), P(), P(), P(None, "ch"), P(None, "ch"),
            P("ch", None), P(), P(None, "ch"), P("ch", None), P(None, "seq", None),
        ),
        out_specs=(
            P(None, "seq", None), P(None, "seq", None), P(), P(), P("ch", None), P("ch", None),
            P("ch", None), P("ch"), P(None, "ch"), P(None, "ch"), P(), P(), P(), P(), P(None, "ch"),
            P(None, "ch"), P("ch", None), P(), P(None, "ch"), P("ch", None),
        ),
        check_vma=False,
    )
```

```python
import functools

import jax
import jax.numpy as jnp
from jax import lax
from jax.experimental import pallas as pl
from jax.experimental.pallas import tpu as pltpu
from jax.sharding import PartitionSpec as P

C = 128
BLK = 256
LANES = 8
STEP = BLK // LANES
EPS = 1e-05
BF = jnp.bfloat16
F32 = jnp.float32
VMEM = 60 * 1024 * 1024


SCALE = 10**9

ORDER = []
LANDED = []


def before():
    ready = ORDER[-1:] + LANDED
    LANDED.clear()
    return ready


def land(*arrays):
    LANDED.extend(arrays)


def done(outs):
    ORDER.append(outs[0] if isinstance(outs, (list, tuple)) else outs)
    return outs


def cost(us):
    return pl.CostEstimate(flops=us * SCALE, bytes_accessed=10**5, transcendentals=0)


def sig(v):
    return 0.5 * jnp.tanh(0.5 * v) + 0.5


def mm(a, b):
    return jnp.dot(a, b, preferred_element_type=F32)


def mm_nt(a, b):
    return lax.dot_general(a, b, (((1,), (1,)), ((), ())), preferred_element_type=F32)


def mm_tn(a, b):
    return lax.dot_general(a, b, (((0,), (0,)), ((), ())), preferred_element_type=F32)


def slope(v, s):
    return s * (1.0 + v * (1.0 - s))


def wide(row):
    return jnp.broadcast_to(row, (LANES, 128))


def lane_iota():
    return lax.broadcasted_iota(jnp.int32, (LANES, 128), 0)


def shift_down(v, k, row):
    return jnp.where(row >= k, pltpu.roll(v, k, axis=0), 0.0)


def shift_up(v, k, row):
    return jnp.where(row < LANES - k, pltpu.roll(v, LANES - k, axis=0), 0.0)


def chain(values, rates, row, shift):
    for k in (1, 2, 4):
        values = [
            v + jnp.exp(r * (-float(STEP * k))) * shift(v, k, row) for v, r in zip(values, rates)
        ]
    return values


def at(t):
    return pl.ds(pl.multiple_of(t * LANES, LANES), LANES)


def one_hot_t(ids, vocab):
    hit = lax.broadcasted_iota(jnp.int32, (vocab, BLK), 0) == ids
    return jnp.where(hit, 1.0, 0.0).astype(BF)


def one_less_exp(rate):
    near = rate * (1.0 - rate * (0.5 - rate * (1.0 / 6.0 - rate * (1.0 / 24.0))))
    return jnp.where(rate < 0.02, near, 1.0 - jnp.exp(-rate))


def prep_kernel(rate_ref, beta_ref, eta_ref, omega_ref, out_ref):
    dims = rate_ref.shape[0]
    rate, beta, eta = rate_ref[...], beta_ref[...], eta_ref[...]
    decay, rise = jnp.exp(-rate), one_less_exp(rate)
    for k, v in enumerate((rate, eta * rise * beta, rise * beta, eta * rise, -decay * eta * beta)):
        out_ref[k * dims : (k + 1) * dims, :] = v
    out_ref[5 * dims :, :] = jnp.broadcast_to(omega_ref[...], (8, omega_ref.shape[1]))


def split3(v):
    parts = []
    for _ in range(3):
        parts.append(v.astype(BF))
        v = v - parts[-1].astype(F32)
    return parts


def skew(v, sign):
    row = lax.broadcasted_iota(jnp.int32, v.shape, 0)
    for b in range(7):
        k = 1 << b
        v = jnp.where((row & k) != 0, pltpu.roll(v, k if sign > 0 else 256 - k, axis=1), v)
    return v


def table_kernel(bias_ref, out_ref):
    v = jnp.broadcast_to(bias_ref[...], (C, 256))
    v = skew(pltpu.roll(v, 256 - (C - 1), axis=1), 1)[:, :C]
    off = jnp.zeros((C, C), F32)
    v = jnp.concatenate(
        [jnp.concatenate([v, off], axis=1), jnp.concatenate([off, v], axis=1)], axis=0
    )
    perm = to_natural(None)
    v = sum(mm_tn(perm, p) for p in split3(v))
    v = sum(mm(p, perm) for p in split3(v))
    r = lax.broadcasted_iota(jnp.int32, (BLK, BLK), 0)
    c = lax.broadcasted_iota(jnp.int32, (BLK, BLK), 1)
    query = (r & (LANES - 1)) * STEP + (r >> 3)
    key = (c & (LANES - 1)) * STEP + (c >> 3)
    seen = jnp.logical_and(key <= query, key >= (query & C))
    out_ref[...] = jnp.where(seen, v, -1e30)


def pack_kernel(wv_ref, wr_ref, wu_ref, wc_ref, wo_ref, up_ref, down_ref, p1_ref, p2_ref, p3_ref):
    p1_ref[0:512, :] = wv_ref[...]
    p1_ref[512:1024, :] = wr_ref[...]
    p2_ref[0:512, 0:128] = wu_ref[...]
    p2_ref[0:512, 128:256] = wc_ref[...]
    p2_ref[512:768, :] = wo_ref[:, 0:256]
    p2_ref[768:1024, :] = wo_ref[:, 256:512]
    p3_ref[0:512, :] = up_ref[...]
    p3_ref[512:768, :] = down_ref[:, 0:256]
    p3_ref[768:1024, :] = down_ref[:, 256:512]


def embed_kernel(ids_ref, tab_ref, gain_ref, x_ref, emb_ref):
    emb = mm_tn(one_hot_t(ids_ref[0], tab_ref.shape[0]), tab_ref[...])
    inv = lax.rsqrt(jnp.mean(emb * emb, axis=-1, keepdims=True) + EPS)
    x_ref[0] = emb * inv * gain_ref[...]
    emb_ref[0] = emb.astype(BF)


def slope_kernel(x_ref, par_ref, e_ref, f_ref):
    dims, width = e_ref.shape[1], e_ref.shape[3]
    half = 8
    for c0 in range(0, width, 128):
        sl = pl.ds(c0, 128)
        for j0 in range(0, dims, half):
            decay = [jnp.exp(-wide(par_ref[pl.ds(j, 1), sl])) for j in range(j0, j0 + half)]

            def body(t, carry):
                e, f = carry
                xt = x_ref[0, at(t), sl]
                f = tuple(d * v + u for d, v, u in zip(decay, f, e))
                e = tuple(d * v + xt for d, v in zip(decay, e))
                return e, f

            zero = x_ref[0, at(0), sl] * 0.0
            e, f = lax.fori_loop(0, STEP, body, ((zero,) * half, (zero,) * half), unroll=4)
            for k in range(half):
                e_ref[0, j0 + k, :, sl] = e[k]
                f_ref[0, j0 + k, :, sl] = f[k]


def enter_kernel(me_ref, x_ref, p0_ref, p1_ref, p2_ref, p3_ref, ex_ref, lv_ref, par_ref):
    dims, width = lv_ref.shape[1:]

    @pl.when(pl.program_id(0) == 0)
    def _():
        for r, ref in enumerate((p0_ref, p1_ref, p2_ref, p3_ref)):
            own = pl.ds(pl.multiple_of((me_ref[0] ^ r) * 128, 128), 128)
            par_ref[:, own] = ref[...]

    row = lane_iota()
    for c0 in range(0, width, 128):
        sl = pl.ds(c0, 128)
        rates = [wide(par_ref[pl.ds(j, 1), sl]) for j in range(dims)]
        decay = [jnp.exp(-r) for r in rates]

        def body(t, s):
            xt = x_ref[0, at(t), sl]
            return tuple(d * v + xt for d, v in zip(decay, s))

        s = lax.fori_loop(
            0, STEP, body, tuple(jnp.zeros((LANES, 128), F32) for _ in range(dims)), unroll=8
        )
        s = chain(list(s), rates, row, shift_down)
        for j in range(dims):
            ex_ref[0, j, :, sl] = shift_down(s[j], 1, row)
            lv_ref[0, pl.ds(j, 1), sl] = s[j][LANES - 1 :, :]


def run_kernel(x_ref, ex_ref, se_ref, par_ref, out_ref):
    dims, width = se_ref.shape[1:]
    place = lane_iota().astype(F32)
    for c0 in range(0, width, 128):
        sl = pl.ds(c0, 128)
        rates = [wide(par_ref[pl.ds(j, 1), sl]) for j in range(dims)]
        decay = [jnp.exp(-r) for r in rates]
        ws = [wide(par_ref[pl.ds(dims + j, 1), sl]) for j in range(dims)]
        omega = wide(par_ref[pl.ds(5 * dims, 1), sl])
        start = tuple(
            ex_ref[0, j, :, sl]
            + jnp.exp(rates[j] * place * (-float(STEP))) * wide(se_ref[0, pl.ds(j, 1), sl])
            for j in range(dims)
        )

        def body(t, s):
            xt = x_ref[0, at(t), sl]
            s = tuple(d * v + xt for d, v in zip(decay, s))
            parts = [w * v for w, v in zip(ws, s)]
            while len(parts) > 1:
                parts = [a + b for a, b in zip(parts[::2], parts[1::2])]
            out_ref[0, at(t), sl] = parts[0] + omega * xt
            return s

        lax.fori_loop(0, STEP, body, start, unroll=4)


def to_natural(mask_row):
    q = lax.broadcasted_iota(jnp.int32, (BLK, BLK), 0)
    r = lax.broadcasted_iota(jnp.int32, (BLK, BLK), 1)
    hit = q == (r & (LANES - 1)) * STEP + (r >> 3)
    if mask_row is not None:
        hit = jnp.logical_and(hit, mask_row >= 0)
    return jnp.where(hit, 1.0, 0.0).astype(BF)


def from_natural(mask_row):
    r = lax.broadcasted_iota(jnp.int32, (BLK, BLK), 0)
    q = lax.broadcasted_iota(jnp.int32, (BLK, BLK), 1)
    hit = q == (r & (LANES - 1)) * STEP + (r >> 3)
    if mask_row is not None:
        hit = jnp.logical_and(hit, mask_row >= 0)
    return jnp.where(hit, 1.0, 0.0).astype(BF)


def fill(refs, rows, to_ref):
    for r, ref in enumerate(refs):
        to_ref[:, pl.ds(r * 256, 256)] = ref[rows : rows + 512, :]


def fill_rows(refs, rows, to_ref):
    for r, ref in enumerate(refs):
        to_ref[pl.ds(r * 256, 256), 0:256] = ref[rows : rows + 256, :]
        to_ref[pl.ds(r * 256, 256), 256:512] = ref[rows + 256 : rows + 512, :]


def fill_gates(me, refs, wu_ref, wc_ref):
    for r, ref in enumerate(refs):
        own = pl.ds(pl.multiple_of((me ^ r) * 128, 128), 128)
        wu_ref[:, own] = ref[0:512, 0:128]
        wc_ref[:, own] = ref[0:512, 128:256]


def slots(keep_ref, send_ref):
    return ((keep_ref, 0), (send_ref, 0), (keep_ref, 1), (send_ref, 1))


def softmax_rows(query, keys, bias, factor):
    scores = mm_nt(query, keys) * factor + bias
    shifted = jnp.exp(scores - jnp.max(scores, axis=-1, keepdims=True))
    return shifted / jnp.sum(shifted, axis=-1, keepdims=True)


def forward_kernel(me_ref, es_ref, x_ref, emb_ref, bias_ref, wz_ref, zs_ref, zo_ref, *rest):
    packs, rest = rest[:8], rest[8:]
    (vp_ref, rp_ref, mix_ref, zp_ref, up_ref, cp_ref, res_ref) = rest[:7]
    (wv_ref, wr_ref, wu_ref, wc_ref, wo_ref) = rest[7:]

    @pl.when(pl.program_id(0) == 0)
    def _():
        fill(packs[0:4], 0, wv_ref)
        fill(packs[0:4], 512, wr_ref)
        fill_gates(me_ref[0], packs[4:8], wu_ref, wc_ref)
        fill_rows(packs[4:8], 512, wo_ref)

    es = es_ref[0]
    e = (es * sig(es)).astype(BF)
    zp = mm(e, wz_ref[...])
    zp_ref[0] = zp
    za = zp * sig(zp)
    query = (za * zs_ref[0:1, :] + zo_ref[0:1, :]).astype(BF)
    keys = (za * zs_ref[1:2, :] + zo_ref[1:2, :]).astype(BF)
    weights = softmax_rows(query, keys, bias_ref[...], zp.shape[-1] ** -0.5).astype(BF)
    vp = mm(x_ref[0].astype(BF), wv_ref[...])
    vp_ref[0] = vp
    values = (vp * sig(vp)).astype(BF)
    mixed = mm(weights, values)
    mix_ref[0] = mixed.astype(BF)
    rp = mm(e, wr_ref[...])
    rp_ref[0] = rp
    gated = (rp * sig(rp) * mixed).astype(BF)
    up = mm(e, wu_ref[...])
    up_ref[0] = up.astype(BF)
    cp = mm(e, wc_ref[...]) + mm(gated, wo_ref[...])
    cp_ref[0] = cp.astype(BF)
    emb = emb_ref[0].astype(F32)
    res_ref[0] = emb + sig(up) * (cp * sig(cp) - emb)


def ff_kernel(me_ref, nat_ref, cot_ref, res_ref, gain_ref, *rest):
    packs, rest = rest[:4], rest[4:]
    out_ref, gr_ref, keep_ref, send_ref, gg_ref, w_up_ref, w_down_ref, au_ref, ad_ref = rest
    step = pl.program_id(0)

    @pl.when(step == 0)
    def _():
        fill(packs, 0, w_up_ref)
        fill_rows(packs, 512, w_down_ref)
        au_ref[...] = jnp.zeros_like(au_ref)
        ad_ref[...] = jnp.zeros_like(ad_ref)
        gg_ref[...] = jnp.zeros_like(gg_ref)

    resid = res_ref[0]
    inv = lax.rsqrt(jnp.mean(resid * resid, axis=-1, keepdims=True) + EPS)
    unit = resid * inv
    gain = gain_ref[...]
    ff_in = (unit * gain).astype(BF)
    hp = mm(ff_in, w_up_ref[...])
    s = sig(hp)
    hidden = (hp * s).astype(BF)
    out = resid + mm(hidden, w_down_ref[...])
    out_ref[0] = mm(to_natural(None), out.astype(BF)).astype(BF)
    grad_out = mm(from_natural(nat_ref[0]), cot_ref[0])
    grad_low = grad_out.astype(BF)
    ad_ref[...] += mm_tn(hidden, grad_low)
    grad_up = (mm_nt(grad_low, w_down_ref[...]) * slope(hp, s)).astype(BF)
    au_ref[...] += mm_tn(ff_in, grad_up)
    grad_norm = mm_nt(grad_up, w_up_ref[...])
    gain_part = jnp.sum(grad_norm * unit, axis=0, keepdims=True)
    for k in range(4):
        gg_ref[k : k + 1, :] += gain_part[:, k * 128 : (k + 1) * 128]
    scaled = grad_norm * gain
    gr_ref[0] = grad_out + inv * (
        scaled - unit * jnp.mean(scaled * unit, axis=-1, keepdims=True)
    )

    @pl.when(step == pl.num_programs(0) - 1)
    def _():
        for r, (ref, slot) in enumerate(slots(keep_ref, send_ref)):
            ref[slot, 0:512, :] = au_ref[:, r * 256 : r * 256 + 256].astype(BF)
            ref[slot, 512:768, :] = ad_ref[r * 256 : r * 256 + 256, 0:256].astype(BF)
            ref[slot, 768:1024, :] = ad_ref[r * 256 : r * 256 + 256, 256:512].astype(BF)


def gates_back_kernel(me_ref, es_ref, emb_ref, rp_ref, mix_ref, up_ref, cp_ref, gr_ref, *rest):
    packs, rest = rest[:8], rest[8:]
    (gm_ref, ge_ref, dir_ref, keep_ref, send_ref) = rest[:5]
    (wr_ref, wu_ref, wc_ref, wo_ref, ar_ref, au_ref, ac_ref, ao_ref) = rest[5:]
    me = me_ref[0]
    step = pl.program_id(0)

    @pl.when(step == 0)
    def _():
        fill(packs[0:4], 0, wr_ref)
        fill_gates(me, packs[4:8], wu_ref, wc_ref)
        fill_rows(packs[4:8], 512, wo_ref)
        for ref in (ar_ref, au_ref, ac_ref, ao_ref):
            ref[...] = jnp.zeros_like(ref)

    es = es_ref[0]
    e_t = (es * sig(es)).astype(BF).T
    emb = emb_ref[0].astype(F32)
    grad_resid = gr_ref[0]
    up = sig(up_ref[0].astype(F32))
    cp = cp_ref[0].astype(F32)
    cs = sig(cp)
    gcp = (grad_resid * up * slope(cp, cs)).astype(BF)
    gup = (grad_resid * (cp * cs - emb) * up * (1.0 - up)).astype(BF)
    dir_ref[0] = (grad_resid * (1.0 - up)).astype(BF)
    ac_ref[...] += mm(e_t, gcp)
    au_ref[...] += mm(e_t, gup)
    rp = rp_ref[0]
    rs = sig(rp)
    reset = rp * rs
    mixed = mix_ref[0].astype(F32)
    ao_ref[...] += mm_tn((reset * mixed).astype(BF), gcp)
    grad_gated = mm_nt(gcp, wo_ref[...])
    gm_ref[0] = (grad_gated * reset).astype(BF)
    grp = (grad_gated * mixed * slope(rp, rs)).astype(BF)
    ar_ref[...] += mm(e_t, grp)
    ge_ref[0] = mm_nt(grp, wr_ref[...]) + mm_nt(gup, wu_ref[...]) + mm_nt(gcp, wc_ref[...])

    @pl.when(step == pl.num_programs(0) - 1)
    def _():
        for r, (ref, slot) in enumerate(slots(keep_ref, send_ref)):
            units = pl.ds(r * 256, 256)
            own = pl.ds(pl.multiple_of((me ^ r) * 128, 128), 128)
            ref[slot, 0:512, :] = ar_ref[:, units].astype(BF)
            ref[slot, 512:1024, 0:128] = au_ref[:, own].astype(BF)
            ref[slot, 512:1024, 128:256] = ac_ref[:, own].astype(BF)
            ref[slot, 1024:1280, :] = ao_ref[units, 0:256].astype(BF)
            ref[slot, 1280:1536, :] = ao_ref[units, 256:512].astype(BF)


def mix_back_kernel(
    es_ref, x_ref, vp_ref, zp_ref, gm_ref, ge_ref,
    bias_ref, wz_ref, zs_ref, zo_ref, par_ref, gg_ref, *rest,
):
    packs, rest = rest[:4], rest[4:]
    (g_ref, gnv_ref, ae_ref, lb_ref, keep_ref, send_ref) = rest[:6]
    (wv_ref, av_ref, az_ref, gz_ref, gb_ref, as_ref) = rest[6:]
    step = pl.program_id(0)

    @pl.when(step == 0)
    def _():
        fill(packs, 0, wv_ref)
        for ref in (av_ref, az_ref, gz_ref, gb_ref):
            ref[...] = jnp.zeros_like(ref)

    es = es_ref[0]
    es_sig = sig(es)
    e_t = (es * es_sig).astype(BF).T
    gm = gm_ref[0]
    zp = zp_ref[0]
    zsig = sig(zp)
    za = zp * zsig
    factor = zp.shape[-1] ** -0.5
    s0, s1 = zs_ref[0:1, :], zs_ref[1:2, :]
    query = (za * s0 + zo_ref[0:1, :]).astype(BF)
    keys = (za * s1 + zo_ref[1:2, :]).astype(BF)
    weights = softmax_rows(query, keys, bias_ref[...], factor)
    vp = vp_ref[0]
    vs = sig(vp)
    values = (vp * vs).astype(BF)
    gvp = (mm_tn(weights.astype(BF), gm) * slope(vp, vs)).astype(BF)
    gnv_ref[0] = mm_nt(gvp, wv_ref[...]).astype(BF)
    av_ref[...] += mm_tn(x_ref[0].astype(BF), gvp)
    gw = mm_nt(gm, values)
    gsf = weights * (gw - jnp.sum(weights * gw, axis=-1, keepdims=True))
    gb_ref[...] += gsf
    gs = gsf.astype(BF)
    gq = mm(gs, keys) * factor
    gk = mm_tn(gs, query) * factor
    gz_ref[0:1, :] += jnp.sum(za * gq, axis=0, keepdims=True)
    gz_ref[1:2, :] += jnp.sum(za * gk, axis=0, keepdims=True)
    gz_ref[2:3, :] += jnp.sum(gq, axis=0, keepdims=True)
    gz_ref[3:4, :] += jnp.sum(gk, axis=0, keepdims=True)
    gzp = ((gq * s0 + gk * s1) * slope(zp, zsig)).astype(BF)
    az_ref[...] += mm(e_t, gzp)
    g_ref[0] = (ge_ref[0] + mm_nt(gzp, wz_ref[...])) * slope(es, es_sig)

    dims, width = lb_ref.shape[1:]
    row = lane_iota()
    for c0 in range(0, width, 128):
        sl = pl.ds(c0, 128)
        rates = [wide(par_ref[pl.ds(j, 1), sl]) for j in range(dims)]
        decay = [jnp.exp(-r) for r in rates]

        def body(t, a):
            gt = g_ref[0, at(STEP - 1 - t), sl]
            return tuple(d * v + gt for d, v in zip(decay, a))

        a = lax.fori_loop(
            0, STEP, body, tuple(jnp.zeros((LANES, 128), F32) for _ in range(dims)), unroll=8
        )
        a = chain(list(a), rates, row, shift_up)
        for j in range(dims):
            ae_ref[0, j, :, sl] = shift_up(a[j], 1, row)
            lb_ref[0, pl.ds(j, 1), sl] = a[j][0:1, :]

    @pl.when(step == pl.num_programs(0) - 1)
    def _():
        perm = to_natural(None)
        v = sum(mm(perm, p) for p in split3(gb_ref[...]))
        v = sum(mm_nt(p, perm) for p in split3(v))
        v = v[:C, :C] + v[C:, C:]
        v = jnp.concatenate([v, jnp.zeros((C, C), F32)], axis=1)
        bias = jnp.sum(pltpu.roll(skew(v, -1), C - 1, axis=1), axis=0, keepdims=True)
        zero = jnp.zeros((6, 128), F32)
        small = jnp.concatenate(
            [gz_ref[0:4, :], bias[:, :128], bias[:, 128:], gg_ref[...], zero], axis=0
        )
        high = small.astype(BF)
        low = (small - high.astype(F32)).astype(BF)
        small = jnp.concatenate([high, low], axis=1)
        as_ref[512:768, 0:128] = az_ref[0:256, :].astype(BF)
        as_ref[512:768, 128:256] = az_ref[256:512, :].astype(BF)
        for r, (ref, slot) in enumerate(slots(keep_ref, send_ref)):
            as_ref[0:512, :] = av_ref[:, r * 256 : r * 256 + 256].astype(BF)
            for k in range(8):
                ref[slot, k * 112 : k * 112 + 96, :] = as_ref[k * 96 : k * 96 + 96, :]
                ref[slot, k * 112 + 96 : k * 112 + 112, :] = small


def adjoint_kernel(x_ref, g_ref, ae_ref, ex_ref, se_ref, par_ref, gn_ref, mn_ref):
    dims, width = se_ref.shape[1:]
    place = lane_iota().astype(F32)
    half = 8
    for c0 in range(0, width, 128):
        sl = pl.ds(c0, 128)
        omega = wide(par_ref[pl.ds(5 * dims, 1), sl])
        for j0 in range(0, dims, half):
            js = range(j0, j0 + half)
            rates = [wide(par_ref[pl.ds(j, 1), sl]) for j in js]
            decay = [jnp.exp(-r) for r in rates]
            ws = [wide(par_ref[pl.ds(dims + j, 1), sl]) for j in js]

            def emit(t, a, gt):
                parts = [w * v for w, v in zip(ws, a)]
                while len(parts) > 1:
                    parts = [p + q for p, q in zip(parts[::2], parts[1::2])]
                if j0 == 0:
                    gn_ref[0, at(t), sl] = parts[0] + omega * gt
                else:
                    gn_ref[0, at(t), sl] += parts[0]

            gt = g_ref[0, at(STEP - 1), sl]
            xt = x_ref[0, at(STEP - 1), sl]
            a = tuple(gt + d * ae_ref[0, j, :, sl] for j, d in zip(js, decay))
            emit(STEP - 1, a, gt)
            m = tuple(xt * v for v in a)
            zero = tuple(jnp.zeros((LANES, 128), F32) for _ in js)

            def body(i, carry):
                a, b, m, n = carry
                t = STEP - 2 - i
                gt = g_ref[0, at(t), sl]
                xt = x_ref[0, at(t), sl]
                b = tuple(u + d * v for d, u, v in zip(decay, a, b))
                a = tuple(gt + d * v for d, v in zip(decay, a))
                emit(t, a, gt)
                m = tuple(u + xt * v for u, v in zip(m, a))
                n = tuple(u + xt * v for u, v in zip(n, b))
                return a, b, m, n

            carry = (a, zero, m, zero)
            for i in range(3):
                carry = body(i, carry)
            a, b, m, n = lax.fori_loop(3, STEP - 1, body, carry, unroll=4)
            for k, j in enumerate(js):
                start = ex_ref[0, j, :, sl] + jnp.exp(rates[k] * place * (-float(STEP))) * wide(
                    se_ref[0, pl.ds(j, 1), sl]
                )
                mn_ref[0, pl.ds(j, 1), sl] = jnp.sum(m[k], axis=0, keepdims=True)
                mn_ref[0, pl.ds(dims + j, 1), sl] = jnp.sum(
                    n[k] + start * (a[k] + decay[k] * b[k]), axis=0, keepdims=True
                )


def leave_kernel(n_parts, me_ref, ids_ref, emb_ref, x_ref, g_ref, ar_ref, ex_ref, se_ref, el_ref, ed_ref,
                 dir_ref, gnv_ref, *rest):
    locals_, rest = rest[: 2 * n_parts], rest[2 * n_parts :]
    par_ref, gain_ref, ig_ref, keep_ref, send_ref = rest[:5]
    gn_ref, ge_ref, go_ref, gg_ref, sum_ref = rest[5:]
    step = pl.program_id(0)
    dims, width = se_ref.shape[1:]

    @pl.when(step == 0)
    def _():
        for ref in (ge_ref, go_ref, gg_ref, sum_ref):
            ref[...] = jnp.zeros_like(ref)

    for k in range(n_parts):

        @pl.when(step == k)
        def _(k=k):
            gn_ref[...] = locals_[2 * k][0]
            sum_ref[0 : 2 * dims, :] += locals_[2 * k + 1][0]

    place = lane_iota().astype(F32)
    for c0 in range(0, width, 128):
        sl = pl.ds(c0, 128)
        rates = [wide(par_ref[pl.ds(j, 1), sl]) for j in range(dims)]
        decay = [jnp.exp(-r) for r in rates]
        ws = [wide(par_ref[pl.ds(dims + j, 1), sl]) for j in range(dims)]
        far = [
            jnp.exp(r * (LANES - 1.0 - place) * (-float(STEP))) * wide(ar_ref[0, pl.ds(j, 1), sl])
            for j, r in enumerate(rates)
        ]
        for j in range(dims):
            start = ex_ref[0, j, :, sl] + jnp.exp(rates[j] * place * (-float(STEP))) * wide(
                se_ref[0, pl.ds(j, 1), sl]
            )
            whole = jnp.exp(rates[j] * (-float(STEP)))
            more_m = far[j] * decay[j] * el_ref[0, j, :, sl]
            more_n = far[j] * (decay[j] * ed_ref[0, j, :, sl] + float(STEP) * whole * start)
            sum_ref[pl.ds(j, 1), sl] += jnp.sum(more_m, axis=0, keepdims=True)
            sum_ref[pl.ds(dims + j, 1), sl] += jnp.sum(more_n, axis=0, keepdims=True)

        def body(i, c):
            t = STEP - 1 - i
            c = tuple(d * v for d, v in zip(decay, c))
            parts = [w * v for w, v in zip(ws, c)]
            while len(parts) > 1:
                parts = [p + q for p, q in zip(parts[::2], parts[1::2])]
            gn_ref[at(t), sl] += parts[0]
            return c

        lax.fori_loop(0, STEP, body, tuple(far), unroll=4)

    go_ref[...] += jnp.sum(g_ref[0] * x_ref[0], axis=0, keepdims=True)
    emb = emb_ref[0].astype(F32)
    inv = lax.rsqrt(jnp.mean(emb * emb, axis=-1, keepdims=True) + EPS)
    unit = emb * inv
    gn = gn_ref[...] + gnv_ref[0].astype(F32)
    gg_ref[...] += jnp.sum(gn * unit, axis=0, keepdims=True)
    scaled = gn * gain_ref[...]
    ig = dir_ref[0].astype(F32) + inv * (
        scaled - unit * jnp.mean(scaled * unit, axis=-1, keepdims=True)
    )
    ig = ig.astype(BF)
    ids = ids_ref[0]
    ig_ref[0] = mm(to_natural(ids), ig).astype(BF)
    ge_ref[...] += mm(one_hot_t(ids, ge_ref.shape[0]), ig)

    @pl.when(step == pl.num_programs(0) - 1)
    def _():
        m, n = sum_ref[0:dims, :], sum_ref[dims : 2 * dims, :]
        rb, er, eb = (par_ref[k * dims : (k + 1) * dims, :] for k in (2, 3, 4))
        rise = one_less_exp(par_ref[0:dims, :])
        sum_ref[0:dims, :] = eb * (rise * n - m)
        sum_ref[dims : 2 * dims, :] = er * m
        sum_ref[2 * dims : 3 * dims, :] = rb * m
        pad = jnp.zeros((8, 128), F32)
        gains = [gg_ref[:, k * 128 : (k + 1) * 128] for k in range(4)]
        for r, (ref, slot) in enumerate(slots(keep_ref, send_ref)):
            own = pl.ds(pl.multiple_of((me_ref[0] ^ r) * 128, 128), 128)
            part = pl.ds(pl.multiple_of((me_ref[0] ^ r) * 64, 64), 64)
            ref[slot, 0:64, :] = ge_ref[part, 0:256].astype(BF)
            ref[slot, 64:128, :] = ge_ref[part, 256:512].astype(BF)
            ref[slot, 128:144, 0:128] = sum_ref[0:dims, own].astype(BF)
            ref[slot, 128:144, 128:256] = sum_ref[dims : 2 * dims, own].astype(BF)
            ref[slot, 144:160, 0:128] = sum_ref[2 * dims : 3 * dims, own].astype(BF)
            ref[slot, 144:160, 128:256] = jnp.concatenate(
                [jnp.broadcast_to(go_ref[:, own], (4, 128)), *gains, pad], axis=0
            ).astype(BF)


def repair(v):
    out = []
    for k in range(0, v.shape[0], 112):
        both = v[k + 96 : k + 112, 0:128] + v[k + 96 : k + 112, 128:256]
        high = both.astype(BF)
        low = (both - high.astype(F32)).astype(BF)
        out += [v[k : k + 96].astype(BF), jnp.concatenate([high, low], axis=1)]
    return jnp.concatenate(out, axis=0)


def plain(v):
    return v.astype(BF)


def add_kernel(n, fix, *refs):
    acc = refs[0][...].astype(F32)
    for ref in refs[1:n]:
        acc = acc + ref[...].astype(F32)
    refs[n][...] = fix(acc[0])
    refs[n + 1][...] = fix(acc[1])


def cut_kernel(bit, fix, at_ref, near_ref, far_ref, keep_ref, send_ref, sum_ref):
    rows = keep_ref.shape[0]
    sum_ref[...] = near_ref[...].astype(F32) + far_ref[...].astype(F32)
    upper = (at_ref[0] // bit) % 2
    keep_ref[...] = fix(sum_ref[pl.ds(pl.multiple_of(upper * rows, rows), rows), :])
    send_ref[...] = fix(sum_ref[pl.ds(pl.multiple_of((1 - upper) * rows, rows), rows), :])


def plain_sum_kernel(near_ref, far_ref, out_ref):
    out_ref[...] = (near_ref[...].astype(F32) + far_ref[...].astype(F32)).astype(out_ref.dtype)


def sum_kernel(fix, *refs):
    refs[-1][...] = fix(total([ref[...] for ref in refs[:-1]]))


def join_kernel(put, at_ref, near_ref, far_ref, *refs):
    rows = near_ref.shape[0]
    upper = at_ref[0] % 2
    refs[-1][pl.ds(pl.multiple_of(upper * rows, rows), rows), :] = near_ref[...].astype(F32)
    refs[-1][pl.ds(pl.multiple_of((1 - upper) * rows, rows), rows), :] = far_ref[...].astype(F32)
    put(refs[-1], *refs[:-1])


def widen_kernel(me_ref, *refs):
    for r, ref in enumerate(refs[:4]):

        @pl.when(pl.program_id(0) == r)
        def _(ref=ref):
            refs[-1][...] = ref[...].astype(F32)


def pairs(axis, bit):
    return [(i, i ^ bit) for i in range(lax.axis_size(axis))]


def swap(v, axis, bit):
    return lax.ppermute(v, axis, pairs(axis, bit))


def hop_kernel(bit, span, backward, at_ref, total_ref, recv_ref, out_ref, rate_ref, next_ref, new_ref):
    place = at_ref[0]
    upper = (place // bit) % 2 == 1
    inside = place % bit
    gap = bit - 1 - inside if backward else inside
    first = jnp.logical_not(upper) if backward else upper
    rate = rate_ref[0 : total_ref.shape[1], :]
    decay = jnp.exp(rate * (-float(bit * span)))
    near = jnp.exp(-rate * (gap * span).astype(F32))
    for k in range(total_ref.shape[0]):
        total, recv = total_ref[k], recv_ref[k]
        new_ref[k] = out_ref[k] + jnp.where(first, recv * near, 0.0)
        next_ref[k] = jnp.where(first, total + decay * recv, recv + decay * total)


def exclusive(total, par, place, span, backward, between):
    count = lax.axis_size("seq")
    out = jnp.zeros_like(total)
    bit = 1
    step = 0
    while bit < count:
        recv = swap(total, "seq", bit)
        if step < len(between):
            between[step]()
        total, out = small_call(
            functools.partial(hop_kernel, bit, span, backward), "hop", [place],
            [total, recv, out, par], [(total.shape, F32)] * 2,
        )
        bit *= 2
        step += 1
    for rest in between[step:]:
        rest()
    return out


def block_states(local, par, place, span, backward, between):
    per = span // BLK
    if per == 1:
        return exclusive(local, par, place, span, backward, between)
    rate = par[: local.shape[1]]
    local = local.reshape((-1, per) + local.shape[1:])
    decay = jnp.exp(rate * (-float(BLK)))
    order = range(per)[::-1] if backward else range(per)
    total = 0.0
    for k in order:
        total = total * decay + local[:, k]
    state = exclusive(total, par, place, span, backward, between)
    states = [None] * per
    for k in order:
        states[k] = state
        state = state * decay + local[:, k]
    return jnp.stack(states, axis=1).reshape((-1,) + rate.shape)


def total(parts):
    acc = parts[0].astype(F32)
    for p in parts[1:]:
        acc = acc + p.astype(F32)
    return acc


def small_call(kernel, name, scalars, args, outs, scratch=()):
    after = before()
    vmem = pl.BlockSpec(memory_space=pltpu.VMEM)
    smem = pl.BlockSpec(memory_space=pltpu.SMEM)
    n = len(scalars) + len(args)

    def body(*refs):
        kernel(*refs[:n], *refs[n + len(after) :])

    made = pl.pallas_call(
        body,
        in_specs=[smem] * len(scalars)
        + [vmem] * len(args)
        + [pl.BlockSpec(memory_space=pl.ANY)] * len(after),
        out_specs=[vmem] * len(outs),
        out_shape=[jax.ShapeDtypeStruct(s, t) for s, t in outs],
        scratch_shapes=[pltpu.VMEM(s, t) for s, t in scratch],
        compiler_params=pltpu.CompilerParams(vmem_limit_bytes=VMEM),
        cost_estimate=cost(2),
        name=name,
    )(*scalars, *args, *after)
    return done(made)


class Reduction:
    def __init__(self, name, at, keeps, sends, fix=plain):
        self.name, self.at, self.fix = name, at, fix
        self.args = list(keeps) + [swap(s, "ch", 1) for s in sends]
        self.wide = lax.axis_size("seq") != 8

    def shards(self):
        shape = self.args[0].shape[1:]
        self.near, far = small_call(
            functools.partial(add_kernel, len(self.args), self.fix), self.name + "_add", [],
            self.args, [(shape, BF), (shape, BF)],
        )
        self.far = swap(far, "ch", 2)
        return [self.near]

    def both(self):
        shape = self.args[0].shape
        (self.near,) = small_call(
            functools.partial(sum_kernel, self.fix), self.name + "_add", [], self.args, [(shape, BF)]
        )
        if self.wide:
            self.near = lax.psum(self.near.astype(F32), "seq").astype(BF)
            self.far = jnp.zeros_like(self.near)
        else:
            self.far = swap(self.near, "seq", 1)

    def split(self):
        shape = self.args[0].shape[1:]
        self.near, far = small_call(
            functools.partial(add_kernel, 2, self.fix), self.name + "_split", [],
            [self.near, self.far], [(shape, BF), (shape, BF)],
        )
        self.far = swap(far, "ch", 2)

    def whole_seq(self):
        kind = F32 if self.wide else BF
        (v,) = small_call(
            plain_sum_kernel, self.name + "_sum", [], [self.near, self.far], [(self.near.shape, kind)]
        )
        self.whole = lax.psum(v, "seq")

    def halve(self):
        if self.wide:
            return []
        rows = self.near.shape[0]
        self.near, far = small_call(
            functools.partial(cut_kernel, 1, self.fix), self.name + "_cut", [self.at],
            [self.near, self.far], [((rows // 2, 256), BF)] * 2, [((rows, 256), F32)],
        )
        self.far = swap(far, "seq", 1)
        return [self.near]

    def hop(self, bit):
        if self.wide:
            return []
        (self.near,) = small_call(
            functools.partial(sum_kernel, self.fix), self.name + "_sum", [], [self.near, self.far],
            [(self.near.shape, BF)],
        )
        self.far = swap(self.near, "seq", bit)
        return [self.near]

    def join(self, put, outs, halved=True):
        if self.wide and halved:
            self.whole_seq()
            return small_call(put, self.name + "_join", [], [self.whole], outs)
        if halved:
            shape = (2 * self.near.shape[0], 256)
            return small_call(
                functools.partial(join_kernel, put), self.name + "_join", [self.at],
                [self.near, self.far], outs, [(shape, F32)],
            )

        def finish(near_ref, far_ref, *refs):
            refs[-1][...] = near_ref[...].astype(F32) + far_ref[...].astype(F32)
            put(refs[-1], *refs[:-1])

        return small_call(
            finish, self.name + "_join", [], [self.near, self.far], outs,
            [(self.near.shape, F32)],
        )


def put_ff(whole, up_ref, down_ref):
    up_ref[...] = whole[0:512, :].astype(F32)
    down_ref[:, 0:256] = whole[512:768, :].astype(F32)
    down_ref[:, 256:512] = whole[768:1024, :].astype(F32)


def put_gates(whole, reset_ref, update_ref, cand_ref, out_ref):
    reset_ref[...] = whole[0:512, :]
    update_ref[...] = whole[512:1024, 0:128]
    cand_ref[...] = whole[512:1024, 128:256]
    out_ref[:, 0:256] = whole[1024:1280, :]
    out_ref[:, 256:512] = whole[1280:1536, :]


def put_mix(whole, value_ref, z_ref, scale_ref, offset_ref, bias_ref, gain_ref):
    for k in range(8):
        part = whole[k * 112 : k * 112 + 96, :]
        if k < 5:
            value_ref[k * 96 : k * 96 + 96, :] = part
        elif k == 5:
            value_ref[480:512, :] = part[0:32]
            z_ref[0:64, :] = part[32:96, 0:128]
            z_ref[256:320, :] = part[32:96, 128:256]
        else:
            first = (k - 6) * 96 + 64
            z_ref[first : first + 96, :] = part[:, 0:128]
            z_ref[256 + first : 256 + first + 96, :] = part[:, 128:256]
    small = whole[96:112, 0:128] + whole[96:112, 128:256]
    scale_ref[...] = small[0:2]
    offset_ref[...] = small[2:4]
    bias_ref[...] = jnp.concatenate([small[4:5], small[5:6]], axis=1)[:, :255]
    for k in range(4):
        gain_ref[:, k * 128 : k * 128 + 128] = small[6 + k : 7 + k]


def put_late(whole, emb_ref, rate_ref, beta_ref, eta_ref, omega_ref, gain_ref):
    emb_ref[:, 0:256] = whole[0:64, :].astype(BF)
    emb_ref[:, 256:512] = whole[64:128, :].astype(BF)
    rate_ref[...] = whole[128:144, 0:128]
    beta_ref[...] = whole[128:144, 128:256]
    eta_ref[...] = whole[144:160, 0:128]
    omega_ref[...] = whole[144:145, 128:256]
    for k in range(4):
        gain_ref[:, k * 128 : k * 128 + 128] = whole[148 + k : 149 + k, 128:256]


def spread(v):
    far = swap(v, "ch", 2)
    return [v, swap(v, "ch", 1), far, swap(far, "ch", 1)]


def widen(parts, me, base, first, blocks):
    n, _, width = parts[0].shape
    step = n if blocks % n == 0 and first % n == 0 else 1
    inner = n // step

    def held(k):
        return lambda r, b, me_ref: (jnp.where(r == k, b, jnp.where(r > k, inner - 1, 0)), 0, 0)

    extra = ([] if base is None else [base]) + before()
    return done(
        pl.pallas_call(
            widen_kernel,
            grid_spec=pltpu.PrefetchScalarGridSpec(
                num_scalar_prefetch=1,
                grid=(4, inner),
                in_specs=[pl.BlockSpec((step, BLK, width), held(k)) for k in range(4)]
                + [pl.BlockSpec(memory_space=pl.ANY)] * len(extra),
                out_specs=pl.BlockSpec(
                    (step, BLK, width),
                    lambda r, b, me_ref: (((me_ref[0] ^ r) * blocks + first) // step + b, 0, 0),
                ),
            ),
            out_shape=jax.ShapeDtypeStruct((4 * blocks, BLK, width), F32),
            input_output_aliases={} if base is None else {5: 0},
            compiler_params=pltpu.CompilerParams(
                dimension_semantics=("arbitrary", "arbitrary"), vmem_limit_bytes=VMEM
            ),
            cost_estimate=cost(4),
            name="widen",
        )(me, *parts, *extra)
    )


def row_block(shape, first=0):
    zeros = (0,) * (len(shape) - 1)
    return pl.BlockSpec((1,) + tuple(shape[1:]), lambda i, *_: (i + first,) + zeros)


def whole_block(shape):
    zeros = (0,) * len(shape)
    return pl.BlockSpec(tuple(shape), lambda i, *_: zeros)


def call(kernel, name, span, us, scalars, rows, fixed, row_outs, fixed_outs, scratch, specs=None):
    first, count = span
    after = before()
    if specs is None:
        specs = [row_block(v.shape, first if v.shape[0] > count else 0) for v in rows]
    specs = specs + [v[1] if isinstance(v, tuple) else whole_block(v.shape) for v in fixed]
    specs = specs + [pl.BlockSpec(memory_space=pl.ANY)] * len(after)
    fixed = [v[0] if isinstance(v, tuple) else v for v in fixed]
    n = len(scalars) + len(rows) + len(fixed)

    def body(*refs):
        kernel(*refs[:n], *refs[n + len(after) :])

    row_outs = [((count,) + s[1:], t) for s, t in row_outs]
    made = pl.pallas_call(
        body,
        grid_spec=pltpu.PrefetchScalarGridSpec(
            num_scalar_prefetch=len(scalars),
            grid=(count,),
            in_specs=specs,
            out_specs=[row_block(s) for s, _ in row_outs] + [whole_block(s) for s, _ in fixed_outs],
            scratch_shapes=[pltpu.VMEM(s, t) for s, t in scratch],
        ),
        out_shape=[jax.ShapeDtypeStruct(s, t) for s, t in row_outs + fixed_outs],
        compiler_params=pltpu.CompilerParams(
            dimension_semantics=("arbitrary",), vmem_limit_bytes=VMEM
        ),
        cost_estimate=cost(us),
        name=name,
    )(*scalars, *rows, *fixed, *after)
    return done(made)


def local(
    token_ids, counts, embedding, gain_one, ema_rate, ema_beta, ema_eta, ema_omega, w_value, w_reset,
    w_z, z_scale, z_offset, position_bias, w_update, w_cand, w_out, gain_two, w_up, w_down, cotangent,
):
    batch, span = token_ids.shape
    vocab, width = embedding.shape
    group = lax.axis_size("ch")
    mine = lax.axis_index("ch")
    channels, dims = ema_rate.shape
    z_width = w_z.shape[1]
    units = w_value.shape[1] * group
    seqs = batch // group
    blocks = seqs * span // BLK
    rows = blocks * BLK
    me = mine.astype(jnp.int32).reshape(1)

    ORDER.clear()
    LANDED.clear()
    (par,) = small_call(
        prep_kernel, "prep", [], [ema_rate.T, ema_beta.T, ema_eta.T, ema_omega[None]],
        [((5 * dims + 8, channels), F32)],
    )
    pars = [par] + [swap(par, "ch", r) for r in (1, 2, 3)]
    packs = small_call(
        pack_kernel, "pack", [], [w_value, w_reset, w_update, w_cand, w_out, w_up, w_down],
        [((1024, 256), BF)] * 3,
    )
    pack1, pack2, pack3 = (spread(v) for v in packs)
    g_one, g_two = gain_one[None], gain_two[None]

    ids = lax.dynamic_slice_in_dim(token_ids, mine * seqs, seqs, 0)
    own_counts = lax.dynamic_slice_in_dim(counts, mine * seqs, seqs, 0)
    places = lax.axis_index("seq") * span + jnp.arange(span, dtype=jnp.int32)
    ids = jnp.where(places[None, :] < own_counts[:, None], ids, -1)
    ids_nat = ids.reshape(blocks, 1, BLK)
    ids_tm = ids.reshape(blocks, LANES, STEP).transpose(0, 2, 1).reshape(blocks, 1, BLK)

    row = (blocks, BLK, width)
    row_v = (blocks, BLK, units)
    states = (blocks, dims, LANES, width)
    edge = (blocks, dims, width)
    every = (0, blocks)
    x, emb = call(
        embed_kernel, "embed", every, 4, [], [ids_tm], [embedding, g_one], [(row, F32), (row, BF)], [], []
    )
    ex, lv, par = call(
        enter_kernel, "enter", every, 6, [me], [x], pars, [(states, F32), (edge, F32)],
        [((5 * dims + 8, width), F32)], [],
    )
    made = {}

    def slopes():
        made["slope"] = call(
            slope_kernel, "slope", every, 8, [], [x], [par], [(states, F32), (states, F32)], [], []
        )

    def table():
        bias = jnp.concatenate([position_bias, jnp.zeros((1,), F32)])[None]
        (made["bias"],) = small_call(table_kernel, "table", [], [bias], [((BLK, BLK), F32)])

    at_seq = lax.axis_index("seq").astype(jnp.int32).reshape(1)
    steps = [
        lambda: None,
        slopes,
        table,
    ]
    se = block_states(lv, par, at_seq, span, False, steps)
    el, ed = made["slope"]
    bias = made["bias"]
    (es,) = call(run_kernel, "run", every, 7, [], [x, ex, se], [par], [(row, F32)], [], [])
    vp, rp, mix, zp, up, cp, res = call(
        forward_kernel, "forward", every, 12, [me], [es, x, emb],
        [bias, w_z, z_scale, z_offset, *pack1, *pack2],
        [(row_v, F32), (row_v, F32), (row_v, BF), ((blocks, BLK, z_width), F32), (row, BF), (row, BF),
         (row, F32)],
        [],
        [((width, units), BF), ((width, units), BF), ((width, width), BF), ((width, width), BF),
         ((units, width), BF)],
    )
    cot = cotangent.reshape(batch * span // BLK, BLK, width)

    def pack_outs(rows):
        return [((2, rows, 256), BF), ((2, rows, 256), BF)]

    out, gr, keep3, send3, gg2 = call(
        ff_kernel, "ff", every, 14, [me], [ids_nat, cot, res], [g_two, *pack3],
        [(row, BF), (row, F32)],
        pack_outs(1024) + [((4, 128), F32)],
        [((width, units), BF), ((units, width), BF), ((width, units), F32), ((units, width), F32)],
        specs=[
            row_block(ids_nat.shape),
            pl.BlockSpec((1, BLK, width), lambda i, me_ref: (me_ref[0] * blocks + i, 0, 0)),
            row_block(res.shape),
        ],
    )
    sum3 = Reduction("ff", at_seq, [keep3], [send3])
    out = spread(out)

    def half_of(pack, k):
        return [(v, pl.BlockSpec((512, 256), lambda i, *_: (k, 0))) for v in pack]

    gm, ge, direct, keep2, send2 = call(
        gates_back_kernel, "gates_back", every, 17, [me], [es, emb, rp, mix, up, cp, gr],
        [*half_of(pack1, 1), *pack2],
        [(row_v, BF), (row, F32), (row, BF)],
        pack_outs(1536),
        [((width, units), BF), ((width, width), BF), ((width, width), BF), ((units, width), BF),
         ((width, units), F32), ((width, width), F32), ((width, width), F32), ((units, width), F32)],
    )
    sum2 = Reduction("gates", at_seq, [keep2], [send2])
    land(out[1])
    sum3.shards()
    g, gnv, ae, lb, keep1, send1 = call(
        mix_back_kernel, "mix_back", every, 24, [], [es, x, vp, zp, gm, ge],
        [bias, w_z, z_scale, z_offset, par, gg2, *half_of(pack1, 0)],
        [(row, F32), (row, BF), (states, F32), (edge, F32)],
        pack_outs(896),
        [((width, units), BF), ((width, units), F32), ((width, z_width), F32),
         ((8, z_width), F32), ((BLK, BLK), F32), ((768, 256), BF)],
    )
    sum1 = Reduction("mix", at_seq, [keep1], [send1], repair)
    locals_ = []

    def adjoint():
        if len(locals_) < blocks:
            locals_.append(
                call(
                    adjoint_kernel, "adjoint", (len(locals_), 1), 6, [], [x, g, ae, ex, se], [par],
                    [(row, F32), ((blocks, 2 * dims, width), F32)], [], [],
                )
            )

    def between0():
        land(out[2])
        sum2.shards()
        sum3.whole_seq()
        adjoint()

    def between1():
        land(out[3])
        adjoint()

    def between2():
        sum1.shards()
        adjoint()
        sum2.halve()

    ar = block_states(lb, par, at_seq, span, True, [between0, between1, between2])
    while len(locals_) < blocks:
        adjoint()
    sum2.hop(2)
    sum1.halve()
    parts = [(0, blocks // 2), (blocks // 2, blocks // 2)]
    keep, send, grads = [], [], []
    for part in parts:
        rows_in = [ids_tm, emb, x, g, ar, ex, se, el, ed, direct, gnv]
        mine_in = [v for k in range(part[0], part[0] + part[1]) for v in locals_[k]]
        ig, kept, sent = call(
            functools.partial(leave_kernel, part[1]), "leave", part, 8, [me],
            rows_in, [*mine_in, par, g_one],
            [(row, BF)],
            pack_outs(160),
            [((BLK, width), F32), ((vocab, width), F32), ((1, width), F32), ((1, width), F32),
             ((3 * dims, width), F32)],
        )
        keep.append(kept)
        send.append(sent)
        grads.append(spread(ig))
        if len(grads) == 1:
            sum1.hop(2)
            sum2.hop(4)
    last = Reduction("late", at_seq, keep, send)
    sum1.hop(4)
    last.both()
    land(grads[0][1], grads[0][2])
    output = widen(out, me, None, 0, blocks).reshape(batch, span, width)
    land(grads[1][1])
    last.hop(2)
    land(grads[0][3])
    sum2.hop(1)
    sum1.hop(1)
    last.hop(4)
    land(grads[1][2])
    input_grad = widen(grads[0], me, None, parts[0][0], blocks)
    grad_reset, grad_update, grad_cand, grad_out = sum2.join(
        put_gates,
        [((width, 256), F32), ((width, 128), F32), ((width, 128), F32), ((256, width), F32)],
    )
    last.split()
    grad_value, grad_z, grad_scale, grad_offset, grad_bias, grad_two = sum1.join(
        put_mix,
        [((width, 256), F32), ((width, z_width), F32), ((2, z_width), F32), ((2, z_width), F32),
         ((1, 255), F32), ((1, width), F32)],
    )
    grad_up, grad_down = small_call(
        put_ff, "ff_join", [], [sum3.whole], [((width, 256), F32), ((256, width), F32)]
    )
    emb_part, grad_rate, grad_beta, grad_eta, grad_omega, grad_one = last.join(
        put_late,
        [((64, width), BF), ((dims, channels), F32), ((dims, channels), F32),
         ((dims, channels), F32), ((1, channels), F32), ((1, width), F32)],
        False,
    )
    ge = lax.all_gather(emb_part, "ch", axis=0, tiled=True).astype(F32)
    input_grad = widen(grads[1], me, input_grad, parts[1][0], blocks).reshape(batch, span, width)
    return (
        output,
        input_grad,
        ge,
        grad_one[0],
        grad_rate.T,
        grad_beta.T,
        grad_eta.T,
        grad_omega[0],
        grad_value,
        grad_reset,
        grad_z,
        grad_scale,
        grad_offset,
        grad_bias[0],
        grad_update,
        grad_cand,
        grad_out,
        grad_two[0],
        grad_up,
        grad_down,
    )


def solution(mesh):
    return jax.shard_map(
        local,
        mesh=mesh,
        in_specs=(
            P(None, "seq"), P(), P(), P(), P("ch", None), P("ch", None), P("ch", None), P("ch"),
            P(None, "ch"), P(None, "ch"), P(), P(), P(), P(), P(None, "ch"), P(None, "ch"),
            P("ch", None), P(), P(None, "ch"), P("ch", None), P(None, "seq", None),
        ),
        out_specs=(
            P(None, "seq", None), P(None, "seq", None), P(), P(), P("ch", None), P("ch", None),
            P("ch", None), P("ch"), P(None, "ch"), P(None, "ch"), P(), P(), P(), P(), P(None, "ch"),
            P(None, "ch"), P("ch", None), P(), P(None, "ch"), P("ch", None),
        ),
        check_vma=False,
    )
```

```python
import functools

import jax
import jax.numpy as jnp
from jax import lax
from jax.experimental import pallas as pl
from jax.experimental.pallas import tpu as pltpu
from jax.sharding import PartitionSpec as P

C = 128
BLK = 256
LANES = 8
STEP = BLK // LANES
EPS = 1e-05
BF = jnp.bfloat16
F32 = jnp.float32
VMEM = 60 * 1024 * 1024
PER = 4


SCALE = 10**9

ORDER = []
LANDED = []


def before():
    ready = ORDER[-1:] + LANDED
    LANDED.clear()
    return ready


def land(*arrays):
    LANDED.extend(arrays)


def done(outs):
    ORDER.append(outs[0] if isinstance(outs, (list, tuple)) else outs)
    return outs


def cost(us):
    return pl.CostEstimate(flops=us * SCALE, bytes_accessed=10**5, transcendentals=0)


def sig(v):
    return 0.5 * jnp.tanh(0.5 * v) + 0.5


def mm(a, b):
    return jnp.dot(a, b, preferred_element_type=F32)


def mm_nt(a, b):
    return lax.dot_general(a, b, (((1,), (1,)), ((), ())), preferred_element_type=F32)


def mm_tn(a, b):
    return lax.dot_general(a, b, (((0,), (0,)), ((), ())), preferred_element_type=F32)


def slope(v, s):
    return s * (1.0 + v * (1.0 - s))


def wide(row):
    return jnp.broadcast_to(row, (LANES, 128))


def lane_iota():
    return lax.broadcasted_iota(jnp.int32, (LANES, 128), 0)


def shift_down(v, k, row):
    return jnp.where(row >= k, pltpu.roll(v, k, axis=0), 0.0)


def shift_up(v, k, row):
    return jnp.where(row < LANES - k, pltpu.roll(v, LANES - k, axis=0), 0.0)


def chain(values, rates, row, shift):
    for k in (1, 2, 4):
        values = [
            v + jnp.exp(r * (-float(STEP * k))) * shift(v, k, row) for v, r in zip(values, rates)
        ]
    return values


def at(t):
    return pl.ds(pl.multiple_of(t * LANES, LANES), LANES)


def one_hot_t(ids, vocab):
    hit = lax.broadcasted_iota(jnp.int32, (vocab, BLK), 0) == ids
    return jnp.where(hit, 1.0, 0.0).astype(BF)


def one_less_exp(rate):
    near = rate * (1.0 - rate * (0.5 - rate * (1.0 / 6.0 - rate * (1.0 / 24.0))))
    return jnp.where(rate < 0.02, near, 1.0 - jnp.exp(-rate))


def prep_kernel(rate_ref, beta_ref, eta_ref, omega_ref, out_ref):
    dims = rate_ref.shape[0]
    rate, beta, eta = rate_ref[...], beta_ref[...], eta_ref[...]
    decay, rise = jnp.exp(-rate), one_less_exp(rate)
    for k, v in enumerate((rate, eta * rise * beta, rise * beta, eta * rise, -decay * eta * beta)):
        out_ref[k * dims : (k + 1) * dims, :] = v
    out_ref[5 * dims :, :] = jnp.broadcast_to(omega_ref[...], (8, omega_ref.shape[1]))


def split3(v):
    parts = []
    for _ in range(3):
        parts.append(v.astype(BF))
        v = v - parts[-1].astype(F32)
    return parts


def skew(v, sign):
    row = lax.broadcasted_iota(jnp.int32, v.shape, 0)
    for b in range(7):
        k = 1 << b
        v = jnp.where((row & k) != 0, pltpu.roll(v, k if sign > 0 else 256 - k, axis=1), v)
    return v


def table_kernel(bias_ref, out_ref):
    v = jnp.broadcast_to(bias_ref[...], (C, 256))
    v = skew(pltpu.roll(v, 256 - (C - 1), axis=1), 1)[:, :C]
    off = jnp.zeros((C, C), F32)
    v = jnp.concatenate(
        [jnp.concatenate([v, off], axis=1), jnp.concatenate([off, v], axis=1)], axis=0
    )
    perm = to_natural(None)
    v = sum(mm_tn(perm, p) for p in split3(v))
    v = sum(mm(p, perm) for p in split3(v))
    r = lax.broadcasted_iota(jnp.int32, (BLK, BLK), 0)
    c = lax.broadcasted_iota(jnp.int32, (BLK, BLK), 1)
    query = (r & (LANES - 1)) * STEP + (r >> 3)
    key = (c & (LANES - 1)) * STEP + (c >> 3)
    seen = jnp.logical_and(key <= query, key >= (query & C))
    out_ref[...] = jnp.where(seen, v, -1e30)


def pack_kernel(wv_ref, wr_ref, wu_ref, wc_ref, wo_ref, up_ref, down_ref, out_ref):
    out_ref[0:512, :] = wv_ref[...]
    out_ref[512:1024, :] = wr_ref[...]
    out_ref[1024:1536, 0:128] = wu_ref[...]
    out_ref[1024:1536, 128:256] = wc_ref[...]
    out_ref[1536:1792, :] = wo_ref[:, 0:256]
    out_ref[1792:2048, :] = wo_ref[:, 256:512]
    out_ref[2048:2560, :] = up_ref[...]
    out_ref[2560:2816, :] = down_ref[:, 0:256]
    out_ref[2816:3072, :] = down_ref[:, 256:512]


def embed_kernel(ids_ref, tab_ref, gain_ref, x_ref, emb_ref):
    emb = mm_tn(one_hot_t(ids_ref[0], tab_ref.shape[0]), tab_ref[...])
    inv = lax.rsqrt(jnp.mean(emb * emb, axis=-1, keepdims=True) + EPS)
    x_ref[0] = emb * inv * gain_ref[...]
    emb_ref[0] = emb.astype(BF)


def slope_kernel(x_ref, par_ref, e_ref, f_ref):
    dims, width = e_ref.shape[1], e_ref.shape[3]
    half = 8
    for c0 in range(0, width, 128):
        sl = pl.ds(c0, 128)
        for j0 in range(0, dims, half):
            decay = [jnp.exp(-wide(par_ref[pl.ds(j, 1), sl])) for j in range(j0, j0 + half)]

            def body(t, carry):
                e, f = carry
                xt = x_ref[0, at(t), sl]
                f = tuple(d * v + u for d, v, u in zip(decay, f, e))
                e = tuple(d * v + xt for d, v in zip(decay, e))
                return e, f

            zero = x_ref[0, at(0), sl] * 0.0
            e, f = lax.fori_loop(0, STEP, body, ((zero,) * half, (zero,) * half), unroll=8)
            for k in range(half):
                e_ref[0, j0 + k, :, sl] = e[k]
                f_ref[0, j0 + k, :, sl] = f[k]


def enter_kernel(me_ref, x_ref, p0_ref, p1_ref, p2_ref, p3_ref, ex_ref, lv_ref, par_ref):
    dims, width = lv_ref.shape[1:]

    @pl.when(pl.program_id(0) == 0)
    def _():
        for r, ref in enumerate((p0_ref, p1_ref, p2_ref, p3_ref)):
            own = pl.ds(pl.multiple_of((me_ref[0] ^ r) * 128, 128), 128)
            par_ref[:, own] = ref[...]

    row = lane_iota()
    for c0 in range(0, width, 128):
        sl = pl.ds(c0, 128)
        rates = [wide(par_ref[pl.ds(j, 1), sl]) for j in range(dims)]
        decay = [jnp.exp(-r) for r in rates]

        def body(t, s):
            xt = x_ref[0, at(t), sl]
            return tuple(d * v + xt for d, v in zip(decay, s))

        s = lax.fori_loop(
            0, STEP, body, tuple(jnp.zeros((LANES, 128), F32) for _ in range(dims)), unroll=32
        )
        s = chain(list(s), rates, row, shift_down)
        for j in range(dims):
            ex_ref[0, j, :, sl] = shift_down(s[j], 1, row)
            lv_ref[0, pl.ds(j, 1), sl] = s[j][LANES - 1 :, :]


def run_kernel(x_ref, ex_ref, se_ref, par_ref, out_ref):
    dims, width = se_ref.shape[1:]
    place = lane_iota().astype(F32)
    for c0 in range(0, width, 128):
        sl = pl.ds(c0, 128)
        rates = [wide(par_ref[pl.ds(j, 1), sl]) for j in range(dims)]
        decay = [jnp.exp(-r) for r in rates]
        ws = [wide(par_ref[pl.ds(dims + j, 1), sl]) for j in range(dims)]
        omega = wide(par_ref[pl.ds(5 * dims, 1), sl])
        start = tuple(
            ex_ref[0, j, :, sl]
            + jnp.exp(rates[j] * place * (-float(STEP))) * wide(se_ref[0, pl.ds(j, 1), sl])
            for j in range(dims)
        )

        def body(t, s):
            xt = x_ref[0, at(t), sl]
            s = tuple(d * v + xt for d, v in zip(decay, s))
            parts = [w * v for w, v in zip(ws, s)]
            while len(parts) > 1:
                parts = [a + b for a, b in zip(parts[::2], parts[1::2])]
            out_ref[0, at(t), sl] = parts[0] + omega * xt
            return s

        lax.fori_loop(0, STEP, body, start, unroll=8)


def to_natural(mask_row):
    q = lax.broadcasted_iota(jnp.int32, (BLK, BLK), 0)
    r = lax.broadcasted_iota(jnp.int32, (BLK, BLK), 1)
    hit = q == (r & (LANES - 1)) * STEP + (r >> 3)
    if mask_row is not None:
        hit = jnp.logical_and(hit, mask_row >= 0)
    return jnp.where(hit, 1.0, 0.0).astype(BF)


def from_natural(mask_row):
    r = lax.broadcasted_iota(jnp.int32, (BLK, BLK), 0)
    q = lax.broadcasted_iota(jnp.int32, (BLK, BLK), 1)
    hit = q == (r & (LANES - 1)) * STEP + (r >> 3)
    if mask_row is not None:
        hit = jnp.logical_and(hit, mask_row >= 0)
    return jnp.where(hit, 1.0, 0.0).astype(BF)


def read(ref):
    return ref[...].reshape((-1, ref.shape[-1]))


def write(ref, v):
    ref[...] = v.reshape(ref.shape)


def fill(refs, rows, to_ref):
    for r, ref in enumerate(refs):
        to_ref[:, pl.ds(r * 256, 256)] = ref[rows : rows + 512, :]


def fill_rows(refs, rows, to_ref):
    for r, ref in enumerate(refs):
        to_ref[pl.ds(r * 256, 256), 0:256] = ref[rows : rows + 256, :]
        to_ref[pl.ds(r * 256, 256), 256:512] = ref[rows + 256 : rows + 512, :]


def fill_gates(me, refs, wu_ref, wc_ref):
    for r, ref in enumerate(refs):
        own = pl.ds(pl.multiple_of((me ^ r) * 128, 128), 128)
        wu_ref[:, own] = ref[0:512, 0:128]
        wc_ref[:, own] = ref[0:512, 128:256]


def slots(keep_ref, send_ref):
    return ((keep_ref, 0), (send_ref, 0), (keep_ref, 1), (send_ref, 1))


def softmax_rows(query, keys, bias, factor):
    scores = mm_nt(query, keys) * factor + bias
    shifted = jnp.exp(scores - jnp.max(scores, axis=-1, keepdims=True))
    return shifted / jnp.sum(shifted, axis=-1, keepdims=True)


def forward_kernel(me_ref, es_ref, x_ref, emb_ref, bias_ref, wz_ref, zs_ref, zo_ref, *rest):
    packs, rest = rest[:8], rest[8:]
    (vp_ref, rp_ref, mix_ref, zp_ref, up_ref, cp_ref, res_ref) = rest[:7]
    (wv_ref, wr_ref, wu_ref, wc_ref, wo_ref) = rest[7:]

    @pl.when(pl.program_id(0) == 0)
    def _():
        fill(packs[0:4], 0, wv_ref)
        fill(packs[0:4], 512, wr_ref)
        fill_gates(me_ref[0], packs[4:8], wu_ref, wc_ref)
        fill_rows(packs[4:8], 512, wo_ref)

    es = es_ref[0]
    e = (es * sig(es)).astype(BF)
    zp = mm(e, wz_ref[...])
    zp_ref[0] = zp
    za = zp * sig(zp)
    query = (za * zs_ref[0:1, :] + zo_ref[0:1, :]).astype(BF)
    keys = (za * zs_ref[1:2, :] + zo_ref[1:2, :]).astype(BF)
    weights = softmax_rows(query, keys, bias_ref[...], zp.shape[-1] ** -0.5).astype(BF)
    vp = mm(x_ref[0].astype(BF), wv_ref[...])
    vp_ref[0] = vp
    values = (vp * sig(vp)).astype(BF)
    mixed = mm(weights, values)
    mix_ref[0] = mixed.astype(BF)
    rp = mm(e, wr_ref[...])
    rp_ref[0] = rp
    gated = (rp * sig(rp) * mixed).astype(BF)
    up = mm(e, wu_ref[...])
    up_ref[0] = up.astype(BF)
    cp = mm(e, wc_ref[...]) + mm(gated, wo_ref[...])
    cp_ref[0] = cp.astype(BF)
    emb = emb_ref[0].astype(F32)
    res_ref[0] = emb + sig(up) * (cp * sig(cp) - emb)


def ff_kernel(me_ref, nat_ref, cot_ref, res_ref, gain_ref, *rest):
    packs, rest = rest[:4], rest[4:]
    out_ref, gr_ref, keep_ref, send_ref, gg_ref, w_up_ref, w_down_ref, au_ref, ad_ref = rest
    step = pl.program_id(0)

    @pl.when(step == 0)
    def _():
        fill(packs, 0, w_up_ref)
        fill_rows(packs, 512, w_down_ref)
        au_ref[...] = jnp.zeros_like(au_ref)
        ad_ref[...] = jnp.zeros_like(ad_ref)
        gg_ref[...] = jnp.zeros_like(gg_ref)

    resid = read(res_ref)
    inv = lax.rsqrt(jnp.mean(resid * resid, axis=-1, keepdims=True) + EPS)
    unit = resid * inv
    gain = gain_ref[...]
    ff_in = (unit * gain).astype(BF)
    hp = mm(ff_in, w_up_ref[...])
    s = sig(hp)
    hidden = (hp * s).astype(BF)
    out = resid + mm(hidden, w_down_ref[...])
    out = out.astype(BF)
    cots = []
    for k in range(out_ref.shape[0]):
        out_ref[k] = mm(to_natural(None), out[k * BLK : k * BLK + BLK]).astype(BF)
        cots.append(mm(from_natural(nat_ref[k]), cot_ref[k]))
    grad_out = jnp.concatenate(cots, axis=0)
    grad_low = grad_out.astype(BF)
    ad_ref[...] += mm_tn(hidden, grad_low)
    grad_up = (mm_nt(grad_low, w_down_ref[...]) * slope(hp, s)).astype(BF)
    au_ref[...] += mm_tn(ff_in, grad_up)
    grad_norm = mm_nt(grad_up, w_up_ref[...])
    gain_part = jnp.sum(grad_norm * unit, axis=0, keepdims=True)
    for k in range(4):
        gg_ref[k : k + 1, :] += gain_part[:, k * 128 : (k + 1) * 128]
    scaled = grad_norm * gain
    write(
        gr_ref,
        grad_out
        + inv * (scaled - unit * jnp.mean(scaled * unit, axis=-1, keepdims=True)),
    )

    @pl.when(step == pl.num_programs(0) - 1)
    def _():
        for r, (ref, slot) in enumerate(slots(keep_ref, send_ref)):
            ref[slot, 0:512, :] = au_ref[:, r * 256 : r * 256 + 256].astype(BF)
            ref[slot, 512:768, :] = ad_ref[r * 256 : r * 256 + 256, 0:256].astype(BF)
            ref[slot, 768:1024, :] = ad_ref[r * 256 : r * 256 + 256, 256:512].astype(BF)


def gates_back_kernel(me_ref, es_ref, emb_ref, rp_ref, mix_ref, up_ref, cp_ref, gr_ref, *rest):
    packs, rest = rest[:8], rest[8:]
    (gm_ref, ge_ref, dir_ref, keep_ref, send_ref) = rest[:5]
    (wr_ref, wu_ref, wc_ref, wo_ref, ar_ref, au_ref, ac_ref, ao_ref) = rest[5:]
    me = me_ref[0]
    step = pl.program_id(0)

    @pl.when(step == 0)
    def _():
        fill(packs[0:4], 0, wr_ref)
        fill_gates(me, packs[4:8], wu_ref, wc_ref)
        fill_rows(packs[4:8], 512, wo_ref)
        for ref in (ar_ref, au_ref, ac_ref, ao_ref):
            ref[...] = jnp.zeros_like(ref)

    es = read(es_ref)
    e_t = (es * sig(es)).astype(BF).T
    emb = read(emb_ref).astype(F32)
    grad_resid = read(gr_ref)
    up = sig(read(up_ref).astype(F32))
    cp = read(cp_ref).astype(F32)
    cs = sig(cp)
    gcp = (grad_resid * up * slope(cp, cs)).astype(BF)
    gup = (grad_resid * (cp * cs - emb) * up * (1.0 - up)).astype(BF)
    write(dir_ref, (grad_resid * (1.0 - up)).astype(BF))
    ac_ref[...] += mm(e_t, gcp)
    au_ref[...] += mm(e_t, gup)
    rp = read(rp_ref)
    rs = sig(rp)
    reset = rp * rs
    mixed = read(mix_ref).astype(F32)
    ao_ref[...] += mm_tn((reset * mixed).astype(BF), gcp)
    grad_gated = mm_nt(gcp, wo_ref[...])
    write(gm_ref, (grad_gated * reset).astype(BF))
    grp = (grad_gated * mixed * slope(rp, rs)).astype(BF)
    ar_ref[...] += mm(e_t, grp)
    write(ge_ref, mm_nt(grp, wr_ref[...]) + mm_nt(gup, wu_ref[...]) + mm_nt(gcp, wc_ref[...]))

    @pl.when(step == pl.num_programs(0) - 1)
    def _():
        for r, (ref, slot) in enumerate(slots(keep_ref, send_ref)):
            units = pl.ds(r * 256, 256)
            own = pl.ds(pl.multiple_of((me ^ r) * 128, 128), 128)
            ref[slot, 0:512, :] = ar_ref[:, units].astype(BF)
            ref[slot, 512:1024, 0:128] = au_ref[:, own].astype(BF)
            ref[slot, 512:1024, 128:256] = ac_ref[:, own].astype(BF)
            ref[slot, 1024:1280, :] = ao_ref[units, 0:256].astype(BF)
            ref[slot, 1280:1536, :] = ao_ref[units, 256:512].astype(BF)


def mix_back_kernel(
    es_ref, x_ref, vp_ref, zp_ref, gm_ref, ge_ref,
    bias_ref, wz_ref, zs_ref, zo_ref, par_ref, gg_ref, *rest,
):
    packs, rest = rest[:4], rest[4:]
    (g_ref, gnv_ref, ae_ref, lb_ref, keep_ref, send_ref) = rest[:6]
    (wv_ref, av_ref, az_ref, gz_ref, gb_ref, as_ref) = rest[6:]
    step = pl.program_id(0)

    @pl.when(step == 0)
    def _():
        fill(packs, 0, wv_ref)
        for ref in (av_ref, az_ref, gz_ref, gb_ref):
            ref[...] = jnp.zeros_like(ref)

    es = es_ref[0]
    es_sig = sig(es)
    e_t = (es * es_sig).astype(BF).T
    gm = gm_ref[0]
    zp = zp_ref[0]
    zsig = sig(zp)
    za = zp * zsig
    factor = zp.shape[-1] ** -0.5
    s0, s1 = zs_ref[0:1, :], zs_ref[1:2, :]
    query = (za * s0 + zo_ref[0:1, :]).astype(BF)
    keys = (za * s1 + zo_ref[1:2, :]).astype(BF)
    weights = softmax_rows(query, keys, bias_ref[...], factor)
    vp = vp_ref[0]
    vs = sig(vp)
    values = (vp * vs).astype(BF)
    gvp = (mm_tn(weights.astype(BF), gm) * slope(vp, vs)).astype(BF)
    gnv_ref[0] = mm_nt(gvp, wv_ref[...]).astype(BF)
    av_ref[...] += mm_tn(x_ref[0].astype(BF), gvp)
    gw = mm_nt(gm, values)
    gsf = weights * (gw - jnp.sum(weights * gw, axis=-1, keepdims=True))
    gb_ref[...] += gsf
    gs = gsf.astype(BF)
    gq = mm(gs, keys) * factor
    gk = mm_tn(gs, query) * factor
    gz_ref[0:1, :] += jnp.sum(za * gq, axis=0, keepdims=True)
    gz_ref[1:2, :] += jnp.sum(za * gk, axis=0, keepdims=True)
    gz_ref[2:3, :] += jnp.sum(gq, axis=0, keepdims=True)
    gz_ref[3:4, :] += jnp.sum(gk, axis=0, keepdims=True)
    gzp = ((gq * s0 + gk * s1) * slope(zp, zsig)).astype(BF)
    az_ref[...] += mm(e_t, gzp)
    g_ref[0] = (ge_ref[0] + mm_nt(gzp, wz_ref[...])) * slope(es, es_sig)

    dims, width = lb_ref.shape[1:]
    row = lane_iota()
    for c0 in range(0, width, 128):
        sl = pl.ds(c0, 128)
        rates = [wide(par_ref[pl.ds(j, 1), sl]) for j in range(dims)]
        decay = [jnp.exp(-r) for r in rates]

        def body(t, a):
            gt = g_ref[0, at(STEP - 1 - t), sl]
            return tuple(d * v + gt for d, v in zip(decay, a))

        a = lax.fori_loop(
            0, STEP, body, tuple(jnp.zeros((LANES, 128), F32) for _ in range(dims)), unroll=32
        )
        a = chain(list(a), rates, row, shift_up)
        for j in range(dims):
            ae_ref[0, j, :, sl] = shift_up(a[j], 1, row)
            lb_ref[0, pl.ds(j, 1), sl] = a[j][0:1, :]

    @pl.when(step == pl.num_programs(0) - 1)
    def _():
        perm = to_natural(None)
        v = sum(mm(perm, p) for p in split3(gb_ref[...]))
        v = sum(mm_nt(p, perm) for p in split3(v))
        v = v[:C, :C] + v[C:, C:]
        v = jnp.concatenate([v, jnp.zeros((C, C), F32)], axis=1)
        bias = jnp.sum(pltpu.roll(skew(v, -1), C - 1, axis=1), axis=0, keepdims=True)
        zero = jnp.zeros((6, 128), F32)
        small = jnp.concatenate(
            [gz_ref[0:4, :], bias[:, :128], bias[:, 128:], gg_ref[...], zero], axis=0
        )
        high = small.astype(BF)
        low = (small - high.astype(F32)).astype(BF)
        small = jnp.concatenate([high, low], axis=1)
        as_ref[512:768, 0:128] = az_ref[0:256, :].astype(BF)
        as_ref[512:768, 128:256] = az_ref[256:512, :].astype(BF)
        for r, (ref, slot) in enumerate(slots(keep_ref, send_ref)):
            as_ref[0:512, :] = av_ref[:, r * 256 : r * 256 + 256].astype(BF)
            for k in range(8):
                ref[slot, k * 112 : k * 112 + 96, :] = as_ref[k * 96 : k * 96 + 96, :]
                ref[slot, k * 112 + 96 : k * 112 + 112, :] = small


def adjoint_kernel(x_ref, g_ref, ae_ref, ex_ref, se_ref, par_ref, gn_ref, mn_ref):
    dims, width = se_ref.shape[1:]
    place = lane_iota().astype(F32)
    half = 8
    for c0 in range(0, width, 128):
        sl = pl.ds(c0, 128)
        omega = wide(par_ref[pl.ds(5 * dims, 1), sl])
        for j0 in range(0, dims, half):
            js = range(j0, j0 + half)
            rates = [wide(par_ref[pl.ds(j, 1), sl]) for j in js]
            decay = [jnp.exp(-r) for r in rates]
            ws = [wide(par_ref[pl.ds(dims + j, 1), sl]) for j in js]

            def emit(t, a, gt):
                parts = [w * v for w, v in zip(ws, a)]
                while len(parts) > 1:
                    parts = [p + q for p, q in zip(parts[::2], parts[1::2])]
                if j0 == 0:
                    gn_ref[0, at(t), sl] = parts[0] + omega * gt
                else:
                    gn_ref[0, at(t), sl] += parts[0]

            gt = g_ref[0, at(STEP - 1), sl]
            xt = x_ref[0, at(STEP - 1), sl]
            a = tuple(gt + d * ae_ref[0, j, :, sl] for j, d in zip(js, decay))
            emit(STEP - 1, a, gt)
            m = tuple(xt * v for v in a)
            zero = tuple(jnp.zeros((LANES, 128), F32) for _ in js)

            def body(i, carry):
                a, b, m, n = carry
                t = STEP - 2 - i
                gt = g_ref[0, at(t), sl]
                xt = x_ref[0, at(t), sl]
                b = tuple(u + d * v for d, u, v in zip(decay, a, b))
                a = tuple(gt + d * v for d, v in zip(decay, a))
                emit(t, a, gt)
                m = tuple(u + xt * v for u, v in zip(m, a))
                n = tuple(u + xt * v for u, v in zip(n, b))
                return a, b, m, n

            carry = (a, zero, m, zero)
            for i in range(3):
                carry = body(i, carry)
            a, b, m, n = lax.fori_loop(3, STEP - 1, body, carry, unroll=7)
            for k, j in enumerate(js):
                start = ex_ref[0, j, :, sl] + jnp.exp(rates[k] * place * (-float(STEP))) * wide(
                    se_ref[0, pl.ds(j, 1), sl]
                )
                mn_ref[0, pl.ds(j, 1), sl] = jnp.sum(m[k], axis=0, keepdims=True)
                mn_ref[0, pl.ds(dims + j, 1), sl] = jnp.sum(
                    n[k] + start * (a[k] + decay[k] * b[k]), axis=0, keepdims=True
                )


def leave_kernel(n_parts, me_ref, ids_ref, emb_ref, x_ref, g_ref, ar_ref, ex_ref, se_ref, el_ref, ed_ref,
                 dir_ref, gnv_ref, *rest):
    locals_, rest = rest[: 2 * n_parts], rest[2 * n_parts :]
    par_ref, gain_ref, ig_ref, keep_ref, send_ref = rest[:5]
    gn_ref, ge_ref, go_ref, gg_ref, sum_ref = rest[5:]
    step = pl.program_id(0)
    dims, width = se_ref.shape[1:]

    @pl.when(step == 0)
    def _():
        for ref in (ge_ref, go_ref, gg_ref, sum_ref):
            ref[...] = jnp.zeros_like(ref)

    for k in range(n_parts):

        @pl.when(step == k)
        def _(k=k):
            gn_ref[...] = locals_[2 * k][0]
            sum_ref[0 : 2 * dims, :] += locals_[2 * k + 1][0]

    place = lane_iota().astype(F32)
    for c0 in range(0, width, 128):
        sl = pl.ds(c0, 128)
        rates = [wide(par_ref[pl.ds(j, 1), sl]) for j in range(dims)]
        decay = [jnp.exp(-r) for r in rates]
        ws = [wide(par_ref[pl.ds(dims + j, 1), sl]) for j in range(dims)]
        far = [
            jnp.exp(r * (LANES - 1.0 - place) * (-float(STEP))) * wide(ar_ref[0, pl.ds(j, 1), sl])
            for j, r in enumerate(rates)
        ]
        for j in range(dims):
            start = ex_ref[0, j, :, sl] + jnp.exp(rates[j] * place * (-float(STEP))) * wide(
                se_ref[0, pl.ds(j, 1), sl]
            )
            whole = jnp.exp(rates[j] * (-float(STEP)))
            more_m = far[j] * decay[j] * el_ref[0, j, :, sl]
            more_n = far[j] * (decay[j] * ed_ref[0, j, :, sl] + float(STEP) * whole * start)
            sum_ref[pl.ds(j, 1), sl] += jnp.sum(more_m, axis=0, keepdims=True)
            sum_ref[pl.ds(dims + j, 1), sl] += jnp.sum(more_n, axis=0, keepdims=True)

        def body(i, c):
            t = STEP - 1 - i
            c = tuple(d * v for d, v in zip(decay, c))
            parts = [w * v for w, v in zip(ws, c)]
            while len(parts) > 1:
                parts = [p + q for p, q in zip(parts[::2], parts[1::2])]
            gn_ref[at(t), sl] += parts[0]
            return c

        lax.fori_loop(0, STEP, body, tuple(far), unroll=8)

    go_ref[...] += jnp.sum(g_ref[0] * x_ref[0], axis=0, keepdims=True)
    emb = emb_ref[0].astype(F32)
    inv = lax.rsqrt(jnp.mean(emb * emb, axis=-1, keepdims=True) + EPS)
    unit = emb * inv
    gn = gn_ref[...] + gnv_ref[0].astype(F32)
    gg_ref[...] += jnp.sum(gn * unit, axis=0, keepdims=True)
    scaled = gn * gain_ref[...]
    ig = dir_ref[0].astype(F32) + inv * (
        scaled - unit * jnp.mean(scaled * unit, axis=-1, keepdims=True)
    )
    ig = ig.astype(BF)
    ids = ids_ref[0]
    ig_ref[0] = mm(to_natural(ids), ig).astype(BF)
    ge_ref[...] += mm(one_hot_t(ids, ge_ref.shape[0]), ig)

    @pl.when(step == pl.num_programs(0) - 1)
    def _():
        m, n = sum_ref[0:dims, :], sum_ref[dims : 2 * dims, :]
        rb, er, eb = (par_ref[k * dims : (k + 1) * dims, :] for k in (2, 3, 4))
        rise = one_less_exp(par_ref[0:dims, :])
        sum_ref[0:dims, :] = eb * (rise * n - m)
        sum_ref[dims : 2 * dims, :] = er * m
        sum_ref[2 * dims : 3 * dims, :] = rb * m
        pad = jnp.zeros((8, 128), F32)
        gains = [gg_ref[:, k * 128 : (k + 1) * 128] for k in range(4)]
        for r, (ref, slot) in enumerate(slots(keep_ref, send_ref)):
            own = pl.ds(pl.multiple_of((me_ref[0] ^ r) * 128, 128), 128)
            part = pl.ds(pl.multiple_of((me_ref[0] ^ r) * 64, 64), 64)
            ref[slot, 0:64, :] = ge_ref[part, 0:256].astype(BF)
            ref[slot, 64:128, :] = ge_ref[part, 256:512].astype(BF)
            ref[slot, 128:144, 0:128] = sum_ref[0:dims, own].astype(BF)
            ref[slot, 128:144, 128:256] = sum_ref[dims : 2 * dims, own].astype(BF)
            ref[slot, 144:160, 0:128] = sum_ref[2 * dims : 3 * dims, own].astype(BF)
            ref[slot, 144:160, 128:256] = jnp.concatenate(
                [jnp.broadcast_to(go_ref[:, own], (4, 128)), *gains, pad], axis=0
            ).astype(BF)


def repair(v):
    out = []
    for k in range(0, v.shape[0], 112):
        both = v[k + 96 : k + 112, 0:128] + v[k + 96 : k + 112, 128:256]
        high = both.astype(BF)
        low = (both - high.astype(F32)).astype(BF)
        out += [v[k : k + 96].astype(BF), jnp.concatenate([high, low], axis=1)]
    return jnp.concatenate(out, axis=0)


def plain(v):
    return v.astype(BF)


def add_kernel(n, fix, *refs):
    acc = refs[0][...].astype(F32)
    for ref in refs[1:n]:
        acc = acc + ref[...].astype(F32)
    refs[n][...] = fix(acc[0])
    refs[n + 1][...] = fix(acc[1])


def cut_kernel(bit, fix, at_ref, near_ref, far_ref, keep_ref, send_ref, sum_ref):
    rows = keep_ref.shape[0]
    sum_ref[...] = near_ref[...].astype(F32) + far_ref[...].astype(F32)
    upper = (at_ref[0] // bit) % 2
    keep_ref[...] = fix(sum_ref[pl.ds(pl.multiple_of(upper * rows, rows), rows), :])
    send_ref[...] = fix(sum_ref[pl.ds(pl.multiple_of((1 - upper) * rows, rows), rows), :])


def sum_kernel(fix, *refs):
    refs[-1][...] = fix(total([ref[...] for ref in refs[:-1]]))


def join_kernel(put, at_ref, near_ref, far_ref, *refs):
    rows = near_ref.shape[0]
    upper = at_ref[0] % 2
    refs[-1][pl.ds(pl.multiple_of(upper * rows, rows), rows), :] = near_ref[...].astype(F32)
    refs[-1][pl.ds(pl.multiple_of((1 - upper) * rows, rows), rows), :] = far_ref[...].astype(F32)
    put(refs[-1], *refs[:-1])


def widen_kernel(me_ref, *refs):
    for r, ref in enumerate(refs[:4]):

        @pl.when(pl.program_id(0) == r)
        def _(ref=ref):
            refs[-1][...] = ref[...].astype(F32)


def pairs(axis, bit):
    return [(i, i ^ bit) for i in range(lax.axis_size(axis))]


def swap(v, axis, bit):
    return lax.ppermute(v, axis, pairs(axis, bit))


def hop_kernel(bit, span, backward, at_ref, total_ref, recv_ref, out_ref, rate_ref, next_ref, new_ref):
    place = at_ref[0]
    upper = (place // bit) % 2 == 1
    inside = place % bit
    gap = bit - 1 - inside if backward else inside
    first = jnp.logical_not(upper) if backward else upper
    rate = rate_ref[0 : total_ref.shape[1], :]
    decay = jnp.exp(rate * (-float(bit * span)))
    near = jnp.exp(-rate * (gap * span).astype(F32))
    for k in range(total_ref.shape[0]):
        total, recv = total_ref[k], recv_ref[k]
        new_ref[k] = out_ref[k] + jnp.where(first, recv * near, 0.0)
        next_ref[k] = jnp.where(first, total + decay * recv, recv + decay * total)


def exclusive(total, par, place, span, backward, between, late):
    count = lax.axis_size("seq")
    out = jnp.zeros_like(total)
    bit = 1
    step = 0
    while bit < count:
        recv = swap(total, "seq", bit)
        if step < len(between):
            between[step]()
        last = bit * 2 >= count
        total, out, *carried = small_call(
            functools.partial(hop_kernel, bit, span, backward), "hop", [place],
            [total, recv, out, par], [(total.shape, F32)] * 2, through=late if last else (),
        )
        if last:
            late[:] = carried
        bit *= 2
        step += 1
    for rest in between[step:]:
        rest()
    return out


def block_states(local, par, place, span, backward, between, late=()):
    late = [] if isinstance(late, tuple) else late
    per = span // BLK
    if per == 1:
        return exclusive(local, par, place, span, backward, between, late)
    rate = par[: local.shape[1]]
    local = local.reshape((-1, per) + local.shape[1:])
    decay = jnp.exp(rate * (-float(BLK)))
    order = range(per)[::-1] if backward else range(per)
    total = 0.0
    for k in order:
        total = total * decay + local[:, k]
    state = exclusive(total, par, place, span, backward, between, late)
    states = [None] * per
    for k in order:
        states[k] = state
        state = state * decay + local[:, k]
    return jnp.stack(states, axis=1).reshape((-1,) + rate.shape)


def total(parts):
    acc = parts[0].astype(F32)
    for p in parts[1:]:
        acc = acc + p.astype(F32)
    return acc


def small_call(kernel, name, scalars, args, outs, scratch=(), through=()):
    after = list(through) + before()
    vmem = pl.BlockSpec(memory_space=pltpu.VMEM)
    smem = pl.BlockSpec(memory_space=pltpu.SMEM)
    n = len(scalars) + len(args)

    def body(*refs):
        kernel(*refs[:n], *refs[n + len(after) : n + len(after) + len(outs)], *refs[n + len(after) + len(outs) + len(through) :])

    made = pl.pallas_call(
        body,
        in_specs=[smem] * len(scalars)
        + [vmem] * len(args)
        + [pl.BlockSpec(memory_space=pl.ANY)] * len(after),
        out_specs=[vmem] * len(outs) + [pl.BlockSpec(memory_space=pl.ANY)] * len(through),
        out_shape=[jax.ShapeDtypeStruct(s, t) for s, t in outs]
        + [jax.ShapeDtypeStruct(v.shape, v.dtype) for v in through],
        input_output_aliases={n + k: len(outs) + k for k in range(len(through))},
        scratch_shapes=[pltpu.VMEM(s, t) for s, t in scratch],
        compiler_params=pltpu.CompilerParams(vmem_limit_bytes=VMEM),
        cost_estimate=cost(2),
        name=name,
    )(*scalars, *args, *after)
    return done(made)


def go(*jobs, through=None):
    jobs = [job for job in jobs if job is not None]
    if not jobs:
        return through
    groups = [sum((list(job[k]) for job in jobs), []) for k in range(1, 5)]

    def kernel(*refs):
        starts = [sum(len(g) for g in groups[:k]) for k in range(4)]
        for job in jobs:
            mine = []
            for k in range(4):
                mine += refs[starts[k] : starts[k] + len(job[k + 1])]
                starts[k] += len(job[k + 1])
            job[0](*mine)

    made = small_call(kernel, "stage", *groups, [] if through is None else [through])
    for job in jobs:
        job[5](*made[: len(job[3])])
        made = made[len(job[3]) :]
    return made[0] if made else None


class Reduction:
    def __init__(self, at, keeps, sends, fix=plain):
        self.at, self.fix = at, fix
        self.args = list(keeps) + [swap(s, "ch", 1) for s in sends]
        self.wide = lax.axis_size("seq") != 8

    def store(self, axis, bit):
        def then(near, far=None):
            self.near = near
            self.far = swap(near if far is None else far, axis, bit)

        return then

    def shards(self):
        shape = self.args[0].shape[1:]
        kernel = functools.partial(add_kernel, len(self.args), self.fix)
        return (kernel, [], self.args, [(shape, BF)] * 2, [], self.store("ch", 2))

    def halve(self):
        if self.wide:
            return None
        rows = self.near.shape[0]
        return (
            functools.partial(cut_kernel, 1, self.fix), [self.at], [self.near, self.far],
            [((rows // 2, 256), BF)] * 2, [((rows, 256), F32)], self.store("seq", 1),
        )

    def hop(self, bit):
        if self.wide:
            return None
        kernel = functools.partial(sum_kernel, self.fix)
        return (
            kernel, [], [self.near, self.far], [(self.near.shape, BF)], [], self.store("seq", bit)
        )

    def both(self):
        shape = self.args[0].shape

        def then(near):
            self.near = near
            if self.wide:
                self.near = lax.psum(near.astype(F32), "seq").astype(BF)
                self.far = jnp.zeros_like(near)
            else:
                self.far = swap(near, "seq", 1)

        return (functools.partial(sum_kernel, self.fix), [], self.args, [(shape, BF)], [], then)

    def split(self):
        shape = self.near.shape[1:]
        kernel = functools.partial(add_kernel, 2, self.fix)
        return (
            kernel, [], [self.near, self.far], [(shape, BF)] * 2, [], self.store("ch", 2)
        )

    def join(self, put, outs, halved=True):
        def then(*made):
            self.made = made

        args, shape = [self.near, self.far], self.near.shape
        if self.wide and halved:
            whole = lax.psum(total(args), "seq")
            return (put, [], [whole], outs, [], then)
        if halved:
            shape = (2 * shape[0], 256)
            return (functools.partial(join_kernel, put), [self.at], args, outs, [(shape, F32)], then)

        def finish(near_ref, far_ref, *refs):
            refs[-1][...] = near_ref[...].astype(F32) + far_ref[...].astype(F32)
            put(refs[-1], *refs[:-1])

        return (finish, [], args, outs, [(shape, F32)], then)


def put_ff(whole, up_ref, down_ref):
    up_ref[...] = whole[0:512, :].astype(F32)
    down_ref[:, 0:256] = whole[512:768, :].astype(F32)
    down_ref[:, 256:512] = whole[768:1024, :].astype(F32)


def put_gates(whole, reset_ref, update_ref, cand_ref, out_ref):
    reset_ref[...] = whole[0:512, :]
    update_ref[...] = whole[512:1024, 0:128]
    cand_ref[...] = whole[512:1024, 128:256]
    out_ref[:, 0:256] = whole[1024:1280, :]
    out_ref[:, 256:512] = whole[1280:1536, :]


def put_mix(whole, value_ref, z_ref, scale_ref, offset_ref, bias_ref, gain_ref):
    for k in range(8):
        part = whole[k * 112 : k * 112 + 96, :]
        if k < 5:
            value_ref[k * 96 : k * 96 + 96, :] = part
        elif k == 5:
            value_ref[480:512, :] = part[0:32]
            z_ref[0:64, :] = part[32:96, 0:128]
            z_ref[256:320, :] = part[32:96, 128:256]
        else:
            first = (k - 6) * 96 + 64
            z_ref[first : first + 96, :] = part[:, 0:128]
            z_ref[256 + first : 256 + first + 96, :] = part[:, 128:256]
    small = whole[96:112, 0:128] + whole[96:112, 128:256]
    scale_ref[...] = small[0:2]
    offset_ref[...] = small[2:4]
    bias_ref[...] = jnp.concatenate([small[4:5], small[5:6]], axis=1)[:, :255]
    for k in range(4):
        gain_ref[:, k * 128 : k * 128 + 128] = small[6 + k : 7 + k]


def put_late(whole, emb_ref, rate_ref, beta_ref, eta_ref, omega_ref, gain_ref):
    emb_ref[:, 0:256] = whole[0:64, :].astype(BF)
    emb_ref[:, 256:512] = whole[64:128, :].astype(BF)
    rate_ref[...] = whole[128:144, 0:128]
    beta_ref[...] = whole[128:144, 128:256]
    eta_ref[...] = whole[144:160, 0:128]
    omega_ref[...] = whole[144:145, 128:256]
    for k in range(4):
        gain_ref[:, k * 128 : k * 128 + 128] = whole[148 + k : 149 + k, 128:256]


def reach(v):
    return [v, swap(v, "ch", 1), swap(v, "ch", 2)]


def relay(parts, far):
    parts[2] = far
    parts.append(swap(far, "ch", 1))


def widen(parts, me, base, first, blocks):
    n, _, width = parts[0].shape
    step = n if blocks % n == 0 and first % n == 0 else 1
    inner = n // step

    def held(k):
        return lambda r, b, me_ref: (jnp.where(r == k, b, jnp.where(r > k, inner - 1, 0)), 0, 0)

    extra = before()
    if base is not None:
        extra = [base] + [v for v in extra if v is not base]
    return done(
        pl.pallas_call(
            widen_kernel,
            grid_spec=pltpu.PrefetchScalarGridSpec(
                num_scalar_prefetch=1,
                grid=(4, inner),
                in_specs=[pl.BlockSpec((step, BLK, width), held(k)) for k in range(4)]
                + [pl.BlockSpec(memory_space=pl.ANY)] * len(extra),
                out_specs=pl.BlockSpec(
                    (step, BLK, width),
                    lambda r, b, me_ref: (((me_ref[0] ^ r) * blocks + first) // step + b, 0, 0),
                ),
            ),
            out_shape=jax.ShapeDtypeStruct((4 * blocks, BLK, width), F32),
            input_output_aliases={} if base is None else {5: 0},
            compiler_params=pltpu.CompilerParams(
                dimension_semantics=("arbitrary", "arbitrary"), vmem_limit_bytes=VMEM
            ),
            cost_estimate=cost(4),
            name="widen",
        )(me, *parts, *extra)
    )


def row_block(shape, first=0, per=1):
    zeros = (0,) * (len(shape) - 1)
    return pl.BlockSpec((per,) + tuple(shape[1:]), lambda i, *_: (i + first // per,) + zeros)


def whole_block(shape):
    zeros = (0,) * len(shape)
    return pl.BlockSpec(tuple(shape), lambda i, *_: zeros)


def call(kernel, name, span, us, scalars, rows, fixed, row_outs, fixed_outs, scratch, specs=None, per=1, into=None):
    first, count = span
    after = before()
    if specs is None:
        specs = [row_block(v.shape, first if v.shape[0] > count else 0, per) for v in rows]
    shapes = [((count,) + s[1:], t) for s, t in row_outs]
    out_specs = [row_block(s, 0, per) for s, _ in shapes] + [whole_block(s) for s, _ in fixed_outs]
    aliases = {}
    if into is not None:
        shapes[0] = row_outs[0]
        out_specs[0] = row_block(row_outs[0][0], first, per)
        if into:
            after = [into[0]] + [v for v in after if v is not into[0]]
            aliases = {len(scalars) + len(rows) + len(fixed): 0}
    specs = specs + [v[1] if isinstance(v, tuple) else whole_block(v.shape) for v in fixed]
    specs = specs + [pl.BlockSpec(memory_space=pl.ANY)] * len(after)
    fixed = [v[0] if isinstance(v, tuple) else v for v in fixed]
    n = len(scalars) + len(rows) + len(fixed)

    def body(*refs):
        kernel(*refs[:n], *refs[n + len(after) :])

    made = pl.pallas_call(
        body,
        grid_spec=pltpu.PrefetchScalarGridSpec(
            num_scalar_prefetch=len(scalars),
            grid=(count // per,),
            in_specs=specs,
            out_specs=out_specs,
            scratch_shapes=[pltpu.VMEM(s, t) for s, t in scratch],
        ),
        out_shape=[jax.ShapeDtypeStruct(s, t) for s, t in shapes + fixed_outs],
        input_output_aliases=aliases,
        compiler_params=pltpu.CompilerParams(
            dimension_semantics=("arbitrary",), vmem_limit_bytes=VMEM
        ),
        cost_estimate=cost(us),
        name=name,
    )(*scalars, *rows, *fixed, *after)
    return done(made)


def local(
    token_ids, counts, embedding, gain_one, ema_rate, ema_beta, ema_eta, ema_omega, w_value, w_reset,
    w_z, z_scale, z_offset, position_bias, w_update, w_cand, w_out, gain_two, w_up, w_down, cotangent,
):
    batch, span = token_ids.shape
    vocab, width = embedding.shape
    group = lax.axis_size("ch")
    mine = lax.axis_index("ch")
    channels, dims = ema_rate.shape
    z_width = w_z.shape[1]
    units = w_value.shape[1] * group
    seqs = batch // group
    blocks = seqs * span // BLK
    rows = blocks * BLK
    me = mine.astype(jnp.int32).reshape(1)

    ORDER.clear()
    LANDED.clear()
    (par,) = small_call(
        prep_kernel, "prep", [], [ema_rate.T, ema_beta.T, ema_eta.T, ema_omega[None]],
        [((5 * dims + 8, channels), F32)],
    )
    pars = [par] + [swap(par, "ch", r) for r in (1, 2, 3)]
    (pack,) = small_call(
        pack_kernel, "pack", [], [w_value, w_reset, w_update, w_cand, w_out, w_up, w_down],
        [((3072, 256), BF)],
    )
    pack = reach(pack)

    def rows_of(size, k):
        return [(v, pl.BlockSpec((size, 256), lambda i, *_: (k, 0))) for v in pack]

    g_one, g_two = gain_one[None], gain_two[None]

    ids = lax.dynamic_slice_in_dim(token_ids, mine * seqs, seqs, 0)
    own_counts = lax.dynamic_slice_in_dim(counts, mine * seqs, seqs, 0)
    places = lax.axis_index("seq") * span + jnp.arange(span, dtype=jnp.int32)
    ids = jnp.where(places[None, :] < own_counts[:, None], ids, -1)
    ids_nat = ids.reshape(blocks, 1, BLK)
    ids_tm = ids.reshape(blocks, LANES, STEP).transpose(0, 2, 1).reshape(blocks, 1, BLK)

    row = (blocks, BLK, width)
    row_v = (blocks, BLK, units)
    states = (blocks, dims, LANES, width)
    edge = (blocks, dims, width)
    every = (0, blocks)
    x, emb = call(
        embed_kernel, "embed", every, 4, [], [ids_tm], [embedding, g_one], [(row, F32), (row, BF)], [], []
    )
    ex, lv, par = call(
        enter_kernel, "enter", every, 6, [me], [x], pars, [(states, F32), (edge, F32)],
        [((5 * dims + 8, width), F32)], [],
    )
    made = {}

    def slopes():
        made["slope"] = call(
            slope_kernel, "slope", every, 8, [], [x], [par], [(states, F32), (states, F32)], [], []
        )

    def table():
        bias = jnp.concatenate([position_bias, jnp.zeros((1,), F32)])[None]
        (made["bias"],) = small_call(table_kernel, "table", [], [bias], [((BLK, BLK), F32)])

    at_seq = lax.axis_index("seq").astype(jnp.int32).reshape(1)
    steps = [
        lambda: None,
        slopes,
        table,
    ]
    far = [pack[2]]
    se = block_states(lv, par, at_seq, span, False, steps, far)
    relay(pack, far[0])
    el, ed = made["slope"]
    bias = made["bias"]
    (es,) = call(run_kernel, "run", every, 7, [], [x, ex, se], [par], [(row, F32)], [], [])
    vp, rp, mix, zp, up, cp, res = call(
        forward_kernel, "forward", every, 12, [me], [es, x, emb],
        [bias, w_z, z_scale, z_offset, *rows_of(1024, 0), *rows_of(1024, 1)],
        [(row_v, F32), (row_v, F32), (row_v, BF), ((blocks, BLK, z_width), F32), (row, BF), (row, BF),
         (row, F32)],
        [],
        [((width, units), BF), ((width, units), BF), ((width, width), BF), ((width, width), BF),
         ((units, width), BF)],
    )
    cot = cotangent.reshape(batch * span // BLK, BLK, width)

    def pack_outs(rows):
        return [((2, rows, 256), BF), ((2, rows, 256), BF)]

    out, gr, keep3, send3, gg2 = call(
        ff_kernel, "ff", every, 14, [me], [ids_nat, cot, res], [g_two, *rows_of(1024, 2)],
        [(row, BF), (row, F32)],
        pack_outs(1024) + [((4, 128), F32)],
        [((width, units), BF), ((units, width), BF), ((width, units), F32), ((units, width), F32)],
        specs=[
            row_block(ids_nat.shape, 0, PER),
            pl.BlockSpec(
                (PER, BLK, width), lambda i, me_ref: (me_ref[0] * (blocks // PER) + i, 0, 0)
            ),
            row_block(res.shape, 0, PER),
        ],
        per=PER,
    )
    sum3 = Reduction(at_seq, [keep3], [send3])
    out = reach(out)

    gm, ge, direct, keep2, send2 = call(
        gates_back_kernel, "gates_back", every, 17, [me], [es, emb, rp, mix, up, cp, gr],
        [*rows_of(512, 1), *rows_of(1024, 1)],
        [(row_v, BF), (row, F32), (row, BF)],
        pack_outs(1536),
        [((width, units), BF), ((width, width), BF), ((width, width), BF), ((units, width), BF),
         ((width, units), F32), ((width, width), F32), ((width, width), F32), ((units, width), F32)],
    )
    sum2 = Reduction(at_seq, [keep2], [send2])
    land(out[1])
    go(sum3.shards())
    g, gnv, ae, lb, keep1, send1 = call(
        mix_back_kernel, "mix_back", every, 24, [], [es, x, vp, zp, gm, ge],
        [bias, w_z, z_scale, z_offset, par, gg2, *rows_of(512, 0)],
        [(row, F32), (row, BF), (states, F32), (edge, F32)],
        pack_outs(896),
        [((width, units), BF), ((width, units), F32), ((width, z_width), F32),
         ((8, z_width), F32), ((BLK, BLK), F32), ((768, 256), BF)],
    )
    sum1 = Reduction(at_seq, [keep1], [send1], repair)
    locals_ = []

    def adjoint():
        if len(locals_) < blocks:
            locals_.append(
                call(
                    adjoint_kernel, "adjoint", (len(locals_), 1), 6, [], [x, g, ae, ex, se], [par],
                    [(row, F32), ((blocks, 2 * dims, width), F32)], [], [],
                )
            )

    def between0():
        relay(out, go(sum3.halve(), sum2.shards(), through=out[2]))
        adjoint()

    def between1():
        land(out[3])
        go(sum3.hop(2))
        adjoint()

    def between2():
        go(sum1.shards(), sum3.hop(4))
        adjoint()
        go(sum2.halve())

    ar = block_states(lb, par, at_seq, span, True, [between0, between1, between2])
    while len(locals_) < blocks:
        adjoint()
    go(sum2.hop(4), sum1.halve(), sum3.hop(1))
    parts = [(0, blocks // 2), (blocks // 2, blocks // 2)]
    keep, send, ig = [], [], []
    for part in parts:
        rows_in = [ids_tm, emb, x, g, ar, ex, se, el, ed, direct, gnv]
        mine_in = [v for k in range(part[0], part[0] + part[1]) for v in locals_[k]]
        whole, kept, sent = call(
            functools.partial(leave_kernel, part[1]), "leave", part, 8, [me],
            rows_in, [*mine_in, par, g_one],
            [(row, BF)],
            pack_outs(160),
            [((BLK, width), F32), ((vocab, width), F32), ((1, width), F32), ((1, width), F32),
             ((3 * dims, width), F32)],
            into=ig,
        )
        keep.append(kept)
        send.append(sent)
        ig = [whole]
        if len(keep) == 1:
            go(sum1.hop(2))
    ig = reach(ig[0])
    last = Reduction(at_seq, keep, send)
    relay(ig, ig[2])
    go(sum1.hop(4), sum2.hop(2))
    go(last.both())
    output = widen(out, me, None, 0, blocks).reshape(batch, span, width)
    land(ig[1])
    go(last.hop(2))
    go(sum2.hop(1), sum1.hop(1))
    go(last.hop(4))
    wide_up, wide_down = ((width, 256), F32), ((256, width), F32)
    go(sum3.join(put_ff, [wide_up, wide_down]))
    grad_up, grad_down = sum3.made
    go(sum2.join(put_gates, [wide_up, ((width, 128), F32), ((width, 128), F32), wide_down]))
    grad_reset, grad_update, grad_cand, grad_out = sum2.made
    go(last.split())
    input_grad = widen(ig, me, None, 0, blocks).reshape(batch, span, width)
    small = ((dims, channels), F32)
    go(
        last.join(
            put_late,
            [((64, width), BF), small, small, small, ((1, channels), F32), ((1, width), F32)],
            False,
        )
    )
    go(
        sum1.join(
            put_mix,
            [wide_up, ((width, z_width), F32), ((2, z_width), F32), ((2, z_width), F32),
             ((1, 255), F32), ((1, width), F32)],
        )
    )
    grad_value, grad_z, grad_scale, grad_offset, grad_bias, grad_two = sum1.made
    emb_part, grad_rate, grad_beta, grad_eta, grad_omega, grad_one = last.made
    ge = lax.all_gather(emb_part, "ch", axis=0, tiled=True).astype(F32)
    return (
        output,
        input_grad,
        ge,
        grad_one[0],
        grad_rate.T,
        grad_beta.T,
        grad_eta.T,
        grad_omega[0],
        grad_value,
        grad_reset,
        grad_z,
        grad_scale,
        grad_offset,
        grad_bias[0],
        grad_update,
        grad_cand,
        grad_out,
        grad_two[0],
        grad_up,
        grad_down,
    )


def solution(mesh):
    return jax.shard_map(
        local,
        mesh=mesh,
        in_specs=(
            P(None, "seq"), P(), P(), P(), P("ch", None), P("ch", None), P("ch", None), P("ch"),
            P(None, "ch"), P(None, "ch"), P(), P(), P(), P(), P(None, "ch"), P(None, "ch"),
            P("ch", None), P(), P(None, "ch"), P("ch", None), P(None, "seq", None),
        ),
        out_specs=(
            P(None, "seq", None), P(None, "seq", None), P(), P(), P("ch", None), P("ch", None),
            P("ch", None), P("ch"), P(None, "ch"), P(None, "ch"), P(), P(), P(), P(), P(None, "ch"),
            P(None, "ch"), P("ch", None), P(), P(None, "ch"), P("ch", None),
        ),
        check_vma=False,
    )
```

```python
import functools

import jax
import jax.numpy as jnp
from jax import lax
from jax.experimental import pallas as pl
from jax.experimental.pallas import tpu as pltpu
from jax.sharding import PartitionSpec as P

C = 128
BLK = 256
LANES = 8
STEP = BLK // LANES
EPS = 1e-05
BF = jnp.bfloat16
F32 = jnp.float32
VMEM = 60 * 1024 * 1024
PER = 4


SCALE = 10**9

ORDER = []
LANDED = []


def before():
    ready = ORDER[-1:] + LANDED
    LANDED.clear()
    return ready


def land(*arrays):
    LANDED.extend(arrays)


def done(outs):
    ORDER.append(outs[0] if isinstance(outs, (list, tuple)) else outs)
    return outs


def cost(us):
    return pl.CostEstimate(flops=us * SCALE, bytes_accessed=10**5, transcendentals=0)


def sig(v):
    return 0.5 * jnp.tanh(0.5 * v) + 0.5


def mm(a, b):
    return jnp.dot(a, b, preferred_element_type=F32)


def mm_nt(a, b):
    return lax.dot_general(a, b, (((1,), (1,)), ((), ())), preferred_element_type=F32)


def mm_tn(a, b):
    return lax.dot_general(a, b, (((0,), (0,)), ((), ())), preferred_element_type=F32)


def slope(v, s):
    return s * (1.0 + v * (1.0 - s))


def wide(row):
    return jnp.broadcast_to(row, (LANES, 128))


def lane_iota():
    return lax.broadcasted_iota(jnp.int32, (LANES, 128), 0)


def shift_down(v, k, row):
    return jnp.where(row >= k, pltpu.roll(v, k, axis=0), 0.0)


def shift_up(v, k, row):
    return jnp.where(row < LANES - k, pltpu.roll(v, LANES - k, axis=0), 0.0)


def chain(values, rates, row, shift):
    for k in (1, 2, 4):
        values = [
            v + jnp.exp(r * (-float(STEP * k))) * shift(v, k, row) for v, r in zip(values, rates)
        ]
    return values


def at(t):
    return pl.ds(pl.multiple_of(t * LANES, LANES), LANES)


def one_hot_t(ids, vocab):
    hit = lax.broadcasted_iota(jnp.int32, (vocab, BLK), 0) == ids
    return jnp.where(hit, 1.0, 0.0).astype(BF)


def one_less_exp(rate):
    near = rate * (1.0 - rate * (0.5 - rate * (1.0 / 6.0 - rate * (1.0 / 24.0))))
    return jnp.where(rate < 0.02, near, 1.0 - jnp.exp(-rate))


def prep_kernel(rate_ref, beta_ref, eta_ref, omega_ref, out_ref):
    dims = rate_ref.shape[0]
    rate, beta, eta = rate_ref[...], beta_ref[...], eta_ref[...]
    decay, rise = jnp.exp(-rate), one_less_exp(rate)
    for k, v in enumerate((rate, eta * rise * beta, rise * beta, eta * rise, -decay * eta * beta)):
        out_ref[k * dims : (k + 1) * dims, :] = v
    out_ref[5 * dims :, :] = jnp.broadcast_to(omega_ref[...], (8, omega_ref.shape[1]))


def split3(v):
    parts = []
    for _ in range(3):
        parts.append(v.astype(BF))
        v = v - parts[-1].astype(F32)
    return parts


def skew(v, sign):
    row = lax.broadcasted_iota(jnp.int32, v.shape, 0)
    for b in range(7):
        k = 1 << b
        v = jnp.where((row & k) != 0, pltpu.roll(v, k if sign > 0 else 256 - k, axis=1), v)
    return v


def table_kernel(bias_ref, out_ref):
    v = jnp.broadcast_to(bias_ref[...], (C, 256))
    v = skew(pltpu.roll(v, 256 - (C - 1), axis=1), 1)[:, :C]
    off = jnp.zeros((C, C), F32)
    v = jnp.concatenate(
        [jnp.concatenate([v, off], axis=1), jnp.concatenate([off, v], axis=1)], axis=0
    )
    perm = to_natural(None)
    v = sum(mm_tn(perm, p) for p in split3(v))
    v = sum(mm(p, perm) for p in split3(v))
    r = lax.broadcasted_iota(jnp.int32, (BLK, BLK), 0)
    c = lax.broadcasted_iota(jnp.int32, (BLK, BLK), 1)
    query = (r & (LANES - 1)) * STEP + (r >> 3)
    key = (c & (LANES - 1)) * STEP + (c >> 3)
    seen = jnp.logical_and(key <= query, key >= (query & C))
    out_ref[...] = jnp.where(seen, v, -1e30)


def pack_kernel(wv_ref, wr_ref, wu_ref, wc_ref, wo_ref, up_ref, down_ref, out_ref):
    out_ref[0:512, :] = wv_ref[...]
    out_ref[512:1024, :] = wr_ref[...]
    out_ref[1024:1536, 0:128] = wu_ref[...]
    out_ref[1024:1536, 128:256] = wc_ref[...]
    out_ref[1536:1792, :] = wo_ref[:, 0:256]
    out_ref[1792:2048, :] = wo_ref[:, 256:512]
    out_ref[2048:2560, :] = up_ref[...]
    out_ref[2560:2816, :] = down_ref[:, 0:256]
    out_ref[2816:3072, :] = down_ref[:, 256:512]


def embed_kernel(ids_ref, tab_ref, gain_ref, x_ref, emb_ref):
    emb = mm_tn(one_hot_t(ids_ref[0], tab_ref.shape[0]), tab_ref[...])
    inv = lax.rsqrt(jnp.mean(emb * emb, axis=-1, keepdims=True) + EPS)
    x_ref[0] = emb * inv * gain_ref[...]
    emb_ref[0] = emb.astype(BF)


def slope_kernel(x_ref, par_ref, e_ref, f_ref):
    dims, width = e_ref.shape[1], e_ref.shape[3]
    half = 8
    for c0 in range(0, width, 128):
        sl = pl.ds(c0, 128)
        for j0 in range(0, dims, half):
            decay = [jnp.exp(-wide(par_ref[pl.ds(j, 1), sl])) for j in range(j0, j0 + half)]

            def body(t, carry):
                e, f = carry
                xt = x_ref[0, at(t), sl]
                f = tuple(d * v + u for d, v, u in zip(decay, f, e))
                e = tuple(d * v + xt for d, v in zip(decay, e))
                return e, f

            zero = x_ref[0, at(0), sl] * 0.0
            e, f = lax.fori_loop(0, STEP, body, ((zero,) * half, (zero,) * half), unroll=8)
            for k in range(half):
                e_ref[0, j0 + k, :, sl] = e[k]
                f_ref[0, j0 + k, :, sl] = f[k]


def enter_kernel(me_ref, x_ref, p0_ref, p1_ref, p2_ref, p3_ref, ex_ref, lv_ref, par_ref):
    dims, width = lv_ref.shape[1:]

    @pl.when(pl.program_id(0) == 0)
    def _():
        for r, ref in enumerate((p0_ref, p1_ref, p2_ref, p3_ref)):
            own = pl.ds(pl.multiple_of((me_ref[0] ^ r) * 128, 128), 128)
            par_ref[:, own] = ref[...]

    row = lane_iota()
    for c0 in range(0, width, 128):
        sl = pl.ds(c0, 128)
        rates = [wide(par_ref[pl.ds(j, 1), sl]) for j in range(dims)]
        decay = [jnp.exp(-r) for r in rates]

        def body(t, s):
            xt = x_ref[0, at(t), sl]
            return tuple(d * v + xt for d, v in zip(decay, s))

        s = lax.fori_loop(
            0, STEP, body, tuple(jnp.zeros((LANES, 128), F32) for _ in range(dims)), unroll=32
        )
        s = chain(list(s), rates, row, shift_down)
        for j in range(dims):
            ex_ref[0, j, :, sl] = shift_down(s[j], 1, row)
            lv_ref[0, pl.ds(j, 1), sl] = s[j][LANES - 1 :, :]


def run_kernel(x_ref, ex_ref, se_ref, par_ref, out_ref):
    dims, width = se_ref.shape[1:]
    place = lane_iota().astype(F32)
    for c0 in range(0, width, 128):
        sl = pl.ds(c0, 128)
        rates = [wide(par_ref[pl.ds(j, 1), sl]) for j in range(dims)]
        decay = [jnp.exp(-r) for r in rates]
        ws = [wide(par_ref[pl.ds(dims + j, 1), sl]) for j in range(dims)]
        omega = wide(par_ref[pl.ds(5 * dims, 1), sl])
        start = tuple(
            ex_ref[0, j, :, sl]
            + jnp.exp(rates[j] * place * (-float(STEP))) * wide(se_ref[0, pl.ds(j, 1), sl])
            for j in range(dims)
        )

        def body(t, s):
            xt = x_ref[0, at(t), sl]
            s = tuple(d * v + xt for d, v in zip(decay, s))
            parts = [w * v for w, v in zip(ws, s)]
            while len(parts) > 1:
                parts = [a + b for a, b in zip(parts[::2], parts[1::2])]
            out_ref[0, at(t), sl] = parts[0] + omega * xt
            return s

        lax.fori_loop(0, STEP, body, start, unroll=8)


def to_natural(mask_row):
    q = lax.broadcasted_iota(jnp.int32, (BLK, BLK), 0)
    r = lax.broadcasted_iota(jnp.int32, (BLK, BLK), 1)
    hit = q == (r & (LANES - 1)) * STEP + (r >> 3)
    if mask_row is not None:
        hit = jnp.logical_and(hit, mask_row >= 0)
    return jnp.where(hit, 1.0, 0.0).astype(BF)


def from_natural(mask_row):
    r = lax.broadcasted_iota(jnp.int32, (BLK, BLK), 0)
    q = lax.broadcasted_iota(jnp.int32, (BLK, BLK), 1)
    hit = q == (r & (LANES - 1)) * STEP + (r >> 3)
    if mask_row is not None:
        hit = jnp.logical_and(hit, mask_row >= 0)
    return jnp.where(hit, 1.0, 0.0).astype(BF)


def read(ref):
    return ref[...].reshape((-1, ref.shape[-1]))


def write(ref, v):
    ref[...] = v.reshape(ref.shape)


def fill(refs, rows, to_ref):
    for r, ref in enumerate(refs):
        to_ref[:, pl.ds(r * 256, 256)] = ref[rows : rows + 512, :]


def fill_rows(refs, rows, to_ref):
    for r, ref in enumerate(refs):
        to_ref[pl.ds(r * 256, 256), 0:256] = ref[rows : rows + 256, :]
        to_ref[pl.ds(r * 256, 256), 256:512] = ref[rows + 256 : rows + 512, :]


def fill_gates(me, refs, wu_ref, wc_ref):
    for r, ref in enumerate(refs):
        own = pl.ds(pl.multiple_of((me ^ r) * 128, 128), 128)
        wu_ref[:, own] = ref[0:512, 0:128]
        wc_ref[:, own] = ref[0:512, 128:256]


def slots(keep_ref, send_ref):
    return ((keep_ref, 0), (send_ref, 0), (keep_ref, 1), (send_ref, 1))


def softmax_rows(query, keys, bias, factor):
    scores = mm_nt(query, keys) * factor + bias
    shifted = jnp.exp(scores - jnp.max(scores, axis=-1, keepdims=True))
    return shifted / jnp.sum(shifted, axis=-1, keepdims=True)


def forward_kernel(me_ref, es_ref, x_ref, emb_ref, bias_ref, wz_ref, zs_ref, zo_ref, *rest):
    packs, rest = rest[:8], rest[8:]
    (vp_ref, rp_ref, mix_ref, zp_ref, up_ref, cp_ref, res_ref) = rest[:7]
    (wv_ref, wr_ref, wu_ref, wc_ref, wo_ref) = rest[7:]

    @pl.when(pl.program_id(0) == 0)
    def _():
        fill(packs[0:4], 0, wv_ref)
        fill(packs[0:4], 512, wr_ref)
        fill_gates(me_ref[0], packs[4:8], wu_ref, wc_ref)
        fill_rows(packs[4:8], 512, wo_ref)

    es = es_ref[0]
    e = (es * sig(es)).astype(BF)
    zp = mm(e, wz_ref[...])
    zp_ref[0] = zp
    za = zp * sig(zp)
    query = (za * zs_ref[0:1, :] + zo_ref[0:1, :]).astype(BF)
    keys = (za * zs_ref[1:2, :] + zo_ref[1:2, :]).astype(BF)
    weights = softmax_rows(query, keys, bias_ref[...], zp.shape[-1] ** -0.5).astype(BF)
    vp = mm(x_ref[0].astype(BF), wv_ref[...])
    vp_ref[0] = vp
    values = (vp * sig(vp)).astype(BF)
    mixed = mm(weights, values)
    mix_ref[0] = mixed.astype(BF)
    rp = mm(e, wr_ref[...])
    rp_ref[0] = rp
    gated = (rp * sig(rp) * mixed).astype(BF)
    up = mm(e, wu_ref[...])
    up_ref[0] = up.astype(BF)
    cp = mm(e, wc_ref[...]) + mm(gated, wo_ref[...])
    cp_ref[0] = cp.astype(BF)
    emb = emb_ref[0].astype(F32)
    res_ref[0] = emb + sig(up) * (cp * sig(cp) - emb)


def ff_kernel(me_ref, nat_ref, cot_ref, res_ref, gain_ref, *rest):
    packs, rest = rest[:4], rest[4:]
    out_ref, gr_ref, keep_ref, send_ref, gg_ref, w_up_ref, w_down_ref, au_ref, ad_ref = rest
    step = pl.program_id(0)

    @pl.when(step == 0)
    def _():
        fill(packs, 0, w_up_ref)
        fill_rows(packs, 512, w_down_ref)
        au_ref[...] = jnp.zeros_like(au_ref)
        ad_ref[...] = jnp.zeros_like(ad_ref)
        gg_ref[...] = jnp.zeros_like(gg_ref)

    resid = read(res_ref)
    inv = lax.rsqrt(jnp.mean(resid * resid, axis=-1, keepdims=True) + EPS)
    unit = resid * inv
    gain = gain_ref[...]
    ff_in = (unit * gain).astype(BF)
    hp = mm(ff_in, w_up_ref[...])
    s = sig(hp)
    hidden = (hp * s).astype(BF)
    out = resid + mm(hidden, w_down_ref[...])
    out = out.astype(BF)
    cots = []
    for k in range(out_ref.shape[0]):
        out_ref[k] = mm(to_natural(None), out[k * BLK : k * BLK + BLK]).astype(BF)
        cots.append(mm(from_natural(nat_ref[k]), cot_ref[k]))
    grad_out = jnp.concatenate(cots, axis=0)
    grad_low = grad_out.astype(BF)
    ad_ref[...] += mm_tn(hidden, grad_low)
    grad_up = (mm_nt(grad_low, w_down_ref[...]) * slope(hp, s)).astype(BF)
    au_ref[...] += mm_tn(ff_in, grad_up)
    grad_norm = mm_nt(grad_up, w_up_ref[...])
    gain_part = jnp.sum(grad_norm * unit, axis=0, keepdims=True)
    for k in range(4):
        gg_ref[k : k + 1, :] += gain_part[:, k * 128 : (k + 1) * 128]
    scaled = grad_norm * gain
    write(
        gr_ref,
        grad_out
        + inv * (scaled - unit * jnp.mean(scaled * unit, axis=-1, keepdims=True)),
    )

    @pl.when(step == pl.num_programs(0) - 1)
    def _():
        for r, (ref, slot) in enumerate(slots(keep_ref, send_ref)):
            ref[slot, 0:512, :] = au_ref[:, r * 256 : r * 256 + 256].astype(BF)
            ref[slot, 512:768, :] = ad_ref[r * 256 : r * 256 + 256, 0:256].astype(BF)
            ref[slot, 768:1024, :] = ad_ref[r * 256 : r * 256 + 256, 256:512].astype(BF)


def gates_back_kernel(me_ref, es_ref, emb_ref, rp_ref, mix_ref, up_ref, cp_ref, gr_ref, *rest):
    packs, rest = rest[:8], rest[8:]
    (gm_ref, ge_ref, dir_ref, keep_ref, send_ref) = rest[:5]
    (wr_ref, wu_ref, wc_ref, wo_ref, ar_ref, au_ref, ac_ref, ao_ref) = rest[5:]
    me = me_ref[0]
    step = pl.program_id(0)

    @pl.when(step == 0)
    def _():
        fill(packs[0:4], 0, wr_ref)
        fill_gates(me, packs[4:8], wu_ref, wc_ref)
        fill_rows(packs[4:8], 512, wo_ref)
        for ref in (ar_ref, au_ref, ac_ref, ao_ref):
            ref[...] = jnp.zeros_like(ref)

    es = read(es_ref)
    e_t = (es * sig(es)).astype(BF).T
    emb = read(emb_ref).astype(F32)
    grad_resid = read(gr_ref)
    up = sig(read(up_ref).astype(F32))
    cp = read(cp_ref).astype(F32)
    cs = sig(cp)
    gcp = (grad_resid * up * slope(cp, cs)).astype(BF)
    gup = (grad_resid * (cp * cs - emb) * up * (1.0 - up)).astype(BF)
    write(dir_ref, (grad_resid * (1.0 - up)).astype(BF))
    ac_ref[...] += mm(e_t, gcp)
    au_ref[...] += mm(e_t, gup)
    rp = read(rp_ref)
    rs = sig(rp)
    reset = rp * rs
    mixed = read(mix_ref).astype(F32)
    ao_ref[...] += mm_tn((reset * mixed).astype(BF), gcp)
    grad_gated = mm_nt(gcp, wo_ref[...])
    write(gm_ref, (grad_gated * reset).astype(BF))
    grp = (grad_gated * mixed * slope(rp, rs)).astype(BF)
    ar_ref[...] += mm(e_t, grp)
    write(ge_ref, mm_nt(grp, wr_ref[...]) + mm_nt(gup, wu_ref[...]) + mm_nt(gcp, wc_ref[...]))

    @pl.when(step == pl.num_programs(0) - 1)
    def _():
        for r, (ref, slot) in enumerate(slots(keep_ref, send_ref)):
            units = pl.ds(r * 256, 256)
            own = pl.ds(pl.multiple_of((me ^ r) * 128, 128), 128)
            ref[slot, 0:512, :] = ar_ref[:, units].astype(BF)
            ref[slot, 512:1024, 0:128] = au_ref[:, own].astype(BF)
            ref[slot, 512:1024, 128:256] = ac_ref[:, own].astype(BF)
            ref[slot, 1024:1280, :] = ao_ref[units, 0:256].astype(BF)
            ref[slot, 1280:1536, :] = ao_ref[units, 256:512].astype(BF)


def mix_back_kernel(
    es_ref, x_ref, vp_ref, zp_ref, gm_ref, ge_ref,
    bias_ref, wz_ref, zs_ref, zo_ref, par_ref, gg_ref, *rest,
):
    packs, rest = rest[:4], rest[4:]
    (g_ref, gnv_ref, ae_ref, lb_ref, keep_ref, send_ref) = rest[:6]
    (wv_ref, av_ref, az_ref, gz_ref, gb_ref, as_ref) = rest[6:]
    step = pl.program_id(0)

    @pl.when(step == 0)
    def _():
        fill(packs, 0, wv_ref)
        for ref in (av_ref, az_ref, gz_ref, gb_ref):
            ref[...] = jnp.zeros_like(ref)

    es = es_ref[0]
    es_sig = sig(es)
    e_t = (es * es_sig).astype(BF).T
    gm = gm_ref[0]
    zp = zp_ref[0]
    zsig = sig(zp)
    za = zp * zsig
    factor = zp.shape[-1] ** -0.5
    s0, s1 = zs_ref[0:1, :], zs_ref[1:2, :]
    query = (za * s0 + zo_ref[0:1, :]).astype(BF)
    keys = (za * s1 + zo_ref[1:2, :]).astype(BF)
    weights = softmax_rows(query, keys, bias_ref[...], factor)
    vp = vp_ref[0]
    vs = sig(vp)
    values = (vp * vs).astype(BF)
    gvp = (mm_tn(weights.astype(BF), gm) * slope(vp, vs)).astype(BF)
    gnv_ref[0] = mm_nt(gvp, wv_ref[...]).astype(BF)
    av_ref[...] += mm_tn(x_ref[0].astype(BF), gvp)
    gw = mm_nt(gm, values)
    gsf = weights * (gw - jnp.sum(weights * gw, axis=-1, keepdims=True))
    gb_ref[...] += gsf
    gs = gsf.astype(BF)
    gq = mm(gs, keys) * factor
    gk = mm_tn(gs, query) * factor
    gz_ref[0:1, :] += jnp.sum(za * gq, axis=0, keepdims=True)
    gz_ref[1:2, :] += jnp.sum(za * gk, axis=0, keepdims=True)
    gz_ref[2:3, :] += jnp.sum(gq, axis=0, keepdims=True)
    gz_ref[3:4, :] += jnp.sum(gk, axis=0, keepdims=True)
    gzp = ((gq * s0 + gk * s1) * slope(zp, zsig)).astype(BF)
    az_ref[...] += mm(e_t, gzp)
    g_ref[0] = (ge_ref[0] + mm_nt(gzp, wz_ref[...])) * slope(es, es_sig)

    dims, width = lb_ref.shape[1:]
    row = lane_iota()
    for c0 in range(0, width, 128):
        sl = pl.ds(c0, 128)
        rates = [wide(par_ref[pl.ds(j, 1), sl]) for j in range(dims)]
        decay = [jnp.exp(-r) for r in rates]

        def body(t, a):
            gt = g_ref[0, at(STEP - 1 - t), sl]
            return tuple(d * v + gt for d, v in zip(decay, a))

        a = lax.fori_loop(
            0, STEP, body, tuple(jnp.zeros((LANES, 128), F32) for _ in range(dims)), unroll=32
        )
        a = chain(list(a), rates, row, shift_up)
        for j in range(dims):
            ae_ref[0, j, :, sl] = shift_up(a[j], 1, row)
            lb_ref[0, pl.ds(j, 1), sl] = a[j][0:1, :]

    @pl.when(step == pl.num_programs(0) - 1)
    def _():
        perm = to_natural(None)
        v = sum(mm(perm, p) for p in split3(gb_ref[...]))
        v = sum(mm_nt(p, perm) for p in split3(v))
        v = v[:C, :C] + v[C:, C:]
        v = jnp.concatenate([v, jnp.zeros((C, C), F32)], axis=1)
        bias = jnp.sum(pltpu.roll(skew(v, -1), C - 1, axis=1), axis=0, keepdims=True)
        zero = jnp.zeros((6, 128), F32)
        small = jnp.concatenate(
            [gz_ref[0:4, :], bias[:, :128], bias[:, 128:], gg_ref[...], zero], axis=0
        )
        high = small.astype(BF)
        low = (small - high.astype(F32)).astype(BF)
        small = jnp.concatenate([high, low], axis=1)
        as_ref[512:768, 0:128] = az_ref[0:256, :].astype(BF)
        as_ref[512:768, 128:256] = az_ref[256:512, :].astype(BF)
        for r, (ref, slot) in enumerate(slots(keep_ref, send_ref)):
            as_ref[0:512, :] = av_ref[:, r * 256 : r * 256 + 256].astype(BF)
            for k in range(8):
                ref[slot, k * 112 : k * 112 + 96, :] = as_ref[k * 96 : k * 96 + 96, :]
                ref[slot, k * 112 + 96 : k * 112 + 112, :] = small


def adjoint_kernel(x_ref, g_ref, ae_ref, ex_ref, se_ref, par_ref, gn_ref, mn_ref):
    dims, width = se_ref.shape[1:]
    place = lane_iota().astype(F32)
    half = 8
    for c0 in range(0, width, 128):
        sl = pl.ds(c0, 128)
        omega = wide(par_ref[pl.ds(5 * dims, 1), sl])
        for j0 in range(0, dims, half):
            js = range(j0, j0 + half)
            rates = [wide(par_ref[pl.ds(j, 1), sl]) for j in js]
            decay = [jnp.exp(-r) for r in rates]
            ws = [wide(par_ref[pl.ds(dims + j, 1), sl]) for j in js]

            def emit(t, a, gt):
                parts = [w * v for w, v in zip(ws, a)]
                while len(parts) > 1:
                    parts = [p + q for p, q in zip(parts[::2], parts[1::2])]
                if j0 == 0:
                    gn_ref[0, at(t), sl] = parts[0] + omega * gt
                else:
                    gn_ref[0, at(t), sl] += parts[0]

            gt = g_ref[0, at(STEP - 1), sl]
            xt = x_ref[0, at(STEP - 1), sl]
            a = tuple(gt + d * ae_ref[0, j, :, sl] for j, d in zip(js, decay))
            emit(STEP - 1, a, gt)
            m = tuple(xt * v for v in a)
            zero = tuple(jnp.zeros((LANES, 128), F32) for _ in js)

            def body(i, carry):
                a, b, m, n = carry
                t = STEP - 2 - i
                gt = g_ref[0, at(t), sl]
                xt = x_ref[0, at(t), sl]
                b = tuple(u + d * v for d, u, v in zip(decay, a, b))
                a = tuple(gt + d * v for d, v in zip(decay, a))
                emit(t, a, gt)
                m = tuple(u + xt * v for u, v in zip(m, a))
                n = tuple(u + xt * v for u, v in zip(n, b))
                return a, b, m, n

            carry = (a, zero, m, zero)
            for i in range(3):
                carry = body(i, carry)
            a, b, m, n = lax.fori_loop(3, STEP - 1, body, carry, unroll=7)
            for k, j in enumerate(js):
                start = ex_ref[0, j, :, sl] + jnp.exp(rates[k] * place * (-float(STEP))) * wide(
                    se_ref[0, pl.ds(j, 1), sl]
                )
                mn_ref[0, pl.ds(j, 1), sl] = jnp.sum(m[k], axis=0, keepdims=True)
                mn_ref[0, pl.ds(dims + j, 1), sl] = jnp.sum(
                    n[k] + start * (a[k] + decay[k] * b[k]), axis=0, keepdims=True
                )


def leave_kernel(n_parts, me_ref, ids_ref, emb_ref, x_ref, g_ref, ar_ref, ex_ref, se_ref, el_ref, ed_ref,
                 dir_ref, gnv_ref, *rest):
    locals_, rest = rest[: 2 * n_parts], rest[2 * n_parts :]
    par_ref, gain_ref, ig_ref, keep_ref, send_ref = rest[:5]
    gn_ref, ge_ref, go_ref, gg_ref, sum_ref = rest[5:]
    step = pl.program_id(0)
    dims, width = se_ref.shape[1:]

    @pl.when(step == 0)
    def _():
        for ref in (ge_ref, go_ref, gg_ref, sum_ref):
            ref[...] = jnp.zeros_like(ref)

    for k in range(n_parts):

        @pl.when(step == k)
        def _(k=k):
            gn_ref[...] = locals_[2 * k][0]
            sum_ref[0 : 2 * dims, :] += locals_[2 * k + 1][0]

    place = lane_iota().astype(F32)
    for c0 in range(0, width, 128):
        sl = pl.ds(c0, 128)
        rates = [wide(par_ref[pl.ds(j, 1), sl]) for j in range(dims)]
        decay = [jnp.exp(-r) for r in rates]
        ws = [wide(par_ref[pl.ds(dims + j, 1), sl]) for j in range(dims)]
        far = [
            jnp.exp(r * (LANES - 1.0 - place) * (-float(STEP))) * wide(ar_ref[0, pl.ds(j, 1), sl])
            for j, r in enumerate(rates)
        ]
        for j in range(dims):
            start = ex_ref[0, j, :, sl] + jnp.exp(rates[j] * place * (-float(STEP))) * wide(
                se_ref[0, pl.ds(j, 1), sl]
            )
            whole = jnp.exp(rates[j] * (-float(STEP)))
            more_m = far[j] * decay[j] * el_ref[0, j, :, sl]
            more_n = far[j] * (decay[j] * ed_ref[0, j, :, sl] + float(STEP) * whole * start)
            sum_ref[pl.ds(j, 1), sl] += jnp.sum(more_m, axis=0, keepdims=True)
            sum_ref[pl.ds(dims + j, 1), sl] += jnp.sum(more_n, axis=0, keepdims=True)

        def body(i, c):
            t = STEP - 1 - i
            c = tuple(d * v for d, v in zip(decay, c))
            parts = [w * v for w, v in zip(ws, c)]
            while len(parts) > 1:
                parts = [p + q for p, q in zip(parts[::2], parts[1::2])]
            gn_ref[at(t), sl] += parts[0]
            return c

        lax.fori_loop(0, STEP, body, tuple(far), unroll=8)

    go_ref[...] += jnp.sum(g_ref[0] * x_ref[0], axis=0, keepdims=True)
    emb = emb_ref[0].astype(F32)
    inv = lax.rsqrt(jnp.mean(emb * emb, axis=-1, keepdims=True) + EPS)
    unit = emb * inv
    gn = gn_ref[...] + gnv_ref[0].astype(F32)
    gg_ref[...] += jnp.sum(gn * unit, axis=0, keepdims=True)
    scaled = gn * gain_ref[...]
    ig = dir_ref[0].astype(F32) + inv * (
        scaled - unit * jnp.mean(scaled * unit, axis=-1, keepdims=True)
    )
    ig = ig.astype(BF)
    ids = ids_ref[0]
    ig_ref[0] = mm(to_natural(ids), ig).astype(BF)
    ge_ref[...] += mm(one_hot_t(ids, ge_ref.shape[0]), ig)

    @pl.when(step == pl.num_programs(0) - 1)
    def _():
        m, n = sum_ref[0:dims, :], sum_ref[dims : 2 * dims, :]
        rb, er, eb = (par_ref[k * dims : (k + 1) * dims, :] for k in (2, 3, 4))
        rise = one_less_exp(par_ref[0:dims, :])
        sum_ref[0:dims, :] = eb * (rise * n - m)
        sum_ref[dims : 2 * dims, :] = er * m
        sum_ref[2 * dims : 3 * dims, :] = rb * m
        pad = jnp.zeros((8, 128), F32)
        gains = [gg_ref[:, k * 128 : (k + 1) * 128] for k in range(4)]
        for r, (ref, slot) in enumerate(slots(keep_ref, send_ref)):
            own = pl.ds(pl.multiple_of((me_ref[0] ^ r) * 128, 128), 128)
            part = pl.ds(pl.multiple_of((me_ref[0] ^ r) * 64, 64), 64)
            ref[slot, 0:64, :] = ge_ref[part, 0:256].astype(BF)
            ref[slot, 64:128, :] = ge_ref[part, 256:512].astype(BF)
            ref[slot, 128:144, 0:128] = sum_ref[0:dims, own].astype(BF)
            ref[slot, 128:144, 128:256] = sum_ref[dims : 2 * dims, own].astype(BF)
            ref[slot, 144:160, 0:128] = sum_ref[2 * dims : 3 * dims, own].astype(BF)
            ref[slot, 144:160, 128:256] = jnp.concatenate(
                [jnp.broadcast_to(go_ref[:, own], (4, 128)), *gains, pad], axis=0
            ).astype(BF)


def repair(v):
    out = []
    for k in range(0, v.shape[0], 112):
        both = v[k + 96 : k + 112, 0:128] + v[k + 96 : k + 112, 128:256]
        high = both.astype(BF)
        low = (both - high.astype(F32)).astype(BF)
        out += [v[k : k + 96].astype(BF), jnp.concatenate([high, low], axis=1)]
    return jnp.concatenate(out, axis=0)


def plain(v):
    return v.astype(BF)


def add_kernel(n, fix, *refs):
    acc = refs[0][...].astype(F32)
    for ref in refs[1:n]:
        acc = acc + ref[...].astype(F32)
    refs[n][...] = fix(acc[0])
    refs[n + 1][...] = fix(acc[1])


def cut_kernel(bit, fix, at_ref, near_ref, far_ref, keep_ref, send_ref, sum_ref):
    rows = keep_ref.shape[0]
    sum_ref[...] = near_ref[...].astype(F32) + far_ref[...].astype(F32)
    upper = (at_ref[0] // bit) % 2
    keep_ref[...] = fix(sum_ref[pl.ds(pl.multiple_of(upper * rows, rows), rows), :])
    send_ref[...] = fix(sum_ref[pl.ds(pl.multiple_of((1 - upper) * rows, rows), rows), :])


def sum_kernel(fix, *refs):
    refs[-1][...] = fix(total([ref[...] for ref in refs[:-1]]))


def join_kernel(put, at_ref, near_ref, far_ref, *refs):
    rows = near_ref.shape[0]
    upper = at_ref[0] % 2
    refs[-1][pl.ds(pl.multiple_of(upper * rows, rows), rows), :] = near_ref[...].astype(F32)
    refs[-1][pl.ds(pl.multiple_of((1 - upper) * rows, rows), rows), :] = far_ref[...].astype(F32)
    put(refs[-1], *refs[:-1])


def widen_kernel(me_ref, *refs):
    for r, ref in enumerate(refs[:4]):

        @pl.when(pl.program_id(0) == r)
        def _(ref=ref):
            refs[-1][...] = ref[...].astype(F32)


def pairs(axis, bit):
    return [(i, i ^ bit) for i in range(lax.axis_size(axis))]


def swap(v, axis, bit):
    return lax.ppermute(v, axis, pairs(axis, bit))


def hop_kernel(bit, span, backward, at_ref, total_ref, recv_ref, out_ref, rate_ref, next_ref, new_ref):
    place = at_ref[0]
    upper = (place // bit) % 2 == 1
    inside = place % bit
    gap = bit - 1 - inside if backward else inside
    first = jnp.logical_not(upper) if backward else upper
    rate = rate_ref[0 : total_ref.shape[1], :]
    decay = jnp.exp(rate * (-float(bit * span)))
    near = jnp.exp(-rate * (gap * span).astype(F32))
    for k in range(total_ref.shape[0]):
        total, recv = total_ref[k], recv_ref[k]
        new_ref[k] = out_ref[k] + jnp.where(first, recv * near, 0.0)
        next_ref[k] = jnp.where(first, total + decay * recv, recv + decay * total)


def exclusive(total, par, place, span, backward, between, late):
    count = lax.axis_size("seq")
    out = jnp.zeros_like(total)
    bit = 1
    step = 0
    while bit < count:
        recv = swap(total, "seq", bit)
        if step < len(between):
            between[step]()
        last = bit * 2 >= count
        total, out, *carried = small_call(
            functools.partial(hop_kernel, bit, span, backward), "hop", [place],
            [total, recv, out, par], [(total.shape, F32)] * 2, through=late if last else (),
        )
        if last:
            late[:] = carried
        bit *= 2
        step += 1
    for rest in between[step:]:
        rest()
    return out


def block_states(local, par, place, span, backward, between, late=()):
    late = [] if isinstance(late, tuple) else late
    per = span // BLK
    if per == 1:
        return exclusive(local, par, place, span, backward, between, late)
    rate = par[: local.shape[1]]
    local = local.reshape((-1, per) + local.shape[1:])
    decay = jnp.exp(rate * (-float(BLK)))
    order = range(per)[::-1] if backward else range(per)
    total = 0.0
    for k in order:
        total = total * decay + local[:, k]
    state = exclusive(total, par, place, span, backward, between, late)
    states = [None] * per
    for k in order:
        states[k] = state
        state = state * decay + local[:, k]
    return jnp.stack(states, axis=1).reshape((-1,) + rate.shape)


def total(parts):
    acc = parts[0].astype(F32)
    for p in parts[1:]:
        acc = acc + p.astype(F32)
    return acc


def small_call(kernel, name, scalars, args, outs, scratch=(), through=()):
    after = list(through) + before()
    vmem = pl.BlockSpec(memory_space=pltpu.VMEM)
    smem = pl.BlockSpec(memory_space=pltpu.SMEM)
    n = len(scalars) + len(args)

    def body(*refs):
        kernel(*refs[:n], *refs[n + len(after) : n + len(after) + len(outs)], *refs[n + len(after) + len(outs) + len(through) :])

    made = pl.pallas_call(
        body,
        in_specs=[smem] * len(scalars)
        + [vmem] * len(args)
        + [pl.BlockSpec(memory_space=pl.ANY)] * len(after),
        out_specs=[vmem] * len(outs) + [pl.BlockSpec(memory_space=pl.ANY)] * len(through),
        out_shape=[jax.ShapeDtypeStruct(s, t) for s, t in outs]
        + [jax.ShapeDtypeStruct(v.shape, v.dtype) for v in through],
        input_output_aliases={n + k: len(outs) + k for k in range(len(through))},
        scratch_shapes=[pltpu.VMEM(s, t) for s, t in scratch],
        compiler_params=pltpu.CompilerParams(vmem_limit_bytes=VMEM),
        cost_estimate=cost(2),
        name=name,
    )(*scalars, *args, *after)
    return done(made)


def go(*jobs, through=None):
    jobs = [job for job in jobs if job is not None]
    if not jobs:
        return through
    groups = [sum((list(job[k]) for job in jobs), []) for k in range(1, 5)]

    def kernel(*refs):
        starts = [sum(len(g) for g in groups[:k]) for k in range(4)]
        for job in jobs:
            mine = []
            for k in range(4):
                mine += refs[starts[k] : starts[k] + len(job[k + 1])]
                starts[k] += len(job[k + 1])
            job[0](*mine)

    made = small_call(kernel, "stage", *groups, [] if through is None else [through])
    for job in jobs:
        job[5](*made[: len(job[3])])
        made = made[len(job[3]) :]
    return made[0] if made else None


class Reduction:
    def __init__(self, at, keeps, sends, fix=plain):
        self.at, self.fix = at, fix
        self.args = list(keeps) + [swap(s, "ch", 1) for s in sends]
        self.wide = lax.axis_size("seq") != 8

    def store(self, axis, bit):
        def then(near, far=None):
            self.near = near
            self.far = swap(near if far is None else far, axis, bit)

        return then

    def shards(self):
        shape = self.args[0].shape[1:]
        kernel = functools.partial(add_kernel, len(self.args), self.fix)
        return (kernel, [], self.args, [(shape, BF)] * 2, [], self.store("ch", 2))

    def halve(self):
        if self.wide:
            return None
        rows = self.near.shape[0]
        return (
            functools.partial(cut_kernel, 1, self.fix), [self.at], [self.near, self.far],
            [((rows // 2, 256), BF)] * 2, [((rows, 256), F32)], self.store("seq", 1),
        )

    def hop(self, bit):
        if self.wide:
            return None
        kernel = functools.partial(sum_kernel, self.fix)
        return (
            kernel, [], [self.near, self.far], [(self.near.shape, BF)], [], self.store("seq", bit)
        )

    def both(self):
        shape = self.args[0].shape

        def then(near):
            self.near = near
            if self.wide:
                self.near = lax.psum(near.astype(F32), "seq").astype(BF)
                self.far = jnp.zeros_like(near)
            else:
                self.far = swap(near, "seq", 1)

        return (functools.partial(sum_kernel, self.fix), [], self.args, [(shape, BF)], [], then)

    def split(self):
        shape = self.near.shape[1:]
        kernel = functools.partial(add_kernel, 2, self.fix)
        return (
            kernel, [], [self.near, self.far], [(shape, BF)] * 2, [], self.store("ch", 2)
        )

    def join(self, put, outs, halved=True):
        def then(*made):
            self.made = made

        args, shape = [self.near, self.far], self.near.shape
        if self.wide and halved:
            whole = lax.psum(total(args), "seq")
            return (put, [], [whole], outs, [], then)
        if halved:
            shape = (2 * shape[0], 256)
            return (functools.partial(join_kernel, put), [self.at], args, outs, [(shape, F32)], then)

        def finish(near_ref, far_ref, *refs):
            refs[-1][...] = near_ref[...].astype(F32) + far_ref[...].astype(F32)
            put(refs[-1], *refs[:-1])

        return (finish, [], args, outs, [(shape, F32)], then)


def put_ff(whole, up_ref, down_ref):
    up_ref[...] = whole[0:512, :].astype(F32)
    down_ref[:, 0:256] = whole[512:768, :].astype(F32)
    down_ref[:, 256:512] = whole[768:1024, :].astype(F32)


def put_gates(whole, reset_ref, update_ref, cand_ref, out_ref):
    reset_ref[...] = whole[0:512, :]
    update_ref[...] = whole[512:1024, 0:128]
    cand_ref[...] = whole[512:1024, 128:256]
    out_ref[:, 0:256] = whole[1024:1280, :]
    out_ref[:, 256:512] = whole[1280:1536, :]


def put_mix(whole, value_ref, z_ref, scale_ref, offset_ref, bias_ref, gain_ref):
    for k in range(8):
        part = whole[k * 112 : k * 112 + 96, :]
        if k < 5:
            value_ref[k * 96 : k * 96 + 96, :] = part
        elif k == 5:
            value_ref[480:512, :] = part[0:32]
            z_ref[0:64, :] = part[32:96, 0:128]
            z_ref[256:320, :] = part[32:96, 128:256]
        else:
            first = (k - 6) * 96 + 64
            z_ref[first : first + 96, :] = part[:, 0:128]
            z_ref[256 + first : 256 + first + 96, :] = part[:, 128:256]
    small = whole[96:112, 0:128] + whole[96:112, 128:256]
    scale_ref[...] = small[0:2]
    offset_ref[...] = small[2:4]
    bias_ref[...] = jnp.concatenate([small[4:5], small[5:6]], axis=1)[:, :255]
    for k in range(4):
        gain_ref[:, k * 128 : k * 128 + 128] = small[6 + k : 7 + k]


def put_late(whole, emb_ref, rate_ref, beta_ref, eta_ref, omega_ref, gain_ref):
    emb_ref[:, 0:256] = whole[0:64, :].astype(BF)
    emb_ref[:, 256:512] = whole[64:128, :].astype(BF)
    rate_ref[...] = whole[128:144, 0:128]
    beta_ref[...] = whole[128:144, 128:256]
    eta_ref[...] = whole[144:160, 0:128]
    omega_ref[...] = whole[144:145, 128:256]
    for k in range(4):
        gain_ref[:, k * 128 : k * 128 + 128] = whole[148 + k : 149 + k, 128:256]


def reach(v):
    return [v, swap(v, "ch", 1), swap(v, "ch", 2)]


def relay(parts, far):
    parts[2] = far
    parts.append(swap(far, "ch", 1))


def widen(parts, me, base, first, blocks):
    n, _, width = parts[0].shape
    step = n if blocks % n == 0 and first % n == 0 else 1
    inner = n // step

    def held(k):
        return lambda r, b, me_ref: (jnp.where(r == k, b, jnp.where(r > k, inner - 1, 0)), 0, 0)

    extra = before()
    if base is not None:
        extra = [base] + [v for v in extra if v is not base]
    return done(
        pl.pallas_call(
            widen_kernel,
            grid_spec=pltpu.PrefetchScalarGridSpec(
                num_scalar_prefetch=1,
                grid=(4, inner),
                in_specs=[pl.BlockSpec((step, BLK, width), held(k)) for k in range(4)]
                + [pl.BlockSpec(memory_space=pl.ANY)] * len(extra),
                out_specs=pl.BlockSpec(
                    (step, BLK, width),
                    lambda r, b, me_ref: (((me_ref[0] ^ r) * blocks + first) // step + b, 0, 0),
                ),
            ),
            out_shape=jax.ShapeDtypeStruct((4 * blocks, BLK, width), F32),
            input_output_aliases={} if base is None else {5: 0},
            compiler_params=pltpu.CompilerParams(
                dimension_semantics=("arbitrary", "arbitrary"), vmem_limit_bytes=VMEM
            ),
            cost_estimate=cost(4),
            name="widen",
        )(me, *parts, *extra)
    )


def row_block(shape, first=0, per=1):
    zeros = (0,) * (len(shape) - 1)
    return pl.BlockSpec((per,) + tuple(shape[1:]), lambda i, *_: (i + first // per,) + zeros)


def whole_block(shape):
    zeros = (0,) * len(shape)
    return pl.BlockSpec(tuple(shape), lambda i, *_: zeros)


def call(kernel, name, span, us, scalars, rows, fixed, row_outs, fixed_outs, scratch, specs=None, per=1, into=None):
    first, count = span
    after = before()
    if specs is None:
        specs = [row_block(v.shape, first if v.shape[0] > count else 0, per) for v in rows]
    shapes = [((count,) + s[1:], t) for s, t in row_outs]
    out_specs = [row_block(s, 0, per) for s, _ in shapes] + [whole_block(s) for s, _ in fixed_outs]
    aliases = {}
    if into is not None:
        shapes[0] = row_outs[0]
        out_specs[0] = row_block(row_outs[0][0], first, per)
        if into:
            after = [into[0]] + [v for v in after if v is not into[0]]
            aliases = {len(scalars) + len(rows) + len(fixed): 0}
    specs = specs + [v[1] if isinstance(v, tuple) else whole_block(v.shape) for v in fixed]
    specs = specs + [pl.BlockSpec(memory_space=pl.ANY)] * len(after)
    fixed = [v[0] if isinstance(v, tuple) else v for v in fixed]
    n = len(scalars) + len(rows) + len(fixed)

    def body(*refs):
        kernel(*refs[:n], *refs[n + len(after) :])

    made = pl.pallas_call(
        body,
        grid_spec=pltpu.PrefetchScalarGridSpec(
            num_scalar_prefetch=len(scalars),
            grid=(count // per,),
            in_specs=specs,
            out_specs=out_specs,
            scratch_shapes=[pltpu.VMEM(s, t) for s, t in scratch],
        ),
        out_shape=[jax.ShapeDtypeStruct(s, t) for s, t in shapes + fixed_outs],
        input_output_aliases=aliases,
        compiler_params=pltpu.CompilerParams(
            dimension_semantics=("arbitrary",), vmem_limit_bytes=VMEM
        ),
        cost_estimate=cost(us),
        name=name,
    )(*scalars, *rows, *fixed, *after)
    return done(made)


def local(
    token_ids, counts, embedding, gain_one, ema_rate, ema_beta, ema_eta, ema_omega, w_value, w_reset,
    w_z, z_scale, z_offset, position_bias, w_update, w_cand, w_out, gain_two, w_up, w_down, cotangent,
):
    batch, span = token_ids.shape
    vocab, width = embedding.shape
    group = lax.axis_size("ch")
    mine = lax.axis_index("ch")
    channels, dims = ema_rate.shape
    z_width = w_z.shape[1]
    units = w_value.shape[1] * group
    seqs = batch // group
    blocks = seqs * span // BLK
    rows = blocks * BLK
    me = mine.astype(jnp.int32).reshape(1)

    ORDER.clear()
    LANDED.clear()
    (par,) = small_call(
        prep_kernel, "prep", [], [ema_rate.T, ema_beta.T, ema_eta.T, ema_omega[None]],
        [((5 * dims + 8, channels), F32)],
    )
    pars = [par] + [swap(par, "ch", r) for r in (1, 2, 3)]
    (pack,) = small_call(
        pack_kernel, "pack", [], [w_value, w_reset, w_update, w_cand, w_out, w_up, w_down],
        [((3072, 256), BF)],
    )
    pack = reach(pack)

    def rows_of(size, k):
        return [(v, pl.BlockSpec((size, 256), lambda i, *_: (k, 0))) for v in pack]

    g_one, g_two = gain_one[None], gain_two[None]

    ids = lax.dynamic_slice_in_dim(token_ids, mine * seqs, seqs, 0)
    own_counts = lax.dynamic_slice_in_dim(counts, mine * seqs, seqs, 0)
    places = lax.axis_index("seq") * span + jnp.arange(span, dtype=jnp.int32)
    ids = jnp.where(places[None, :] < own_counts[:, None], ids, -1)
    ids_nat = ids.reshape(blocks, 1, BLK)
    ids_tm = ids.reshape(blocks, LANES, STEP).transpose(0, 2, 1).reshape(blocks, 1, BLK)

    row = (blocks, BLK, width)
    row_v = (blocks, BLK, units)
    states = (blocks, dims, LANES, width)
    edge = (blocks, dims, width)
    every = (0, blocks)
    x, emb = call(
        embed_kernel, "embed", every, 4, [], [ids_tm], [embedding, g_one], [(row, F32), (row, BF)], [], []
    )
    ex, lv, par = call(
        enter_kernel, "enter", every, 6, [me], [x], pars, [(states, F32), (edge, F32)],
        [((5 * dims + 8, width), F32)], [],
    )
    made = {}

    def slopes():
        made["slope"] = call(
            slope_kernel, "slope", every, 8, [], [x], [par], [(states, F32), (states, F32)], [], []
        )

    def table():
        bias = jnp.concatenate([position_bias, jnp.zeros((1,), F32)])[None]
        (made["bias"],) = small_call(table_kernel, "table", [], [bias], [((BLK, BLK), F32)])

    at_seq = lax.axis_index("seq").astype(jnp.int32).reshape(1)
    steps = [
        lambda: None,
        slopes,
        table,
    ]
    far = [pack[2]]
    se = block_states(lv, par, at_seq, span, False, steps, far)
    relay(pack, far[0])
    el, ed = made["slope"]
    bias = made["bias"]
    (es,) = call(run_kernel, "run", every, 7, [], [x, ex, se], [par], [(row, F32)], [], [])
    vp, rp, mix, zp, up, cp, res = call(
        forward_kernel, "forward", every, 12, [me], [es, x, emb],
        [bias, w_z, z_scale, z_offset, *rows_of(1024, 0), *rows_of(1024, 1)],
        [(row_v, F32), (row_v, F32), (row_v, BF), ((blocks, BLK, z_width), F32), (row, BF), (row, BF),
         (row, F32)],
        [],
        [((width, units), BF), ((width, units), BF), ((width, width), BF), ((width, width), BF),
         ((units, width), BF)],
    )
    cot = cotangent.reshape(batch * span // BLK, BLK, width)

    def pack_outs(rows):
        return [((2, rows, 256), BF), ((2, rows, 256), BF)]

    out, gr, keep3, send3, gg2 = call(
        ff_kernel, "ff", every, 14, [me], [ids_nat, cot, res], [g_two, *rows_of(1024, 2)],
        [(row, BF), (row, F32)],
        pack_outs(1024) + [((4, 128), F32)],
        [((width, units), BF), ((units, width), BF), ((width, units), F32), ((units, width), F32)],
        specs=[
            row_block(ids_nat.shape, 0, PER),
            pl.BlockSpec(
                (PER, BLK, width), lambda i, me_ref: (me_ref[0] * (blocks // PER) + i, 0, 0)
            ),
            row_block(res.shape, 0, PER),
        ],
        per=PER,
    )
    sum3 = Reduction(at_seq, [keep3], [send3])
    out = reach(out)

    gm, ge, direct, keep2, send2 = call(
        gates_back_kernel, "gates_back", every, 17, [me], [es, emb, rp, mix, up, cp, gr],
        [*rows_of(512, 1), *rows_of(1024, 1)],
        [(row_v, BF), (row, F32), (row, BF)],
        pack_outs(1536),
        [((width, units), BF), ((width, width), BF), ((width, width), BF), ((units, width), BF),
         ((width, units), F32), ((width, width), F32), ((width, width), F32), ((units, width), F32)],
    )
    sum2 = Reduction(at_seq, [keep2], [send2])
    land(out[1])
    go(sum3.shards())
    g, gnv, ae, lb, keep1, send1 = call(
        mix_back_kernel, "mix_back", every, 24, [], [es, x, vp, zp, gm, ge],
        [bias, w_z, z_scale, z_offset, par, gg2, *rows_of(512, 0)],
        [(row, F32), (row, BF), (states, F32), (edge, F32)],
        pack_outs(896),
        [((width, units), BF), ((width, units), F32), ((width, z_width), F32),
         ((8, z_width), F32), ((BLK, BLK), F32), ((768, 256), BF)],
    )
    sum1 = Reduction(at_seq, [keep1], [send1], repair)
    locals_ = []

    def adjoint():
        if len(locals_) < blocks:
            locals_.append(
                call(
                    adjoint_kernel, "adjoint", (len(locals_), 1), 6, [], [x, g, ae, ex, se], [par],
                    [(row, F32), ((blocks, 2 * dims, width), F32)], [], [],
                )
            )

    def between0():
        relay(out, go(sum3.halve(), sum2.shards(), through=out[2]))
        adjoint()

    def between1():
        land(out[3])
        go(sum3.hop(2))
        adjoint()

    def between2():
        go(sum1.shards(), sum3.hop(4))
        adjoint()
        go(sum2.halve())

    ar = block_states(lb, par, at_seq, span, True, [between0, between1, between2])
    while len(locals_) < blocks:
        adjoint()
    go(sum2.hop(4), sum1.halve(), sum3.hop(1))
    parts = [(0, blocks // 2), (blocks // 2, blocks // 2)]
    keep, send, ig = [], [], []
    for part in parts:
        rows_in = [ids_tm, emb, x, g, ar, ex, se, el, ed, direct, gnv]
        mine_in = [v for k in range(part[0], part[0] + part[1]) for v in locals_[k]]
        whole, kept, sent = call(
            functools.partial(leave_kernel, part[1]), "leave", part, 8, [me],
            rows_in, [*mine_in, par, g_one],
            [(row, BF)],
            pack_outs(160),
            [((BLK, width), F32), ((vocab, width), F32), ((1, width), F32), ((1, width), F32),
             ((3 * dims, width), F32)],
            into=ig,
        )
        keep.append(kept)
        send.append(sent)
        ig = [whole]
        if len(keep) == 1:
            go(sum1.hop(2))
    ig = reach(ig[0])
    last = Reduction(at_seq, keep, send)
    relay(ig, ig[2])
    go(sum1.hop(4), sum2.hop(2))
    go(last.both())
    output = widen(out, me, None, 0, blocks).reshape(batch, span, width)
    go(last.hop(2))
    go(sum2.hop(1), sum1.hop(1))
    go(last.hop(4))
    wide_up, wide_down = ((width, 256), F32), ((256, width), F32)
    go(sum3.join(put_ff, [wide_up, wide_down]))
    grad_up, grad_down = sum3.made
    go(sum2.join(put_gates, [wide_up, ((width, 128), F32), ((width, 128), F32), wide_down]))
    grad_reset, grad_update, grad_cand, grad_out = sum2.made
    go(last.split())
    input_grad = widen(ig, me, None, 0, blocks).reshape(batch, span, width)
    small = ((dims, channels), F32)
    go(
        last.join(
            put_late,
            [((64, width), BF), small, small, small, ((1, channels), F32), ((1, width), F32)],
            False,
        )
    )
    go(
        sum1.join(
            put_mix,
            [wide_up, ((width, z_width), F32), ((2, z_width), F32), ((2, z_width), F32),
             ((1, 255), F32), ((1, width), F32)],
        )
    )
    grad_value, grad_z, grad_scale, grad_offset, grad_bias, grad_two = sum1.made
    emb_part, grad_rate, grad_beta, grad_eta, grad_omega, grad_one = last.made
    ge = lax.all_gather(emb_part, "ch", axis=0, tiled=True).astype(F32)
    return (
        output,
        input_grad,
        ge,
        grad_one[0],
        grad_rate.T,
        grad_beta.T,
        grad_eta.T,
        grad_omega[0],
        grad_value,
        grad_reset,
        grad_z,
        grad_scale,
        grad_offset,
        grad_bias[0],
        grad_update,
        grad_cand,
        grad_out,
        grad_two[0],
        grad_up,
        grad_down,
    )


def solution(mesh):
    return jax.shard_map(
        local,
        mesh=mesh,
        in_specs=(
            P(None, "seq"), P(), P(), P(), P("ch", None), P("ch", None), P("ch", None), P("ch"),
            P(None, "ch"), P(None, "ch"), P(), P(), P(), P(), P(None, "ch"), P(None, "ch"),
            P("ch", None), P(), P(None, "ch"), P("ch", None), P(None, "seq", None),
        ),
        out_specs=(
            P(None, "seq", None), P(None, "seq", None), P(), P(), P("ch", None), P("ch", None),
            P("ch", None), P("ch"), P(None, "ch"), P(None, "ch"), P(), P(), P(), P(), P(None, "ch"),
            P(None, "ch"), P("ch", None), P(), P(None, "ch"), P("ch", None),
        ),
        check_vma=False,
    )
```

```python
import functools

import jax
import jax.numpy as jnp
from jax import lax
from jax.experimental import pallas as pl
from jax.experimental.pallas import tpu as pltpu
from jax.sharding import PartitionSpec as P

C = 128
BLK = 256
LANES = 8
STEP = BLK // LANES
EPS = 1e-05
BF = jnp.bfloat16
F32 = jnp.float32
VMEM = 60 * 1024 * 1024
PER = 4


SCALE = 10**9

ORDER = []
LANDED = []


def before():
    ready = ORDER[-1:] + LANDED
    LANDED.clear()
    return ready


def land(*arrays):
    LANDED.extend(arrays)


def done(outs):
    ORDER.append(outs[0] if isinstance(outs, (list, tuple)) else outs)
    return outs


def cost(us):
    return pl.CostEstimate(flops=us * SCALE, bytes_accessed=10**5, transcendentals=0)


def sig(v):
    return 0.5 * jnp.tanh(0.5 * v) + 0.5


def mm(a, b):
    return jnp.dot(a, b, preferred_element_type=F32)


def mm_nt(a, b):
    return lax.dot_general(a, b, (((1,), (1,)), ((), ())), preferred_element_type=F32)


def mm_tn(a, b):
    return lax.dot_general(a, b, (((0,), (0,)), ((), ())), preferred_element_type=F32)


def slope(v, s):
    return s * (1.0 + v * (1.0 - s))


def wide(row):
    return jnp.broadcast_to(row, (LANES, 128))


def lane_iota():
    return lax.broadcasted_iota(jnp.int32, (LANES, 128), 0)


def shift_down(v, k, row):
    return jnp.where(row >= k, pltpu.roll(v, k, axis=0), 0.0)


def shift_up(v, k, row):
    return jnp.where(row < LANES - k, pltpu.roll(v, LANES - k, axis=0), 0.0)


def chain(values, rates, row, shift):
    for k in (1, 2, 4):
        values = [
            v + jnp.exp(r * (-float(STEP * k))) * shift(v, k, row) for v, r in zip(values, rates)
        ]
    return values


def at(t):
    return pl.ds(pl.multiple_of(t * LANES, LANES), LANES)


def one_hot_t(ids, vocab):
    hit = lax.broadcasted_iota(jnp.int32, (vocab, BLK), 0) == ids
    return jnp.where(hit, 1.0, 0.0).astype(BF)


def one_less_exp(rate):
    near = rate * (1.0 - rate * (0.5 - rate * (1.0 / 6.0 - rate * (1.0 / 24.0))))
    return jnp.where(rate < 0.02, near, 1.0 - jnp.exp(-rate))


def prep_kernel(rate_ref, beta_ref, eta_ref, omega_ref, out_ref):
    dims = rate_ref.shape[0]
    rate, beta, eta = rate_ref[...], beta_ref[...], eta_ref[...]
    decay, rise = jnp.exp(-rate), one_less_exp(rate)
    for k, v in enumerate((rate, eta * rise * beta, rise * beta, eta * rise, -decay * eta * beta)):
        out_ref[k * dims : (k + 1) * dims, :] = v
    out_ref[5 * dims :, :] = jnp.broadcast_to(omega_ref[...], (8, omega_ref.shape[1]))


def split3(v):
    parts = []
    for _ in range(3):
        parts.append(v.astype(BF))
        v = v - parts[-1].astype(F32)
    return parts


def skew(v, sign):
    row = lax.broadcasted_iota(jnp.int32, v.shape, 0)
    for b in range(7):
        k = 1 << b
        v = jnp.where((row & k) != 0, pltpu.roll(v, k if sign > 0 else 256 - k, axis=1), v)
    return v


def table_kernel(bias_ref, out_ref):
    v = jnp.broadcast_to(bias_ref[...], (C, 256))
    v = skew(pltpu.roll(v, 256 - (C - 1), axis=1), 1)[:, :C]
    off = jnp.zeros((C, C), F32)
    v = jnp.concatenate(
        [jnp.concatenate([v, off], axis=1), jnp.concatenate([off, v], axis=1)], axis=0
    )
    perm = to_natural(None)
    v = sum(mm_tn(perm, p) for p in split3(v))
    v = sum(mm(p, perm) for p in split3(v))
    r = lax.broadcasted_iota(jnp.int32, (BLK, BLK), 0)
    c = lax.broadcasted_iota(jnp.int32, (BLK, BLK), 1)
    query = (r & (LANES - 1)) * STEP + (r >> 3)
    key = (c & (LANES - 1)) * STEP + (c >> 3)
    seen = jnp.logical_and(key <= query, key >= (query & C))
    out_ref[...] = jnp.where(seen, v, -1e30)


def pack_kernel(wv_ref, wr_ref, wu_ref, wc_ref, wo_ref, up_ref, down_ref, out_ref):
    out_ref[0:512, :] = wv_ref[...]
    out_ref[512:1024, :] = wr_ref[...]
    out_ref[1024:1536, 0:128] = wu_ref[...]
    out_ref[1024:1536, 128:256] = wc_ref[...]
    out_ref[1536:1792, :] = wo_ref[:, 0:256]
    out_ref[1792:2048, :] = wo_ref[:, 256:512]
    out_ref[2048:2560, :] = up_ref[...]
    out_ref[2560:2816, :] = down_ref[:, 0:256]
    out_ref[2816:3072, :] = down_ref[:, 256:512]


def embed_kernel(ids_ref, tab_ref, gain_ref, x_ref, emb_ref):
    emb = mm_tn(one_hot_t(ids_ref[0], tab_ref.shape[0]), tab_ref[...])
    inv = lax.rsqrt(jnp.mean(emb * emb, axis=-1, keepdims=True) + EPS)
    x_ref[0] = emb * inv * gain_ref[...]
    emb_ref[0] = emb.astype(BF)


def slope_kernel(x_ref, par_ref, e_ref, f_ref):
    dims, width = e_ref.shape[1], e_ref.shape[3]
    half = 8
    for c0 in range(0, width, 128):
        sl = pl.ds(c0, 128)
        for j0 in range(0, dims, half):
            decay = [jnp.exp(-wide(par_ref[pl.ds(j, 1), sl])) for j in range(j0, j0 + half)]

            def body(t, carry):
                e, f = carry
                xt = x_ref[0, at(t), sl]
                f = tuple(d * v + u for d, v, u in zip(decay, f, e))
                e = tuple(d * v + xt for d, v in zip(decay, e))
                return e, f

            zero = x_ref[0, at(0), sl] * 0.0
            e, f = lax.fori_loop(0, STEP, body, ((zero,) * half, (zero,) * half), unroll=8)
            for k in range(half):
                e_ref[0, j0 + k, :, sl] = e[k]
                f_ref[0, j0 + k, :, sl] = f[k]


def enter_kernel(me_ref, x_ref, p0_ref, p1_ref, p2_ref, p3_ref, ex_ref, lv_ref, par_ref):
    dims, width = lv_ref.shape[1:]

    @pl.when(pl.program_id(0) == 0)
    def _():
        for r, ref in enumerate((p0_ref, p1_ref, p2_ref, p3_ref)):
            own = pl.ds(pl.multiple_of((me_ref[0] ^ r) * 128, 128), 128)
            par_ref[:, own] = ref[...]

    row = lane_iota()
    for c0 in range(0, width, 128):
        sl = pl.ds(c0, 128)
        rates = [wide(par_ref[pl.ds(j, 1), sl]) for j in range(dims)]
        decay = [jnp.exp(-r) for r in rates]

        def body(t, s):
            xt = x_ref[0, at(t), sl]
            return tuple(d * v + xt for d, v in zip(decay, s))

        s = lax.fori_loop(
            0, STEP, body, tuple(jnp.zeros((LANES, 128), F32) for _ in range(dims)), unroll=32
        )
        s = chain(list(s), rates, row, shift_down)
        for j in range(dims):
            ex_ref[0, j, :, sl] = shift_down(s[j], 1, row)
            lv_ref[0, pl.ds(j, 1), sl] = s[j][LANES - 1 :, :]


def run_kernel(x_ref, ex_ref, se_ref, par_ref, out_ref):
    dims, width = se_ref.shape[1:]
    place = lane_iota().astype(F32)
    for c0 in range(0, width, 128):
        sl = pl.ds(c0, 128)
        rates = [wide(par_ref[pl.ds(j, 1), sl]) for j in range(dims)]
        decay = [jnp.exp(-r) for r in rates]
        ws = [wide(par_ref[pl.ds(dims + j, 1), sl]) for j in range(dims)]
        omega = wide(par_ref[pl.ds(5 * dims, 1), sl])
        start = tuple(
            ex_ref[0, j, :, sl]
            + jnp.exp(rates[j] * place * (-float(STEP))) * wide(se_ref[0, pl.ds(j, 1), sl])
            for j in range(dims)
        )

        def body(t, s):
            xt = x_ref[0, at(t), sl]
            s = tuple(d * v + xt for d, v in zip(decay, s))
            parts = [w * v for w, v in zip(ws, s)]
            while len(parts) > 1:
                parts = [a + b for a, b in zip(parts[::2], parts[1::2])]
            out_ref[0, at(t), sl] = parts[0] + omega * xt
            return s

        lax.fori_loop(0, STEP, body, start, unroll=8)


def to_natural(mask_row):
    q = lax.broadcasted_iota(jnp.int32, (BLK, BLK), 0)
    r = lax.broadcasted_iota(jnp.int32, (BLK, BLK), 1)
    hit = q == (r & (LANES - 1)) * STEP + (r >> 3)
    if mask_row is not None:
        hit = jnp.logical_and(hit, mask_row >= 0)
    return jnp.where(hit, 1.0, 0.0).astype(BF)


def from_natural(mask_row):
    r = lax.broadcasted_iota(jnp.int32, (BLK, BLK), 0)
    q = lax.broadcasted_iota(jnp.int32, (BLK, BLK), 1)
    hit = q == (r & (LANES - 1)) * STEP + (r >> 3)
    if mask_row is not None:
        hit = jnp.logical_and(hit, mask_row >= 0)
    return jnp.where(hit, 1.0, 0.0).astype(BF)


def read(ref):
    return ref[...].reshape((-1, ref.shape[-1]))


def write(ref, v):
    ref[...] = v.reshape(ref.shape)


def fill(refs, rows, to_ref):
    for r, ref in enumerate(refs):
        to_ref[:, pl.ds(r * 256, 256)] = ref[rows : rows + 512, :]


def fill_rows(refs, rows, to_ref):
    for r, ref in enumerate(refs):
        to_ref[pl.ds(r * 256, 256), 0:256] = ref[rows : rows + 256, :]
        to_ref[pl.ds(r * 256, 256), 256:512] = ref[rows + 256 : rows + 512, :]


def fill_gates(me, refs, wu_ref, wc_ref):
    for r, ref in enumerate(refs):
        own = pl.ds(pl.multiple_of((me ^ r) * 128, 128), 128)
        wu_ref[:, own] = ref[0:512, 0:128]
        wc_ref[:, own] = ref[0:512, 128:256]


def slots(keep_ref, send_ref):
    return ((keep_ref, 0), (send_ref, 0), (keep_ref, 1), (send_ref, 1))


def softmax_rows(query, keys, bias, factor):
    scores = mm_nt(query, keys) * factor + bias
    shifted = jnp.exp(scores - jnp.max(scores, axis=-1, keepdims=True))
    return shifted / jnp.sum(shifted, axis=-1, keepdims=True)


def forward_kernel(me_ref, es_ref, x_ref, emb_ref, bias_ref, wz_ref, zs_ref, zo_ref, *rest):
    packs, rest = rest[:8], rest[8:]
    (vp_ref, rp_ref, mix_ref, zp_ref, up_ref, cp_ref, res_ref) = rest[:7]
    (wv_ref, wr_ref, wu_ref, wc_ref, wo_ref) = rest[7:]

    @pl.when(pl.program_id(0) == 0)
    def _():
        fill(packs[0:4], 0, wv_ref)
        fill(packs[0:4], 512, wr_ref)
        fill_gates(me_ref[0], packs[4:8], wu_ref, wc_ref)
        fill_rows(packs[4:8], 512, wo_ref)

    es = es_ref[0]
    e = (es * sig(es)).astype(BF)
    zp = mm(e, wz_ref[...])
    zp_ref[0] = zp
    za = zp * sig(zp)
    query = (za * zs_ref[0:1, :] + zo_ref[0:1, :]).astype(BF)
    keys = (za * zs_ref[1:2, :] + zo_ref[1:2, :]).astype(BF)
    weights = softmax_rows(query, keys, bias_ref[...], zp.shape[-1] ** -0.5).astype(BF)
    vp = mm(x_ref[0].astype(BF), wv_ref[...])
    vp_ref[0] = vp
    values = (vp * sig(vp)).astype(BF)
    mixed = mm(weights, values)
    mix_ref[0] = mixed.astype(BF)
    rp = mm(e, wr_ref[...])
    rp_ref[0] = rp
    gated = (rp * sig(rp) * mixed).astype(BF)
    up = mm(e, wu_ref[...])
    up_ref[0] = up.astype(BF)
    cp = mm(e, wc_ref[...]) + mm(gated, wo_ref[...])
    cp_ref[0] = cp.astype(BF)
    emb = emb_ref[0].astype(F32)
    res_ref[0] = emb + sig(up) * (cp * sig(cp) - emb)


def ff_kernel(me_ref, nat_ref, cot_ref, res_ref, gain_ref, *rest):
    packs, rest = rest[:4], rest[4:]
    out_ref, gr_ref, keep_ref, send_ref, gg_ref, w_up_ref, w_down_ref, au_ref, ad_ref = rest
    step = pl.program_id(0)

    @pl.when(step == 0)
    def _():
        fill(packs, 0, w_up_ref)
        fill_rows(packs, 512, w_down_ref)
        au_ref[...] = jnp.zeros_like(au_ref)
        ad_ref[...] = jnp.zeros_like(ad_ref)
        gg_ref[...] = jnp.zeros_like(gg_ref)

    resid = read(res_ref)
    inv = lax.rsqrt(jnp.mean(resid * resid, axis=-1, keepdims=True) + EPS)
    unit = resid * inv
    gain = gain_ref[...]
    ff_in = (unit * gain).astype(BF)
    hp = mm(ff_in, w_up_ref[...])
    s = sig(hp)
    hidden = (hp * s).astype(BF)
    out = resid + mm(hidden, w_down_ref[...])
    out = out.astype(BF)
    cots = []
    for k in range(out_ref.shape[0]):
        out_ref[k] = mm(to_natural(None), out[k * BLK : k * BLK + BLK]).astype(BF)
        cots.append(mm(from_natural(nat_ref[k]), cot_ref[k]))
    grad_out = jnp.concatenate(cots, axis=0)
    grad_low = grad_out.astype(BF)
    ad_ref[...] += mm_tn(hidden, grad_low)
    grad_up = (mm_nt(grad_low, w_down_ref[...]) * slope(hp, s)).astype(BF)
    au_ref[...] += mm_tn(ff_in, grad_up)
    grad_norm = mm_nt(grad_up, w_up_ref[...])
    gain_part = jnp.sum(grad_norm * unit, axis=0, keepdims=True)
    for k in range(4):
        gg_ref[k : k + 1, :] += gain_part[:, k * 128 : (k + 1) * 128]
    scaled = grad_norm * gain
    write(
        gr_ref,
        grad_out
        + inv * (scaled - unit * jnp.mean(scaled * unit, axis=-1, keepdims=True)),
    )

    @pl.when(step == pl.num_programs(0) - 1)
    def _():
        for r, (ref, slot) in enumerate(slots(keep_ref, send_ref)):
            ref[slot, 0:512, :] = au_ref[:, r * 256 : r * 256 + 256].astype(BF)
            ref[slot, 512:768, :] = ad_ref[r * 256 : r * 256 + 256, 0:256].astype(BF)
            ref[slot, 768:1024, :] = ad_ref[r * 256 : r * 256 + 256, 256:512].astype(BF)


def gates_back_kernel(me_ref, es_ref, emb_ref, rp_ref, mix_ref, up_ref, cp_ref, gr_ref, *rest):
    packs, rest = rest[:8], rest[8:]
    (gm_ref, ge_ref, dir_ref, keep_ref, send_ref) = rest[:5]
    (wr_ref, wu_ref, wc_ref, wo_ref, ar_ref, au_ref, ac_ref, ao_ref) = rest[5:]
    me = me_ref[0]
    step = pl.program_id(0)

    @pl.when(step == 0)
    def _():
        fill(packs[0:4], 0, wr_ref)
        fill_gates(me, packs[4:8], wu_ref, wc_ref)
        fill_rows(packs[4:8], 512, wo_ref)
        for ref in (ar_ref, au_ref, ac_ref, ao_ref):
            ref[...] = jnp.zeros_like(ref)

    es = read(es_ref)
    e_t = (es * sig(es)).astype(BF).T
    emb = read(emb_ref).astype(F32)
    grad_resid = read(gr_ref)
    up = sig(read(up_ref).astype(F32))
    cp = read(cp_ref).astype(F32)
    cs = sig(cp)
    gcp = (grad_resid * up * slope(cp, cs)).astype(BF)
    gup = (grad_resid * (cp * cs - emb) * up * (1.0 - up)).astype(BF)
    write(dir_ref, (grad_resid * (1.0 - up)).astype(BF))
    ac_ref[...] += mm(e_t, gcp)
    au_ref[...] += mm(e_t, gup)
    rp = read(rp_ref)
    rs = sig(rp)
    reset = rp * rs
    mixed = read(mix_ref).astype(F32)
    ao_ref[...] += mm_tn((reset * mixed).astype(BF), gcp)
    grad_gated = mm_nt(gcp, wo_ref[...])
    write(gm_ref, (grad_gated * reset).astype(BF))
    grp = (grad_gated * mixed * slope(rp, rs)).astype(BF)
    ar_ref[...] += mm(e_t, grp)
    write(ge_ref, mm_nt(grp, wr_ref[...]) + mm_nt(gup, wu_ref[...]) + mm_nt(gcp, wc_ref[...]))

    @pl.when(step == pl.num_programs(0) - 1)
    def _():
        for r, (ref, slot) in enumerate(slots(keep_ref, send_ref)):
            units = pl.ds(r * 256, 256)
            own = pl.ds(pl.multiple_of((me ^ r) * 128, 128), 128)
            ref[slot, 0:512, :] = ar_ref[:, units].astype(BF)
            ref[slot, 512:1024, 0:128] = au_ref[:, own].astype(BF)
            ref[slot, 512:1024, 128:256] = ac_ref[:, own].astype(BF)
            ref[slot, 1024:1280, :] = ao_ref[units, 0:256].astype(BF)
            ref[slot, 1280:1536, :] = ao_ref[units, 256:512].astype(BF)


def mix_back_kernel(
    es_ref, x_ref, vp_ref, zp_ref, gm_ref, ge_ref,
    bias_ref, wz_ref, zs_ref, zo_ref, par_ref, gg_ref, *rest,
):
    packs, rest = rest[:4], rest[4:]
    (g_ref, gnv_ref, ae_ref, lb_ref, keep_ref, send_ref) = rest[:6]
    (wv_ref, av_ref, az_ref, gz_ref, gb_ref, as_ref) = rest[6:]
    step = pl.program_id(0)

    @pl.when(step == 0)
    def _():
        fill(packs, 0, wv_ref)
        for ref in (av_ref, az_ref, gz_ref, gb_ref):
            ref[...] = jnp.zeros_like(ref)

    es = es_ref[0]
    es_sig = sig(es)
    e_t = (es * es_sig).astype(BF).T
    gm = gm_ref[0]
    zp = zp_ref[0]
    zsig = sig(zp)
    za = zp * zsig
    factor = zp.shape[-1] ** -0.5
    s0, s1 = zs_ref[0:1, :], zs_ref[1:2, :]
    query = (za * s0 + zo_ref[0:1, :]).astype(BF)
    keys = (za * s1 + zo_ref[1:2, :]).astype(BF)
    weights = softmax_rows(query, keys, bias_ref[...], factor)
    vp = vp_ref[0]
    vs = sig(vp)
    values = (vp * vs).astype(BF)
    gvp = (mm_tn(weights.astype(BF), gm) * slope(vp, vs)).astype(BF)
    gnv_ref[0] = mm_nt(gvp, wv_ref[...]).astype(BF)
    av_ref[...] += mm_tn(x_ref[0].astype(BF), gvp)
    gw = mm_nt(gm, values)
    gsf = weights * (gw - jnp.sum(weights * gw, axis=-1, keepdims=True))
    gb_ref[...] += gsf
    gs = gsf.astype(BF)
    gq = mm(gs, keys) * factor
    gk = mm_tn(gs, query) * factor
    gz_ref[0:1, :] += jnp.sum(za * gq, axis=0, keepdims=True)
    gz_ref[1:2, :] += jnp.sum(za * gk, axis=0, keepdims=True)
    gz_ref[2:3, :] += jnp.sum(gq, axis=0, keepdims=True)
    gz_ref[3:4, :] += jnp.sum(gk, axis=0, keepdims=True)
    gzp = ((gq * s0 + gk * s1) * slope(zp, zsig)).astype(BF)
    az_ref[...] += mm(e_t, gzp)
    g_ref[0] = (ge_ref[0] + mm_nt(gzp, wz_ref[...])) * slope(es, es_sig)

    dims, width = lb_ref.shape[1:]
    row = lane_iota()
    for c0 in range(0, width, 128):
        sl = pl.ds(c0, 128)
        rates = [wide(par_ref[pl.ds(j, 1), sl]) for j in range(dims)]
        decay = [jnp.exp(-r) for r in rates]

        def body(t, a):
            gt = g_ref[0, at(STEP - 1 - t), sl]
            return tuple(d * v + gt for d, v in zip(decay, a))

        a = lax.fori_loop(
            0, STEP, body, tuple(jnp.zeros((LANES, 128), F32) for _ in range(dims)), unroll=32
        )
        a = chain(list(a), rates, row, shift_up)
        for j in range(dims):
            ae_ref[0, j, :, sl] = shift_up(a[j], 1, row)
            lb_ref[0, pl.ds(j, 1), sl] = a[j][0:1, :]

    @pl.when(step == pl.num_programs(0) - 1)
    def _():
        perm = to_natural(None)
        v = sum(mm(perm, p) for p in split3(gb_ref[...]))
        v = sum(mm_nt(p, perm) for p in split3(v))
        v = v[:C, :C] + v[C:, C:]
        v = jnp.concatenate([v, jnp.zeros((C, C), F32)], axis=1)
        bias = jnp.sum(pltpu.roll(skew(v, -1), C - 1, axis=1), axis=0, keepdims=True)
        zero = jnp.zeros((6, 128), F32)
        small = jnp.concatenate(
            [gz_ref[0:4, :], bias[:, :128], bias[:, 128:], gg_ref[...], zero], axis=0
        )
        high = small.astype(BF)
        low = (small - high.astype(F32)).astype(BF)
        small = jnp.concatenate([high, low], axis=1)
        as_ref[512:768, 0:128] = az_ref[0:256, :].astype(BF)
        as_ref[512:768, 128:256] = az_ref[256:512, :].astype(BF)
        for r, (ref, slot) in enumerate(slots(keep_ref, send_ref)):
            as_ref[0:512, :] = av_ref[:, r * 256 : r * 256 + 256].astype(BF)
            for k in range(8):
                ref[slot, k * 112 : k * 112 + 96, :] = as_ref[k * 96 : k * 96 + 96, :]
                ref[slot, k * 112 + 96 : k * 112 + 112, :] = small


def adjoint_kernel(x_ref, g_ref, ae_ref, ex_ref, se_ref, par_ref, gn_ref, mn_ref):
    dims, width = se_ref.shape[1:]
    place = lane_iota().astype(F32)
    half = 8
    for c0 in range(0, width, 128):
        sl = pl.ds(c0, 128)
        omega = wide(par_ref[pl.ds(5 * dims, 1), sl])
        for j0 in range(0, dims, half):
            js = range(j0, j0 + half)
            rates = [wide(par_ref[pl.ds(j, 1), sl]) for j in js]
            decay = [jnp.exp(-r) for r in rates]
            ws = [wide(par_ref[pl.ds(dims + j, 1), sl]) for j in js]

            def emit(t, a, gt):
                parts = [w * v for w, v in zip(ws, a)]
                while len(parts) > 1:
                    parts = [p + q for p, q in zip(parts[::2], parts[1::2])]
                if j0 == 0:
                    gn_ref[0, at(t), sl] = parts[0] + omega * gt
                else:
                    gn_ref[0, at(t), sl] += parts[0]

            gt = g_ref[0, at(STEP - 1), sl]
            xt = x_ref[0, at(STEP - 1), sl]
            a = tuple(gt + d * ae_ref[0, j, :, sl] for j, d in zip(js, decay))
            emit(STEP - 1, a, gt)
            m = tuple(xt * v for v in a)
            zero = tuple(jnp.zeros((LANES, 128), F32) for _ in js)

            def body(i, carry):
                a, b, m, n = carry
                t = STEP - 2 - i
                gt = g_ref[0, at(t), sl]
                xt = x_ref[0, at(t), sl]
                b = tuple(u + d * v for d, u, v in zip(decay, a, b))
                a = tuple(gt + d * v for d, v in zip(decay, a))
                emit(t, a, gt)
                m = tuple(u + xt * v for u, v in zip(m, a))
                n = tuple(u + xt * v for u, v in zip(n, b))
                return a, b, m, n

            carry = (a, zero, m, zero)
            for i in range(3):
                carry = body(i, carry)
            a, b, m, n = lax.fori_loop(3, STEP - 1, body, carry, unroll=7)
            for k, j in enumerate(js):
                start = ex_ref[0, j, :, sl] + jnp.exp(rates[k] * place * (-float(STEP))) * wide(
                    se_ref[0, pl.ds(j, 1), sl]
                )
                mn_ref[0, pl.ds(j, 1), sl] = jnp.sum(m[k], axis=0, keepdims=True)
                mn_ref[0, pl.ds(dims + j, 1), sl] = jnp.sum(
                    n[k] + start * (a[k] + decay[k] * b[k]), axis=0, keepdims=True
                )


def leave_kernel(n_parts, me_ref, ids_ref, emb_ref, x_ref, g_ref, ar_ref, ex_ref, se_ref, el_ref, ed_ref,
                 dir_ref, gnv_ref, *rest):
    locals_, rest = rest[: 2 * n_parts], rest[2 * n_parts :]
    par_ref, gain_ref, ig_ref, keep_ref, send_ref = rest[:5]
    gn_ref, ge_ref, go_ref, gg_ref, sum_ref = rest[5:]
    step = pl.program_id(0)
    dims, width = se_ref.shape[1:]

    @pl.when(step == 0)
    def _():
        for ref in (ge_ref, go_ref, gg_ref, sum_ref):
            ref[...] = jnp.zeros_like(ref)

    for k in range(n_parts):

        @pl.when(step == k)
        def _(k=k):
            gn_ref[...] = locals_[2 * k][0]
            sum_ref[0 : 2 * dims, :] += locals_[2 * k + 1][0]

    place = lane_iota().astype(F32)
    for c0 in range(0, width, 128):
        sl = pl.ds(c0, 128)
        rates = [wide(par_ref[pl.ds(j, 1), sl]) for j in range(dims)]
        decay = [jnp.exp(-r) for r in rates]
        ws = [wide(par_ref[pl.ds(dims + j, 1), sl]) for j in range(dims)]
        far = [
            jnp.exp(r * (LANES - 1.0 - place) * (-float(STEP))) * wide(ar_ref[0, pl.ds(j, 1), sl])
            for j, r in enumerate(rates)
        ]
        for j in range(dims):
            start = ex_ref[0, j, :, sl] + jnp.exp(rates[j] * place * (-float(STEP))) * wide(
                se_ref[0, pl.ds(j, 1), sl]
            )
            whole = jnp.exp(rates[j] * (-float(STEP)))
            more_m = far[j] * decay[j] * el_ref[0, j, :, sl]
            more_n = far[j] * (decay[j] * ed_ref[0, j, :, sl] + float(STEP) * whole * start)
            sum_ref[pl.ds(j, 1), sl] += jnp.sum(more_m, axis=0, keepdims=True)
            sum_ref[pl.ds(dims + j, 1), sl] += jnp.sum(more_n, axis=0, keepdims=True)

        def body(i, c):
            t = STEP - 1 - i
            c = tuple(d * v for d, v in zip(decay, c))
            parts = [w * v for w, v in zip(ws, c)]
            while len(parts) > 1:
                parts = [p + q for p, q in zip(parts[::2], parts[1::2])]
            gn_ref[at(t), sl] += parts[0]
            return c

        lax.fori_loop(0, STEP, body, tuple(far), unroll=8)

    go_ref[...] += jnp.sum(g_ref[0] * x_ref[0], axis=0, keepdims=True)
    emb = emb_ref[0].astype(F32)
    inv = lax.rsqrt(jnp.mean(emb * emb, axis=-1, keepdims=True) + EPS)
    unit = emb * inv
    gn = gn_ref[...] + gnv_ref[0].astype(F32)
    gg_ref[...] += jnp.sum(gn * unit, axis=0, keepdims=True)
    scaled = gn * gain_ref[...]
    ig = dir_ref[0].astype(F32) + inv * (
        scaled - unit * jnp.mean(scaled * unit, axis=-1, keepdims=True)
    )
    ig = ig.astype(BF)
    ids = ids_ref[0]
    ig_ref[0] = mm(to_natural(ids), ig).astype(BF)
    ge_ref[...] += mm(one_hot_t(ids, ge_ref.shape[0]), ig)

    @pl.when(step == pl.num_programs(0) - 1)
    def _():
        m, n = sum_ref[0:dims, :], sum_ref[dims : 2 * dims, :]
        rb, er, eb = (par_ref[k * dims : (k + 1) * dims, :] for k in (2, 3, 4))
        rise = one_less_exp(par_ref[0:dims, :])
        sum_ref[0:dims, :] = eb * (rise * n - m)
        sum_ref[dims : 2 * dims, :] = er * m
        sum_ref[2 * dims : 3 * dims, :] = rb * m
        pad = jnp.zeros((8, 128), F32)
        gains = [gg_ref[:, k * 128 : (k + 1) * 128] for k in range(4)]
        for r, (ref, slot) in enumerate(slots(keep_ref, send_ref)):
            own = pl.ds(pl.multiple_of((me_ref[0] ^ r) * 128, 128), 128)
            part = pl.ds(pl.multiple_of((me_ref[0] ^ r) * 64, 64), 64)
            ref[slot, 0:64, :] = ge_ref[part, 0:256].astype(BF)
            ref[slot, 64:128, :] = ge_ref[part, 256:512].astype(BF)
            ref[slot, 128:144, 0:128] = sum_ref[0:dims, own].astype(BF)
            ref[slot, 128:144, 128:256] = sum_ref[dims : 2 * dims, own].astype(BF)
            ref[slot, 144:160, 0:128] = sum_ref[2 * dims : 3 * dims, own].astype(BF)
            ref[slot, 144:160, 128:256] = jnp.concatenate(
                [jnp.broadcast_to(go_ref[:, own], (4, 128)), *gains, pad], axis=0
            ).astype(BF)


def repair(v):
    out = []
    for k in range(0, v.shape[0], 112):
        both = v[k + 96 : k + 112, 0:128] + v[k + 96 : k + 112, 128:256]
        high = both.astype(BF)
        low = (both - high.astype(F32)).astype(BF)
        out += [v[k : k + 96].astype(BF), jnp.concatenate([high, low], axis=1)]
    return jnp.concatenate(out, axis=0)


def plain(v):
    return v.astype(BF)


def add_kernel(n, fix, *refs):
    acc = refs[0][...].astype(F32)
    for ref in refs[1:n]:
        acc = acc + ref[...].astype(F32)
    refs[n][...] = fix(acc[0])
    refs[n + 1][...] = fix(acc[1])


def cut_kernel(bit, fix, at_ref, near_ref, far_ref, keep_ref, send_ref, sum_ref):
    rows = keep_ref.shape[0]
    sum_ref[...] = near_ref[...].astype(F32) + far_ref[...].astype(F32)
    upper = (at_ref[0] // bit) % 2
    keep_ref[...] = fix(sum_ref[pl.ds(pl.multiple_of(upper * rows, rows), rows), :])
    send_ref[...] = fix(sum_ref[pl.ds(pl.multiple_of((1 - upper) * rows, rows), rows), :])


def sum_kernel(fix, *refs):
    refs[-1][...] = fix(total([ref[...] for ref in refs[:-1]]))


def join_kernel(put, at_ref, near_ref, far_ref, *refs):
    rows = near_ref.shape[0]
    upper = at_ref[0] % 2
    refs[-1][pl.ds(pl.multiple_of(upper * rows, rows), rows), :] = near_ref[...].astype(F32)
    refs[-1][pl.ds(pl.multiple_of((1 - upper) * rows, rows), rows), :] = far_ref[...].astype(F32)
    put(refs[-1], *refs[:-1])


def widen_kernel(me_ref, *refs):
    for r, ref in enumerate(refs[:4]):

        @pl.when(pl.program_id(0) == r)
        def _(ref=ref):
            refs[-1][...] = ref[...].astype(F32)


def pairs(axis, bit):
    return [(i, i ^ bit) for i in range(lax.axis_size(axis))]


def swap(v, axis, bit):
    return lax.ppermute(v, axis, pairs(axis, bit))


def hop_kernel(
    bit, span, backward, at_ref, total_ref, recv_ref, out_ref, rate_ref, next_ref, new_ref, wire_ref
):
    place = at_ref[0]
    upper = (place // bit) % 2 == 1
    inside = place % bit
    gap = bit - 1 - inside if backward else inside
    first = jnp.logical_not(upper) if backward else upper
    rate = rate_ref[0 : total_ref.shape[1], :]
    decay = jnp.exp(rate * (-float(bit * span)))
    near = jnp.exp(-rate * (gap * span).astype(F32))
    for k in range(total_ref.shape[0]):
        total, recv = total_ref[k], recv_ref[k].astype(F32)
        new_ref[k] = out_ref[k] + jnp.where(first, recv * near, 0.0)
        following = jnp.where(first, total + decay * recv, recv + decay * total)
        next_ref[k] = following
        wire_ref[k] = following.astype(wire_ref.dtype)


def exclusive(total, par, place, span, backward, between, late):
    count = lax.axis_size("seq")
    out = jnp.zeros_like(total)
    wire = total if backward else total.astype(BF)
    bit = 1
    step = 0
    while bit < count:
        recv = swap(wire, "seq", bit)
        if step < len(between):
            between[step]()
        last = bit * 2 >= count
        total, out, wire, *carried = small_call(
            functools.partial(hop_kernel, bit, span, backward), "hop", [place],
            [total, recv, out, par],
            [(total.shape, F32)] * 2 + [(total.shape, wire.dtype)], through=late if last else (),
        )
        if last:
            late[:] = carried
        bit *= 2
        step += 1
    for rest in between[step:]:
        rest()
    return out


def block_states(local, par, place, span, backward, between, late=()):
    late = [] if isinstance(late, tuple) else late
    per = span // BLK
    if per == 1:
        return exclusive(local, par, place, span, backward, between, late)
    rate = par[: local.shape[1]]
    local = local.reshape((-1, per) + local.shape[1:])
    decay = jnp.exp(rate * (-float(BLK)))
    order = range(per)[::-1] if backward else range(per)
    total = 0.0
    for k in order:
        total = total * decay + local[:, k]
    state = exclusive(total, par, place, span, backward, between, late)
    states = [None] * per
    for k in order:
        states[k] = state
        state = state * decay + local[:, k]
    return jnp.stack(states, axis=1).reshape((-1,) + rate.shape)


def total(parts):
    acc = parts[0].astype(F32)
    for p in parts[1:]:
        acc = acc + p.astype(F32)
    return acc


def small_call(kernel, name, scalars, args, outs, scratch=(), through=()):
    after = list(through) + before()
    vmem = pl.BlockSpec(memory_space=pltpu.VMEM)
    smem = pl.BlockSpec(memory_space=pltpu.SMEM)
    n = len(scalars) + len(args)

    def body(*refs):
        kernel(*refs[:n], *refs[n + len(after) : n + len(after) + len(outs)], *refs[n + len(after) + len(outs) + len(through) :])

    made = pl.pallas_call(
        body,
        in_specs=[smem] * len(scalars)
        + [vmem] * len(args)
        + [pl.BlockSpec(memory_space=pl.ANY)] * len(after),
        out_specs=[vmem] * len(outs) + [pl.BlockSpec(memory_space=pl.ANY)] * len(through),
        out_shape=[jax.ShapeDtypeStruct(s, t) for s, t in outs]
        + [jax.ShapeDtypeStruct(v.shape, v.dtype) for v in through],
        input_output_aliases={n + k: len(outs) + k for k in range(len(through))},
        scratch_shapes=[pltpu.VMEM(s, t) for s, t in scratch],
        compiler_params=pltpu.CompilerParams(vmem_limit_bytes=VMEM),
        cost_estimate=cost(2),
        name=name,
    )(*scalars, *args, *after)
    return done(made)


def go(*jobs, through=None):
    jobs = [job for job in jobs if job is not None]
    if not jobs:
        return through
    groups = [sum((list(job[k]) for job in jobs), []) for k in range(1, 5)]

    def kernel(*refs):
        starts = [sum(len(g) for g in groups[:k]) for k in range(4)]
        for job in jobs:
            mine = []
            for k in range(4):
                mine += refs[starts[k] : starts[k] + len(job[k + 1])]
                starts[k] += len(job[k + 1])
            job[0](*mine)

    made = small_call(kernel, "stage", *groups, [] if through is None else [through])
    for job in jobs:
        job[5](*made[: len(job[3])])
        made = made[len(job[3]) :]
    return made[0] if made else None


class Reduction:
    def __init__(self, at, keeps, sends, fix=plain):
        self.at, self.fix = at, fix
        self.args = list(keeps) + [swap(s, "ch", 1) for s in sends]
        self.wide = lax.axis_size("seq") != 8

    def store(self, axis, bit):
        def then(near, far=None):
            self.near = near
            self.far = swap(near if far is None else far, axis, bit)

        return then

    def shards(self):
        shape = self.args[0].shape[1:]
        kernel = functools.partial(add_kernel, len(self.args), self.fix)
        return (kernel, [], self.args, [(shape, BF)] * 2, [], self.store("ch", 2))

    def halve(self):
        if self.wide:
            return None
        rows = self.near.shape[0]
        return (
            functools.partial(cut_kernel, 1, self.fix), [self.at], [self.near, self.far],
            [((rows // 2, 256), BF)] * 2, [((rows, 256), F32)], self.store("seq", 1),
        )

    def hop(self, bit):
        if self.wide:
            return None
        kernel = functools.partial(sum_kernel, self.fix)
        return (
            kernel, [], [self.near, self.far], [(self.near.shape, BF)], [], self.store("seq", bit)
        )

    def both(self):
        shape = self.args[0].shape

        def then(near):
            self.near = near
            if self.wide:
                self.near = lax.psum(near.astype(F32), "seq").astype(BF)
                self.far = jnp.zeros_like(near)
            else:
                self.far = swap(near, "seq", 1)

        return (functools.partial(sum_kernel, self.fix), [], self.args, [(shape, BF)], [], then)

    def split(self):
        shape = self.near.shape[1:]
        kernel = functools.partial(add_kernel, 2, self.fix)
        return (
            kernel, [], [self.near, self.far], [(shape, BF)] * 2, [], self.store("ch", 2)
        )

    def join(self, put, outs, halved=True):
        def then(*made):
            self.made = made

        args, shape = [self.near, self.far], self.near.shape
        if self.wide and halved:
            whole = lax.psum(total(args), "seq")
            return (put, [], [whole], outs, [], then)
        if halved:
            shape = (2 * shape[0], 256)
            return (functools.partial(join_kernel, put), [self.at], args, outs, [(shape, F32)], then)

        def finish(near_ref, far_ref, *refs):
            refs[-1][...] = near_ref[...].astype(F32) + far_ref[...].astype(F32)
            put(refs[-1], *refs[:-1])

        return (finish, [], args, outs, [(shape, F32)], then)


def put_ff(whole, up_ref, down_ref):
    up_ref[...] = whole[0:512, :].astype(F32)
    down_ref[:, 0:256] = whole[512:768, :].astype(F32)
    down_ref[:, 256:512] = whole[768:1024, :].astype(F32)


def put_gates(whole, reset_ref, update_ref, cand_ref, out_ref):
    reset_ref[...] = whole[0:512, :]
    update_ref[...] = whole[512:1024, 0:128]
    cand_ref[...] = whole[512:1024, 128:256]
    out_ref[:, 0:256] = whole[1024:1280, :]
    out_ref[:, 256:512] = whole[1280:1536, :]


def put_mix(whole, value_ref, z_ref, scale_ref, offset_ref, bias_ref, gain_ref):
    for k in range(8):
        part = whole[k * 112 : k * 112 + 96, :]
        if k < 5:
            value_ref[k * 96 : k * 96 + 96, :] = part
        elif k == 5:
            value_ref[480:512, :] = part[0:32]
            z_ref[0:64, :] = part[32:96, 0:128]
            z_ref[256:320, :] = part[32:96, 128:256]
        else:
            first = (k - 6) * 96 + 64
            z_ref[first : first + 96, :] = part[:, 0:128]
            z_ref[256 + first : 256 + first + 96, :] = part[:, 128:256]
    small = whole[96:112, 0:128] + whole[96:112, 128:256]
    scale_ref[...] = small[0:2]
    offset_ref[...] = small[2:4]
    bias_ref[...] = jnp.concatenate([small[4:5], small[5:6]], axis=1)[:, :255]
    for k in range(4):
        gain_ref[:, k * 128 : k * 128 + 128] = small[6 + k : 7 + k]


def put_late(whole, emb_ref, rate_ref, beta_ref, eta_ref, omega_ref, gain_ref):
    emb_ref[:, 0:256] = whole[0:64, :].astype(BF)
    emb_ref[:, 256:512] = whole[64:128, :].astype(BF)
    rate_ref[...] = whole[128:144, 0:128]
    beta_ref[...] = whole[128:144, 128:256]
    eta_ref[...] = whole[144:160, 0:128]
    omega_ref[...] = whole[144:145, 128:256]
    for k in range(4):
        gain_ref[:, k * 128 : k * 128 + 128] = whole[148 + k : 149 + k, 128:256]


def reach(v):
    return [v, swap(v, "ch", 1), swap(v, "ch", 2)]


def relay(parts, far):
    parts[2] = far
    parts.append(swap(far, "ch", 1))


def widen(parts, me, base, first, blocks):
    n, _, width = parts[0].shape
    step = n if blocks % n == 0 and first % n == 0 else 1
    inner = n // step

    def held(k):
        return lambda r, b, me_ref: (jnp.where(r == k, b, jnp.where(r > k, inner - 1, 0)), 0, 0)

    extra = before()
    if base is not None:
        extra = [base] + [v for v in extra if v is not base]
    return done(
        pl.pallas_call(
            widen_kernel,
            grid_spec=pltpu.PrefetchScalarGridSpec(
                num_scalar_prefetch=1,
                grid=(4, inner),
                in_specs=[pl.BlockSpec((step, BLK, width), held(k)) for k in range(4)]
                + [pl.BlockSpec(memory_space=pl.ANY)] * len(extra),
                out_specs=pl.BlockSpec(
                    (step, BLK, width),
                    lambda r, b, me_ref: (((me_ref[0] ^ r) * blocks + first) // step + b, 0, 0),
                ),
            ),
            out_shape=jax.ShapeDtypeStruct((4 * blocks, BLK, width), F32),
            input_output_aliases={} if base is None else {5: 0},
            compiler_params=pltpu.CompilerParams(
                dimension_semantics=("arbitrary", "arbitrary"), vmem_limit_bytes=VMEM
            ),
            cost_estimate=cost(4),
            name="widen",
        )(me, *parts, *extra)
    )


def row_block(shape, first=0, per=1):
    zeros = (0,) * (len(shape) - 1)
    return pl.BlockSpec((per,) + tuple(shape[1:]), lambda i, *_: (i + first // per,) + zeros)


def whole_block(shape):
    zeros = (0,) * len(shape)
    return pl.BlockSpec(tuple(shape), lambda i, *_: zeros)


def call(kernel, name, span, us, scalars, rows, fixed, row_outs, fixed_outs, scratch, specs=None, per=1, into=None):
    first, count = span
    after = before()
    if specs is None:
        specs = [row_block(v.shape, first if v.shape[0] > count else 0, per) for v in rows]
    shapes = [((count,) + s[1:], t) for s, t in row_outs]
    out_specs = [row_block(s, 0, per) for s, _ in shapes] + [whole_block(s) for s, _ in fixed_outs]
    aliases = {}
    if into is not None:
        shapes[0] = row_outs[0]
        out_specs[0] = row_block(row_outs[0][0], first, per)
        if into:
            after = [into[0]] + [v for v in after if v is not into[0]]
            aliases = {len(scalars) + len(rows) + len(fixed): 0}
    specs = specs + [v[1] if isinstance(v, tuple) else whole_block(v.shape) for v in fixed]
    specs = specs + [pl.BlockSpec(memory_space=pl.ANY)] * len(after)
    fixed = [v[0] if isinstance(v, tuple) else v for v in fixed]
    n = len(scalars) + len(rows) + len(fixed)

    def body(*refs):
        kernel(*refs[:n], *refs[n + len(after) :])

    made = pl.pallas_call(
        body,
        grid_spec=pltpu.PrefetchScalarGridSpec(
            num_scalar_prefetch=len(scalars),
            grid=(count // per,),
            in_specs=specs,
            out_specs=out_specs,
            scratch_shapes=[pltpu.VMEM(s, t) for s, t in scratch],
        ),
        out_shape=[jax.ShapeDtypeStruct(s, t) for s, t in shapes + fixed_outs],
        input_output_aliases=aliases,
        compiler_params=pltpu.CompilerParams(
            dimension_semantics=("arbitrary",), vmem_limit_bytes=VMEM
        ),
        cost_estimate=cost(us),
        name=name,
    )(*scalars, *rows, *fixed, *after)
    return done(made)


def local(
    token_ids, counts, embedding, gain_one, ema_rate, ema_beta, ema_eta, ema_omega, w_value, w_reset,
    w_z, z_scale, z_offset, position_bias, w_update, w_cand, w_out, gain_two, w_up, w_down, cotangent,
):
    batch, span = token_ids.shape
    vocab, width = embedding.shape
    group = lax.axis_size("ch")
    mine = lax.axis_index("ch")
    channels, dims = ema_rate.shape
    z_width = w_z.shape[1]
    units = w_value.shape[1] * group
    seqs = batch // group
    blocks = seqs * span // BLK
    rows = blocks * BLK
    me = mine.astype(jnp.int32).reshape(1)

    ORDER.clear()
    LANDED.clear()
    (par,) = small_call(
        prep_kernel, "prep", [], [ema_rate.T, ema_beta.T, ema_eta.T, ema_omega[None]],
        [((5 * dims + 8, channels), F32)],
    )
    pars = [par] + [swap(par, "ch", r) for r in (1, 2, 3)]
    (pack,) = small_call(
        pack_kernel, "pack", [], [w_value, w_reset, w_update, w_cand, w_out, w_up, w_down],
        [((3072, 256), BF)],
    )
    pack = reach(pack)

    def rows_of(size, k):
        return [(v, pl.BlockSpec((size, 256), lambda i, *_: (k, 0))) for v in pack]

    g_one, g_two = gain_one[None], gain_two[None]

    ids = lax.dynamic_slice_in_dim(token_ids, mine * seqs, seqs, 0)
    own_counts = lax.dynamic_slice_in_dim(counts, mine * seqs, seqs, 0)
    places = lax.axis_index("seq") * span + jnp.arange(span, dtype=jnp.int32)
    ids = jnp.where(places[None, :] < own_counts[:, None], ids, -1)
    ids_nat = ids.reshape(blocks, 1, BLK)
    ids_tm = ids.reshape(blocks, LANES, STEP).transpose(0, 2, 1).reshape(blocks, 1, BLK)

    row = (blocks, BLK, width)
    row_v = (blocks, BLK, units)
    states = (blocks, dims, LANES, width)
    edge = (blocks, dims, width)
    every = (0, blocks)
    x, emb = call(
        embed_kernel, "embed", every, 4, [], [ids_tm], [embedding, g_one], [(row, F32), (row, BF)], [], []
    )
    ex, lv, par = call(
        enter_kernel, "enter", every, 6, [me], [x], pars, [(states, F32), (edge, F32)],
        [((5 * dims + 8, width), F32)], [],
    )
    made = {}

    def slopes():
        made["slope"] = call(
            slope_kernel, "slope", every, 8, [], [x], [par], [(states, F32), (states, F32)], [], []
        )

    def table():
        bias = jnp.concatenate([position_bias, jnp.zeros((1,), F32)])[None]
        (made["bias"],) = small_call(table_kernel, "table", [], [bias], [((BLK, BLK), F32)])

    at_seq = lax.axis_index("seq").astype(jnp.int32).reshape(1)
    steps = [
        lambda: None,
        slopes,
        table,
    ]
    far = [pack[2]]
    se = block_states(lv, par, at_seq, span, False, steps, far)
    relay(pack, far[0])
    el, ed = made["slope"]
    bias = made["bias"]
    (es,) = call(run_kernel, "run", every, 7, [], [x, ex, se], [par], [(row, F32)], [], [])
    vp, rp, mix, zp, up, cp, res = call(
        forward_kernel, "forward", every, 12, [me], [es, x, emb],
        [bias, w_z, z_scale, z_offset, *rows_of(1024, 0), *rows_of(1024, 1)],
        [(row_v, F32), (row_v, F32), (row_v, BF), ((blocks, BLK, z_width), F32), (row, BF), (row, BF),
         (row, F32)],
        [],
        [((width, units), BF), ((width, units), BF), ((width, width), BF), ((width, width), BF),
         ((units, width), BF)],
    )
    cot = cotangent.reshape(batch * span // BLK, BLK, width)

    def pack_outs(rows):
        return [((2, rows, 256), BF), ((2, rows, 256), BF)]

    out, gr, keep3, send3, gg2 = call(
        ff_kernel, "ff", every, 14, [me], [ids_nat, cot, res], [g_two, *rows_of(1024, 2)],
        [(row, BF), (row, F32)],
        pack_outs(1024) + [((4, 128), F32)],
        [((width, units), BF), ((units, width), BF), ((width, units), F32), ((units, width), F32)],
        specs=[
            row_block(ids_nat.shape, 0, PER),
            pl.BlockSpec(
                (PER, BLK, width), lambda i, me_ref: (me_ref[0] * (blocks // PER) + i, 0, 0)
            ),
            row_block(res.shape, 0, PER),
        ],
        per=PER,
    )
    sum3 = Reduction(at_seq, [keep3], [send3])
    out = reach(out)

    gm, ge, direct, keep2, send2 = call(
        gates_back_kernel, "gates_back", every, 17, [me], [es, emb, rp, mix, up, cp, gr],
        [*rows_of(512, 1), *rows_of(1024, 1)],
        [(row_v, BF), (row, F32), (row, BF)],
        pack_outs(1536),
        [((width, units), BF), ((width, width), BF), ((width, width), BF), ((units, width), BF),
         ((width, units), F32), ((width, width), F32), ((width, width), F32), ((units, width), F32)],
    )
    sum2 = Reduction(at_seq, [keep2], [send2])
    land(out[1])
    go(sum3.shards())
    g, gnv, ae, lb, keep1, send1 = call(
        mix_back_kernel, "mix_back", every, 24, [], [es, x, vp, zp, gm, ge],
        [bias, w_z, z_scale, z_offset, par, gg2, *rows_of(512, 0)],
        [(row, F32), (row, BF), (states, F32), (edge, F32)],
        pack_outs(896),
        [((width, units), BF), ((width, units), F32), ((width, z_width), F32),
         ((8, z_width), F32), ((BLK, BLK), F32), ((768, 256), BF)],
    )
    sum1 = Reduction(at_seq, [keep1], [send1], repair)
    locals_ = []

    def adjoint():
        if len(locals_) < blocks:
            locals_.append(
                call(
                    adjoint_kernel, "adjoint", (len(locals_), 1), 6, [], [x, g, ae, ex, se], [par],
                    [(row, F32), ((blocks, 2 * dims, width), F32)], [], [],
                )
            )

    def between0():
        relay(out, go(sum3.halve(), sum2.shards(), through=out[2]))
        adjoint()

    def between1():
        land(out[3])
        go(sum3.hop(2))
        adjoint()

    def between2():
        go(sum1.shards(), sum3.hop(4))
        adjoint()
        go(sum2.halve())

    ar = block_states(lb, par, at_seq, span, True, [between0, between1, between2])
    while len(locals_) < blocks:
        adjoint()
    go(sum2.hop(4), sum1.halve(), sum3.hop(1))
    parts = [(0, blocks // 2), (blocks // 2, blocks // 2)]
    keep, send, ig = [], [], []
    for part in parts:
        rows_in = [ids_tm, emb, x, g, ar, ex, se, el, ed, direct, gnv]
        mine_in = [v for k in range(part[0], part[0] + part[1]) for v in locals_[k]]
        whole, kept, sent = call(
            functools.partial(leave_kernel, part[1]), "leave", part, 8, [me],
            rows_in, [*mine_in, par, g_one],
            [(row, BF)],
            pack_outs(160),
            [((BLK, width), F32), ((vocab, width), F32), ((1, width), F32), ((1, width), F32),
             ((3 * dims, width), F32)],
            into=ig,
        )
        keep.append(kept)
        send.append(sent)
        ig = [whole]
        if len(keep) == 1:
            go(sum1.hop(2))
    ig = reach(ig[0])
    last = Reduction(at_seq, keep, send)
    relay(ig, ig[2])
    go(sum1.hop(4), sum2.hop(2))
    go(last.both())
    output = widen(out, me, None, 0, blocks).reshape(batch, span, width)
    go(last.hop(2))
    go(sum2.hop(1), sum1.hop(1))
    go(last.hop(4))
    wide_up, wide_down = ((width, 256), F32), ((256, width), F32)
    go(sum3.join(put_ff, [wide_up, wide_down]))
    grad_up, grad_down = sum3.made
    go(sum2.join(put_gates, [wide_up, ((width, 128), F32), ((width, 128), F32), wide_down]))
    grad_reset, grad_update, grad_cand, grad_out = sum2.made
    go(last.split())
    input_grad = widen(ig, me, None, 0, blocks).reshape(batch, span, width)
    small = ((dims, channels), F32)
    go(
        last.join(
            put_late,
            [((64, width), BF), small, small, small, ((1, channels), F32), ((1, width), F32)],
            False,
        )
    )
    go(
        sum1.join(
            put_mix,
            [wide_up, ((width, z_width), F32), ((2, z_width), F32), ((2, z_width), F32),
             ((1, 255), F32), ((1, width), F32)],
        )
    )
    grad_value, grad_z, grad_scale, grad_offset, grad_bias, grad_two = sum1.made
    emb_part, grad_rate, grad_beta, grad_eta, grad_omega, grad_one = last.made
    ge = lax.all_gather(emb_part, "ch", axis=0, tiled=True).astype(F32)
    return (
        output,
        input_grad,
        ge,
        grad_one[0],
        grad_rate.T,
        grad_beta.T,
        grad_eta.T,
        grad_omega[0],
        grad_value,
        grad_reset,
        grad_z,
        grad_scale,
        grad_offset,
        grad_bias[0],
        grad_update,
        grad_cand,
        grad_out,
        grad_two[0],
        grad_up,
        grad_down,
    )


def solution(mesh):
    return jax.shard_map(
        local,
        mesh=mesh,
        in_specs=(
            P(None, "seq"), P(), P(), P(), P("ch", None), P("ch", None), P("ch", None), P("ch"),
            P(None, "ch"), P(None, "ch"), P(), P(), P(), P(), P(None, "ch"), P(None, "ch"),
            P("ch", None), P(), P(None, "ch"), P("ch", None), P(None, "seq", None),
        ),
        out_specs=(
            P(None, "seq", None), P(None, "seq", None), P(), P(), P("ch", None), P("ch", None),
            P("ch", None), P("ch"), P(None, "ch"), P(None, "ch"), P(), P(), P(), P(), P(None, "ch"),
            P(None, "ch"), P("ch", None), P(), P(None, "ch"), P("ch", None),
        ),
        check_vma=False,
    )
```
